256 devices in a mesh: twist: 8 (over z_lo, y), walker: 16 (over z_hi, x), mp: 2 (over core).
Axes of the slice: x: 4, y: 4, z: 8 (z_hi: 4, z_lo: 2; z = z_hi * 2 + z_lo), core: 2. Of those that a mesh axis runs over, the one named last changes fastest.
Arguments:
- features: bfloat16 [8, 256, 64, 256], P('twist', 'walker', 'mp'), may hold values from -6 to 6
- psi_grad: bfloat16 [8, 256, 64, 256], P('twist', 'walker', 'mp'), may hold values from -6 to 6
- pair_means: bfloat16 [8, 2, 256, 64, 128], P('twist', None, 'walker', 'mp'), may hold values from -6 to 6
- energies: float32 [8, 256], P('twist', 'walker'), may hold values from -8 to -6
- multiplicity: int32 [8], P('twist'), may hold values from 1 to 48
- weights: bfloat16 [2, 896, 256], replicated, may hold values from -0.1875 to 0.1875
- a_inverse: float32 [2, 896, 896], P('mp'), as said below
- s_inverse: float32 [2, 256, 256], P('mp'), as said below
Outputs:
- a_batch: float32 [2, 896, 896], P('mp')
- s_batch: float32 [2, 256, 256], P('mp')
- direction: float32 [2, 896, 256], P('mp')
The draws below stay inside these ranges and needn't reach their ends.
Inputs may be any that keep to these rules, and one draw needn't show every extreme that they name: `multiplicity`: the number of symmetry-equivalent twists that each irreducible twist stands for. `a_inverse`: each layer's matrix is symmetric with a positive diagonal that exceeds the sum of the magnitudes of its row's other entries. `s_inverse`: each layer's matrix is symmetric with a positive diagonal that exceeds the sum of the magnitudes of its row's other entries.
All inputs are finite; a program needn't handle non-finite values.
Results may differ from the reference program's by a relative error of at most 0.0047.
Values sent between devices are 32-bit elements; how exact they have to be, the bound alone decides.
No kernel may reach another device: no remote copies, remote signals or barrier semaphores. Data moves between devices by JAX's collectives and lax.ppermute only.
A program may use at most 64 MiB of HBM per device.

```python
import jax
import jax.numpy as jnp
from jax import lax

D = 256
PAIR = 64
NE = 64
LAYERS = 2
DIN = 896
TWISTS = 8
WALKERS = 256


def spd_stack(key, order, diag_high):
    key_diag, key_off = jax.random.split(key)
    off_part = jax.random.uniform(key_off, (LAYERS, order, order), jnp.float32, -1.0, 1.0) * (0.2 / order)
    off_part = off_part + jnp.swapaxes(off_part, 1, 2)
    ramp = jax.random.uniform(key_diag, (LAYERS, order), jnp.float32, 0.0, 1.0)
    diag_part = jnp.exp(ramp * jnp.log(diag_high))
    eye_part = jnp.eye(order, dtype=jnp.float32)
    return off_part * (1.0 - eye_part) + diag_part[:, :, None] * eye_part


def draw_a_inverse(key, part):
    key = jax.random.fold_in(key, 11)
    return spd_stack(key, DIN, 4.0)


def draw_s_inverse(key, part):
    key = jax.random.fold_in(key, 12)
    return spd_stack(key, D, 4.0)


def place_ends(entries, key, least, high):
    longest = entries.shape.index(max(entries.shape))
    spots = []
    for shift in (0, 1):
        where = [jax.random.randint(jax.random.fold_in(key, axis), (), 0, length) for axis, length in enumerate(entries.shape)]
        where[longest] = (where[longest] + shift) % entries.shape[longest]
        spots.append(tuple(where))
    return entries.at[spots[0]].set(least).at[spots[1]].set(high)


def block_levels(stream_key, extent, shards, smallest, top_value):
    level, own = 1.0, jax.random.fold_in(stream_key, 6)
    for dim, blocks in shards:
        steps = jnp.exp(jax.random.uniform(jax.random.fold_in(own, dim), (blocks,), jnp.float32, smallest / len(shards), top_value / len(shards)))
        level = level * jnp.repeat(steps, extent[dim] // blocks).reshape([-1 if axis == dim else 1 for axis in range(len(extent))])
    return level


def normal_values(key, extent, scale, reach, cuts=(), held_as=jnp.bfloat16):
    factor_of = block_levels(key, extent, cuts, -0.22, 0.18) if cuts else 1.0
    result = jax.random.normal(key, extent, jnp.float32) * scale * factor_of
    return jnp.minimum(jnp.maximum(result, -reach), reach).astype(held_as)


def setup_inputs(seed: int = 0) -> dict:
    arg_keys = jax.random.split(jax.random.key(seed), 9)
    return {
        "features": normal_values(arg_keys[0], (TWISTS, WALKERS, NE, D), 1.0, 6.0, ((0, 8), (1, 16), (2, 2))),
        "psi_grad": normal_values(arg_keys[1], (TWISTS, WALKERS, NE, D), 1.0, 6.0, ((0, 8), (1, 16), (2, 2))),
        "pair_means": normal_values(arg_keys[2], (TWISTS, LAYERS, WALKERS, NE, 2 * PAIR), 1.0, 6.0, ((0, 8), (2, 16), (3, 2))),
        "energies": jnp.clip(-8.0 + 2.0 * jax.random.uniform(arg_keys[3], (TWISTS, WALKERS), jnp.float32) ** block_levels(arg_keys[3], (TWISTS, WALKERS), ((0, 8), (1, 16)), -0.2, 0.2), -8.0, -6.0),
        "multiplicity": place_ends(jax.random.randint(arg_keys[4], (TWISTS,), 1, 49), jax.random.fold_in(arg_keys[4], 1), 1, 48).astype(jnp.int32),
        "weights": normal_values(arg_keys[5], (LAYERS, DIN, D), DIN ** -0.5, 0.1875),
        "a_inverse": draw_a_inverse(jax.random.fold_in(arg_keys[8], 71), 0),
        "s_inverse": draw_s_inverse(jax.random.fold_in(arg_keys[8], 71), 0),
    }


def reference(features, psi_grad, pair_means, energies, multiplicity, weights, a_inverse, s_inverse):
    mult_value = multiplicity.astype(jnp.float32)
    mult_total = jnp.sum(mult_value)
    walker_count = energies.shape[1]
    half_count = NE // 2
    electron_index = jnp.arange(NE)
    is_up = electron_index < half_count
    spin_table = jnp.stack([is_up, jnp.logical_not(is_up)], 1).astype(jnp.float32)

    def per_twist(items):
        feats, grads, pairs, energy, mult_one = items
        row_scale = mult_one / mult_total / (walker_count * NE)
        hidden = feats
        inputs_seen = []
        tanh_list = []
        for layer in range(LAYERS):
            spin_sums = jnp.einsum('wed,es->wsd', hidden.astype(jnp.float32), spin_table, precision=lax.Precision.HIGHEST)
            means = (spin_sums / half_count).astype(jnp.bfloat16)
            shape_full = hidden.shape
            wide = jnp.concatenate([hidden, jnp.broadcast_to(means[:, None, 0], shape_full), jnp.broadcast_to(means[:, None, 1], shape_full), pairs[layer]], -1)
            inputs_seen.append(wide)
            z_value = jnp.dot(wide.reshape(-1, DIN), weights[layer], preferred_element_type=jnp.float32).reshape(shape_full)
            tanh_value = jnp.tanh(z_value)
            tanh_list.append(tanh_value)
            if layer + 1 < LAYERS:
                hidden = (hidden.astype(jnp.float32) + tanh_value).astype(jnp.bfloat16)
        mean_energy = jnp.sum(energy) / walker_count
        centered = (energy - mean_energy)[:, None, None]
        upstream = grads.astype(jnp.float32)
        blocks_a = [None] * LAYERS
        blocks_s = [None] * LAYERS
        blocks_g = [None] * LAYERS
        for layer in reversed(range(LAYERS)):
            slope = (upstream * (1.0 - tanh_list[layer] ** 2)).astype(jnp.bfloat16)
            weighted = (centered * slope.astype(jnp.float32)).astype(jnp.bfloat16)
            left = inputs_seen[layer].reshape(-1, DIN)
            slope_flat = slope.reshape(-1, D)
            blocks_a[layer] = jnp.dot(left.T, left, preferred_element_type=jnp.float32) * row_scale
            blocks_s[layer] = jnp.dot(slope_flat.T, slope_flat, preferred_element_type=jnp.float32) * row_scale
            blocks_g[layer] = jnp.dot(left.T, weighted.reshape(-1, D), preferred_element_type=jnp.float32) * row_scale
            if layer > 0:
                layer_weight = weights[layer]
                direct = jnp.dot(slope_flat, layer_weight[:D].T, preferred_element_type=jnp.float32).reshape(upstream.shape)
                slope_total = lax.optimization_barrier(jnp.sum(slope.astype(jnp.float32), axis=1))
                up_part = jnp.dot(slope_total, layer_weight[D:2 * D].astype(jnp.float32).T, precision=lax.Precision.HIGHEST) / half_count
                down_part = jnp.dot(slope_total, layer_weight[2 * D:3 * D].astype(jnp.float32).T, precision=lax.Precision.HIGHEST) / half_count
                spin_part = jnp.where(is_up[None, :, None], up_part[:, None, :], down_part[:, None, :])
                upstream = upstream + direct + spin_part
        return (jnp.stack(blocks_a), jnp.stack(blocks_s), jnp.stack(blocks_g))
    terms_a, terms_s, terms_g = lax.map(per_twist, (features, psi_grad, pair_means, energies, mult_value))
    a_batch = lax.optimization_barrier(jnp.sum(terms_a, axis=0))
    s_batch = lax.optimization_barrier(jnp.sum(terms_s, axis=0))
    grad_all = lax.optimization_barrier(jnp.sum(terms_g, axis=0))
    half_all = jnp.einsum('lij,ljk->lik', grad_all, s_inverse, precision=lax.Precision.HIGHEST)
    natural = jnp.einsum('lij,ljk->lik', a_inverse, half_all, precision=lax.Precision.HIGHEST)
    curvature = jnp.sum(natural * grad_all)
    direction = natural * lax.rsqrt(curvature / (LAYERS * DIN * D))
    return (a_batch, s_batch, direction)
```

```python
import functools

import jax
import jax.numpy as jnp
from jax import lax
from jax.experimental import pallas as pl
from jax.experimental.pallas import tpu as pltpu
from jax.sharding import Mesh, PartitionSpec as P

F32, BF16 = jnp.float32, jnp.bfloat16
D, PAIR, DIN = 256, 128, 896
WALK, HALF, ROWS = 16, 512, 1024
B = 128
GROUP = 32
PACKED = 4352
EXTRA = 33 * B
CHUNK = PACKED // GROUP
ENTRIES = 2 * DIN * D
VMEM_LIMIT = 56 * 1024 * 1024


def dot_t(a, b):
    return lax.dot_general(a, b, (((0,), (0,)), ((), ())), preferred_element_type=F32)


def dot_nt(a, b):
    return lax.dot_general(a, b, (((1,), (1,)), ((), ())), preferred_element_type=F32)


def dot(a, b):
    return jnp.dot(a, b, preferred_element_type=F32)


def split(a):
    high = a.astype(BF16)
    return high, (a - high.astype(F32)).astype(BF16)


def per_walker(a):
    n = a.shape[1]
    return jnp.broadcast_to(a[:, None, :], (WALK, HALF // WALK, n)).reshape(HALF, n)


def square_iotas():
    return lax.broadcasted_iota(jnp.int32, (B, B), 0), lax.broadcasted_iota(jnp.int32, (B, B), 1)


def factors_kernel(
    feat, pair, psi, other, weights, energy, mean, scale, mult, out, x_s, s_s, d_s, m_s
):
    mp = lax.axis_index("c")
    own_row = pl.multiple_of(D + D * mp, D)
    oth_row = pl.multiple_of(2 * D - D * mp, D)
    x_s[0, :HALF, :D] = feat[...]
    x_s[0, HALF:, :D] = other[:, :D].astype(BF16)
    for l in range(2):
        x_s[l, :HALF, D:] = pair[l]
        x_s[l, HALF:, D:] = other[:, 2 * D + l * PAIR : 2 * D + (l + 1) * PAIR].astype(BF16)
    group = lax.broadcasted_iota(jnp.int32, (2 * WALK, ROWS), 1) // (HALF // WALK)
    pick = (group == lax.broadcasted_iota(jnp.int32, (2 * WALK, ROWS), 0)).astype(BF16)

    for l in range(2):
        means = (dot(pick, x_s[l, :, :D]) * (1.0 / 32.0)).astype(BF16)
        m_s[l] = means
        z_walk = dot(means[:WALK], weights[l, pl.ds(own_row, D), :]) + dot(
            means[WALK:], weights[l, pl.ds(oth_row, D), :]
        )
        z_wide = per_walker(z_walk)
        for half in range(2):
            rows = slice(half * HALF, (half + 1) * HALF)
            z = dot(x_s[l, rows, :D], weights[l, :D, :]) + dot(
                x_s[l, rows, D:], weights[l, 3 * D :, :]
            )
            t = jnp.tanh(z + z_wide)
            d_s[l, rows, :] = 1.0 - t * t
            if l == 0:
                x_s[1, rows, :D] = (x_s[0, rows, :D].astype(F32) + t).astype(BF16)

    s_s[1, :HALF, :] = (psi[...].astype(F32) * d_s[1, :HALF, :]).astype(BF16)
    s_s[1, HALF:, :] = (other[:, D : 2 * D] * d_s[1, HALF:, :]).astype(BF16)
    q_both = dot(pick, s_s[1])
    q_high, q_low = split(q_both[:WALK] + q_both[WALK:])
    for half in range(2):
        rows = slice(half * HALF, (half + 1) * HALF)
        w_spin = weights[1, pl.ds(own_row if half == 0 else oth_row, D), :]
        spin = (dot_nt(q_high, w_spin) + dot_nt(q_low, w_spin)) * (1.0 / 32.0)
        up = psi[...].astype(F32) if half == 0 else other[:, D : 2 * D]
        u = up + dot_nt(s_s[1, rows, :], weights[1, :D, :]) + per_walker(spin)
        s_s[0, rows, :] = (u * d_s[0, rows, :]).astype(BF16)

    l = mp
    row_scale = scale[0, 0]
    x = x_s[l]
    s = s_s[l]
    centered = energy[...] - mean[0, 0]
    c_wide = jnp.broadcast_to(centered, (WALK, HALF // WALK, D)).reshape(HALF, D)
    c = jnp.concatenate(
        [(c_wide * s[:HALF].astype(F32)).astype(BF16), (c_wide * s[HALF:].astype(F32)).astype(BF16)], 0
    )
    h, p = x[:, :D], x[:, D:]
    row, col = square_iotas()

    def put(slot, value):
        out[slot * B : (slot + 1) * B, :] = value * row_scale

    def put_symmetric(slot, line, full):
        low = full[B:, B:]
        put(slot, jnp.where(col >= row, full[:B, :B], low))
        put(slot + 1, full[:B, B:])
        out[EXTRA + line : EXTRA + line + 1, :] = (
            jnp.sum(jnp.where(col == row, low, 0.0), axis=0, keepdims=True) * row_scale
        )

    out[EXTRA:, :] = jnp.zeros((PACKED - EXTRA, B), F32)
    put_symmetric(0, 0, dot_t(h, h))
    hp = dot_t(h, p)
    put(11, hp[:B])
    put(12, hp[B:])
    put(10, dot_t(p, p))
    hc = dot_t(h, c)
    pc = dot_t(p, c)
    for j in range(2):
        cols = slice(j * B, (j + 1) * B)
        put(19 + j, hc[:B, cols])
        put(21 + j, hc[B:, cols])
        put(31 + j, pc[:, cols])
    put_symmetric(17, 3, dot_t(s, s))

    means = m_s[l]
    up_first = mp == 0
    up = jnp.where(up_first, means[:WALK].astype(F32), means[WALK:].astype(F32)).astype(BF16)
    down = jnp.where(up_first, means[WALK:].astype(F32), means[:WALK].astype(F32)).astype(BF16)
    both = jnp.concatenate([up, down], 1)
    mm = dot_t(both, both) * 64.0
    put_symmetric(2, 1, mm[:D, :D])
    put_symmetric(4, 2, mm[D:, D:])
    for i in range(2):
        for j in range(2):
            put(6 + 2 * i + j, mm[i * B : (i + 1) * B, D + j * B : D + (j + 1) * B])
    totals = dot(pick, jnp.concatenate([p, c], 1))
    t_high, t_low = split(totals[:WALK] + totals[WALK:])
    side = dot_t(jnp.concatenate([both, both], 0), jnp.concatenate([t_high, t_low], 0))
    for i in range(4):
        rows = slice(i * B, (i + 1) * B)
        put(13 + i, side[rows, :B])
        put(23 + 2 * i, side[rows, B : 2 * B])
        put(24 + 2 * i, side[rows, 2 * B :])
    out[EXTRA + 4 : EXTRA + 5, :] = jnp.full((1, B), mult[0, 0], F32)


def finish_kernel(packed, a_inverse, s_inverse, a_out, s_out, natural, curvature):
    row, col = square_iotas()
    inverse = 1.0 / packed[EXTRA + 4 : EXTRA + 5, :]

    def get(slot):
        return packed[slot * B : (slot + 1) * B, :] * inverse

    def symmetric(slot, line):
        tri = get(slot)
        off = get(slot + 1)
        flipped = tri.T
        diag = packed[EXTRA + line : EXTRA + line + 1, :] * inverse
        first = jnp.where(col >= row, tri, flipped)
        second = jnp.where(col < row, tri, flipped)
        second = jnp.where(col == row, jnp.broadcast_to(diag, (B, B)), second)
        return [[first, off], [off.T, second]]

    def place(target, i, j, value):
        target[i * B : (i + 1) * B, j * B : (j + 1) * B] = value

    ss = symmetric(17, 3)
    hh = symmetric(0, 0)
    for i in range(2):
        for j in range(2):
            place(s_out, i, j, ss[i][j])
            place(a_out, i, j, hh[i][j])
    uu = symmetric(2, 1)
    dd = symmetric(4, 2)
    ud = [[get(6 + 2 * i + j) for j in range(2)] for i in range(2)]
    du = [[ud[j][i].T for j in range(2)] for i in range(2)]
    for i in range(2):
        for j in range(2):
            place(a_out, 2 + i, 2 + j, uu[i][j])
            place(a_out, 4 + i, 4 + j, dd[i][j])
            place(a_out, 2 + i, 4 + j, ud[i][j])
            place(a_out, 4 + i, 2 + j, du[i][j])
            place(a_out, i, 2 + j, (uu[i][j] + du[i][j]) * 0.5)
            place(a_out, i, 4 + j, (ud[i][j] + dd[i][j]) * 0.5)
            place(a_out, 2 + i, j, (uu[i][j] + ud[i][j]) * 0.5)
            place(a_out, 4 + i, j, (du[i][j] + dd[i][j]) * 0.5)
    place(a_out, 6, 6, get(10))
    for i in range(6):
        block = get(11 + i)
        place(a_out, i, 6, block)
        place(a_out, 6, i, block.T)

    grad = jnp.concatenate(
        [jnp.concatenate([get(19 + 2 * i), get(20 + 2 * i)], 1) for i in range(7)], 0
    )
    g_high, g_low = split(grad)
    s_high, s_low = split(s_inverse[...])
    half = dot(g_high, s_high) + (dot(g_high, s_low) + dot(g_low, s_high))
    h_high, h_low = split(half)
    total = jnp.zeros((1, D), F32)
    for i in range(7):
        rows = slice(i * B, (i + 1) * B)
        a_high, a_low = split(a_inverse[rows, :])
        part = dot(a_high, h_high) + (dot(a_high, h_low) + dot(a_low, h_high))
        natural[rows, :] = part
        total = total + jnp.sum(part * grad[rows, :], axis=0, keepdims=True)
    curvature[...] = jnp.broadcast_to(jnp.sum(total, axis=1, keepdims=True), (1, B))


def vmem(count):
    return [pl.BlockSpec(memory_space=pltpu.VMEM)] * count


def body(features, psi_grad, pair_means, energies, multiplicity, weights, a_inverse, s_inverse):
    feat = features.reshape(HALF, D)
    psi = psi_grad.reshape(HALF, D)
    pair = pair_means.reshape(2, HALF, PAIR)
    swap = [(0, 1), (1, 0)]
    sent = jnp.concatenate([feat, psi, pair[0], pair[1]], 1).astype(F32)
    other = lax.ppermute(sent, "c", swap)

    total = jnp.broadcast_to(jnp.sum(energies), (1, B))
    for axis in ("x", "zh"):
        total = total + sum(
            lax.ppermute(total, axis, [(i, (i + k) % 4) for i in range(4)]) for k in (1, 2, 3)
        )
    mean = total / 256.0
    energy = jnp.broadcast_to(energies.reshape(WALK, 1, 1), (WALK, 1, D))
    mult = jnp.broadcast_to(multiplicity.astype(F32).reshape(1, 1), (1, B))

    packed = pl.pallas_call(
        factors_kernel,
        out_shape=jax.ShapeDtypeStruct((PACKED, B), F32),
        in_specs=vmem(6) + [pl.BlockSpec(memory_space=pltpu.SMEM)] * 3,
        out_specs=pl.BlockSpec(memory_space=pltpu.VMEM),
        scratch_shapes=[
            pltpu.VMEM((2, ROWS, D + PAIR), BF16),
            pltpu.VMEM((2, ROWS, D), BF16),
            pltpu.VMEM((2, ROWS, D), F32),
            pltpu.VMEM((2, 2 * WALK, D), BF16),
        ],
        compiler_params=pltpu.CompilerParams(vmem_limit_bytes=VMEM_LIMIT),
        name="factors",
    )(feat, pair, psi, other, weights, energy, mean, mult / 16384.0, mult / 16.0)

    ring = ("zl", "y", "x")
    parts = lax.all_to_all(packed, ring, 0, 0, tiled=True)
    mine = jnp.sum(parts.reshape(GROUP, CHUNK, B), axis=0)
    one, two, three = (
        lax.ppermute(mine, "zh", [(i, (i + k) % 4) for i in range(4)]) for k in (1, 2, 3)
    )
    mine = (mine + two) + (one + three)
    copies = jnp.broadcast_to(mine[None], (GROUP, CHUNK, B)).reshape(PACKED, B)
    summed = lax.all_to_all(copies, ring, 0, 0, tiled=True)

    a_sum, s_sum, natural, curvature = pl.pallas_call(
        finish_kernel,
        out_shape=(
            jax.ShapeDtypeStruct((DIN, DIN), F32),
            jax.ShapeDtypeStruct((D, D), F32),
            jax.ShapeDtypeStruct((DIN, D), F32),
            jax.ShapeDtypeStruct((1, B), F32),
        ),
        in_specs=vmem(3),
        out_specs=tuple(vmem(4)),
        compiler_params=pltpu.CompilerParams(vmem_limit_bytes=VMEM_LIMIT),
        name="finish",
    )(summed, a_inverse[0], s_inverse[0])
    curvature = curvature + lax.ppermute(curvature, "c", swap)
    direction = natural * lax.rsqrt(curvature[:, :1] / ENTRIES)
    return a_sum[None], s_sum[None], direction[None]


def solution(mesh):
    fine = Mesh(mesh.devices.reshape(2, 4, 4, 4, 2), ("zl", "y", "zh", "x", "c"))
    twist, walker = ("zl", "y"), ("zh", "x")
    return jax.shard_map(
        body,
        mesh=fine,
        in_specs=(
            P(twist, walker, "c", None),
            P(twist, walker, "c", None),
            P(twist, None, walker, "c", None),
            P(twist, walker),
            P(twist),
            P(),
            P("c", None, None),
            P("c", None, None),
        ),
        out_specs=(P("c", None, None),) * 3,
        check_vma=False,
    )
```

```python
import jax
import jax.numpy as jnp
from jax import lax
from jax.experimental import pallas as pl
from jax.experimental.pallas import tpu as pltpu
from jax.sharding import Mesh, PartitionSpec as P

F32, BF16 = jnp.float32, jnp.bfloat16
D, PAIR, DIN = 256, 128, 896
WALK, HALF, ROWS = 16, 512, 1024
B = 128
GROUP = 32
PACKED = 4352
EXTRA = 33 * B
CHUNK = PACKED // GROUP
ENTRIES = 2 * DIN * D


def dot_t(a, b):
    return lax.dot_general(a, b, (((0,), (0,)), ((), ())), preferred_element_type=F32)


def dot_nt(a, b):
    return lax.dot_general(a, b, (((1,), (1,)), ((), ())), preferred_element_type=F32)


def dot(a, b):
    return jnp.dot(a, b, preferred_element_type=F32)


def split(a):
    high = a.astype(BF16)
    return high, (a - high.astype(F32)).astype(BF16)


def per_walker(a):
    n = a.shape[1]
    return jnp.broadcast_to(a[:, None, :], (WALK, HALF // WALK, n)).reshape(HALF, n)


def square_iotas():
    return lax.broadcasted_iota(jnp.int32, (B, B), 0), lax.broadcasted_iota(jnp.int32, (B, B), 1)


def walker_table():
    group = lax.broadcasted_iota(jnp.int32, (2 * WALK, ROWS), 1) // (HALF // WALK)
    return (group == lax.broadcasted_iota(jnp.int32, (2 * WALK, ROWS), 0)).astype(BF16)


def forward_kernel(feat, pair, oth_feat, oth_pair, weights, x_s, d_s, m_s):
    mp = lax.axis_index("c")
    own_row = pl.multiple_of(D + D * mp, D)
    oth_row = pl.multiple_of(2 * D - D * mp, D)
    x_s[0, :HALF, :D] = feat[...]
    x_s[0, HALF:, :D] = oth_feat[...].astype(BF16)
    for l in range(2):
        x_s[l, :HALF, D:] = pair[l]
        x_s[l, HALF:, D:] = oth_pair[l].astype(BF16)
    pick = walker_table()
    for l in range(2):
        means = (dot(pick, x_s[l, :, :D]) * (1.0 / 32.0)).astype(BF16)
        m_s[l] = means
        z_walk = dot(means[:WALK], weights[l, pl.ds(own_row, D), :]) + dot(
            means[WALK:], weights[l, pl.ds(oth_row, D), :]
        )
        z_wide = per_walker(z_walk)
        for half in range(2):
            rows = slice(half * HALF, (half + 1) * HALF)
            z = dot(x_s[l, rows, :D], weights[l, :D, :]) + dot(
                x_s[l, rows, D:], weights[l, 3 * D :, :]
            )
            t = jnp.tanh(z + z_wide)
            d_s[l, rows, :] = 1.0 - t * t
            if l == 0:
                x_s[1, rows, :D] = (x_s[0, rows, :D].astype(F32) + t).astype(BF16)


def factors_kernel(
    x_s, d_s, m_s, psi, oth_psi, weights, sum_0, sum_1, sum_2, sum_3, energy, multiplicity, out, s_s, c_s
):
    mp = lax.axis_index("c")
    own_row = pl.multiple_of(D + D * mp, D)
    oth_row = pl.multiple_of(2 * D - D * mp, D)
    pick = walker_table()
    s_s[1, :HALF, :] = (psi[...].astype(F32) * d_s[1, :HALF, :]).astype(BF16)
    s_s[1, HALF:, :] = (oth_psi[...] * d_s[1, HALF:, :]).astype(BF16)
    q_both = dot(pick, s_s[1])
    q_high, q_low = split(q_both[:WALK] + q_both[WALK:])
    for half in range(2):
        rows = slice(half * HALF, (half + 1) * HALF)
        w_spin = weights[1, pl.ds(own_row if half == 0 else oth_row, D), :]
        spin = (dot_nt(q_high, w_spin) + dot_nt(q_low, w_spin)) * (1.0 / 32.0)
        up = psi[...].astype(F32) if half == 0 else oth_psi[...]
        u = up + dot_nt(s_s[1, rows, :], weights[1, :D, :]) + per_walker(spin)
        s_s[0, rows, :] = (u * d_s[0, rows, :]).astype(BF16)

    l = mp
    mult = multiplicity[0].astype(F32)
    row_scale = mult * (1.0 / 16384.0)
    x = x_s[l]
    s = s_s[l]
    mean = jnp.sum((sum_0[...] + sum_2[...]) + (sum_1[...] + sum_3[...]), axis=1, keepdims=True)
    mean = mean * (1.0 / 256.0)
    step = HALF // WALK
    for w in range(WALK):
        centered = energy[0, w] - mean
        for first in (w * step, HALF + w * step):
            rows = slice(first, first + step)
            c_s[rows, :] = (centered * s_s[l, rows, :].astype(F32)).astype(BF16)
    c = c_s[...]
    h, p = x[:, :D], x[:, D:]
    row, col = square_iotas()

    def put(slot, value):
        out[slot * B : (slot + 1) * B, :] = value * row_scale

    def put_symmetric(slot, line, full):
        low = full[B:, B:]
        put(slot, jnp.where(col >= row, full[:B, :B], low))
        put(slot + 1, full[:B, B:])
        out[EXTRA + line : EXTRA + line + 1, :] = (
            jnp.sum(jnp.where(col == row, low, 0.0), axis=0, keepdims=True) * row_scale
        )

    out[EXTRA:, :] = jnp.zeros((PACKED - EXTRA, B), F32)
    put_symmetric(0, 0, dot_t(h, h))
    hp = dot_t(h, p)
    put(11, hp[:B])
    put(12, hp[B:])
    put(10, dot_t(p, p))
    hc = dot_t(h, c)
    pc = dot_t(p, c)
    for j in range(2):
        cols = slice(j * B, (j + 1) * B)
        put(19 + j, hc[:B, cols])
        put(21 + j, hc[B:, cols])
        put(31 + j, pc[:, cols])
    put_symmetric(17, 3, dot_t(s, s))

    means = m_s[l]
    up_first = mp == 0
    up = jnp.where(up_first, means[:WALK].astype(F32), means[WALK:].astype(F32)).astype(BF16)
    down = jnp.where(up_first, means[WALK:].astype(F32), means[:WALK].astype(F32)).astype(BF16)
    both = jnp.concatenate([up, down], 1)
    mm = dot_t(both, both) * 64.0
    put_symmetric(2, 1, mm[:D, :D])
    put_symmetric(4, 2, mm[D:, D:])
    for i in range(2):
        for j in range(2):
            put(6 + 2 * i + j, mm[i * B : (i + 1) * B, D + j * B : D + (j + 1) * B])
    totals = dot(pick, jnp.concatenate([p, c], 1))
    t_high, t_low = split(totals[:WALK] + totals[WALK:])
    side = dot_t(jnp.concatenate([both, both], 0), jnp.concatenate([t_high, t_low], 0))
    for i in range(4):
        rows = slice(i * B, (i + 1) * B)
        put(13 + i, side[rows, :B])
        put(23 + 2 * i, side[rows, B : 2 * B])
        put(24 + 2 * i, side[rows, 2 * B :])
    out[EXTRA + 4 : EXTRA + 5, :] = jnp.full((1, B), mult * (1.0 / 16.0), F32)


def unpack_kernel(packed, a_out, s_out):
    row, col = square_iotas()
    inverse = 1.0 / packed[EXTRA + 4 : EXTRA + 5, :]

    def get(slot):
        return packed[slot * B : (slot + 1) * B, :] * inverse

    def symmetric(slot, line):
        tri = get(slot)
        off = get(slot + 1)
        flipped = tri.T
        diag = packed[EXTRA + line : EXTRA + line + 1, :] * inverse
        first = jnp.where(col >= row, tri, flipped)
        second = jnp.where(col < row, tri, flipped)
        second = jnp.where(col == row, jnp.broadcast_to(diag, (B, B)), second)
        return [[first, off], [off.T, second]]

    def place(target, i, j, value):
        target[i * B : (i + 1) * B, j * B : (j + 1) * B] = value

    ss = symmetric(17, 3)
    hh = symmetric(0, 0)
    for i in range(2):
        for j in range(2):
            place(s_out, i, j, ss[i][j])
            place(a_out, i, j, hh[i][j])
    uu = symmetric(2, 1)
    dd = symmetric(4, 2)
    ud = [[get(6 + 2 * i + j) for j in range(2)] for i in range(2)]
    du = [[ud[j][i].T for j in range(2)] for i in range(2)]
    for i in range(2):
        for j in range(2):
            place(a_out, 2 + i, 2 + j, uu[i][j])
            place(a_out, 4 + i, 4 + j, dd[i][j])
            place(a_out, 2 + i, 4 + j, ud[i][j])
            place(a_out, 4 + i, 2 + j, du[i][j])
            place(a_out, i, 2 + j, (uu[i][j] + du[i][j]) * 0.5)
            place(a_out, i, 4 + j, (ud[i][j] + dd[i][j]) * 0.5)
            place(a_out, 2 + i, j, (uu[i][j] + ud[i][j]) * 0.5)
            place(a_out, 4 + i, j, (du[i][j] + dd[i][j]) * 0.5)
    place(a_out, 6, 6, get(10))
    for i in range(6):
        block = get(11 + i)
        place(a_out, i, 6, block)
        place(a_out, 6, i, block.T)


def natural_kernel(packed, a_inverse, s_inverse, natural, curvature):
    def get(slot):
        return packed[slot * B : (slot + 1) * B, :]

    grad = jnp.concatenate(
        [jnp.concatenate([get(19 + 2 * i), get(20 + 2 * i)], 1) for i in range(7)], 0
    )
    g_high, g_low = split(grad)
    s_high, s_low = split(s_inverse[...])
    half = dot(g_high, s_high) + (dot(g_high, s_low) + dot(g_low, s_high))
    h_high, h_low = split(half)
    total = jnp.zeros((1, D), F32)
    for i in range(7):
        rows = slice(i * B, (i + 1) * B)
        a_high, a_low = split(a_inverse[rows, :])
        part = dot(a_high, h_high) + (dot(a_high, h_low) + dot(a_low, h_high))
        natural[rows, :] = part
        total = total + jnp.sum(part * grad[rows, :], axis=0, keepdims=True)
    curvature[...] = jnp.broadcast_to(jnp.sum(total, axis=1, keepdims=True), (1, B))


def scale_kernel(natural, curvature, other, direction):
    total = curvature[:, :1] + other[:, :1]
    direction[...] = natural[...] * lax.rsqrt(total * (1.0 / ENTRIES))


def call(kernel, out_shapes, in_spaces, limit_mib, name, scratch=(), flops=0, moved=0):
    return pl.pallas_call(
        kernel,
        out_shape=tuple(jax.ShapeDtypeStruct(shape, dtype) for shape, dtype in out_shapes),
        in_specs=[pl.BlockSpec(memory_space=space) for space in in_spaces],
        out_specs=tuple(pl.BlockSpec(memory_space=pltpu.VMEM) for _ in out_shapes),
        scratch_shapes=scratch,
        compiler_params=pltpu.CompilerParams(vmem_limit_bytes=limit_mib * 1024 * 1024),
        cost_estimate=pl.CostEstimate(flops=flops, bytes_accessed=moved, transcendentals=0),
        name=name,
    )


V, S = pltpu.VMEM, pltpu.SMEM


def body(features, psi_grad, pair_means, energies, multiplicity, weights, a_inverse, s_inverse):
    feat = features.reshape(HALF, D)
    psi = psi_grad.reshape(HALF, D)
    pair = pair_means.reshape(2, HALF, PAIR)
    swap = [(0, 1), (1, 0)]

    def turned(value, axis):
        return [lax.ppermute(value, axis, [(i, (i + k) % 4) for i in range(4)]) for k in (1, 2, 3)]

    one, two, three = turned(energies, "x")
    row_sum = (energies + two) + (one + three)
    oth_feat = lax.ppermute(feat.astype(F32), "c", swap)
    oth_pair = lax.ppermute(pair.astype(F32), "c", swap)
    oth_psi = lax.ppermute(psi.astype(F32), "c", swap)
    one, two, three = turned(row_sum, "zh")

    x_s, d_s, m_s = call(
        forward_kernel,
        [((2, ROWS, D + PAIR), BF16), ((2, ROWS, D), F32), ((2, 2 * WALK, D), BF16)],
        [V] * 5,
        16,
        "forward",
        flops=1_000_000_000,
        moved=6_000_000,
    )(feat, pair, oth_feat, oth_pair, weights)
    (packed,) = call(
        factors_kernel,
        [((PACKED, B), F32)],
        [V] * 10 + [S] * 2,
        20,
        "factors",
        scratch=[pltpu.VMEM((2, ROWS, D), BF16), pltpu.VMEM((ROWS, D), BF16)],
        flops=1_500_000_000,
        moved=8_000_000,
    )(x_s, d_s, m_s, psi, oth_psi, weights, row_sum, one, two, three, energies, multiplicity)

    ring = ("zl", "y", "x")
    parts = lax.all_to_all(packed, ring, 0, 0, tiled=True)
    mine = jnp.sum(parts.reshape(GROUP, CHUNK, B), axis=0)
    one, two, three = turned(mine, "zh")
    mine = (mine + two) + (one + three)
    copies = jnp.broadcast_to(mine[None], (GROUP, CHUNK, B)).reshape(PACKED, B)
    summed = lax.all_to_all(copies, ring, 0, 0, tiled=True)

    natural, curvature = call(
        natural_kernel,
        [((DIN, D), F32), ((1, B), F32)],
        [V] * 3,
        18,
        "natural",
        flops=1_500_000_000,
        moved=5_000_000,
    )(summed, a_inverse[0], s_inverse[0])
    other = lax.ppermute(curvature, "c", swap)
    a_sum, s_sum = call(
        unpack_kernel,
        [((DIN, DIN), F32), ((D, D), F32)],
        [V],
        14,
        "unpack",
        flops=10_000_000,
        moved=6_000_000,
    )(summed)
    (direction,) = call(
        scale_kernel, [((DIN, D), F32)], [V] * 3, 6, "scale", flops=1_000_000, moved=2_000_000
    )(natural, curvature, other)
    return a_sum[None], s_sum[None], direction[None]


def solution(mesh):
    fine = Mesh(mesh.devices.reshape(2, 4, 4, 4, 2), ("zl", "y", "zh", "x", "c"))
    twist, walker = ("zl", "y"), ("zh", "x")
    return jax.shard_map(
        body,
        mesh=fine,
        in_specs=(
            P(twist, walker, "c", None),
            P(twist, walker, "c", None),
            P(twist, None, walker, "c", None),
            P(twist, walker),
            P(twist),
            P(),
            P("c", None, None),
            P("c", None, None),
        ),
        out_specs=(P("c", None, None),) * 3,
        check_vma=False,
    )
```

```python
import jax
import jax.numpy as jnp
from jax import lax
from jax.experimental import pallas as pl
from jax.experimental.pallas import tpu as pltpu
from jax.sharding import Mesh, PartitionSpec as P

F32, BF16 = jnp.float32, jnp.bfloat16
D, PAIR, DIN = 256, 128, 896
WALK, HALF, ROWS = 16, 512, 1024
B = 128
GROUP = 16
SLOTS = 17
KEPT = SLOTS * B
CHUNK = KEPT // GROUP
STREAMS = ((0, 6), (6, 12), (12, 17))
ENTRIES = 2 * DIN * D


def dot_t(a, b):
    return lax.dot_general(a, b, (((0,), (0,)), ((), ())), preferred_element_type=F32)


def dot_nt(a, b):
    return lax.dot_general(a, b, (((1,), (1,)), ((), ())), preferred_element_type=F32)


def dot(a, b):
    return jnp.dot(a, b, preferred_element_type=F32)


def split(a):
    high = a.astype(BF16)
    return high, (a - high.astype(F32)).astype(BF16)


def per_walker(a):
    n = a.shape[1]
    return jnp.broadcast_to(a[:, None, :], (WALK, HALF // WALK, n)).reshape(HALF, n)


def square_iotas():
    return lax.broadcasted_iota(jnp.int32, (B, B), 0), lax.broadcasted_iota(jnp.int32, (B, B), 1)


def own_parity():
    return lax.rem(lax.axis_index("x") + lax.axis_index("y") + lax.axis_index("zl"), 2)


def walker_table():
    group = lax.broadcasted_iota(jnp.int32, (2 * WALK, ROWS), 1) // (HALF // WALK)
    return (group == lax.broadcasted_iota(jnp.int32, (2 * WALK, ROWS), 0)).astype(BF16)


def widen_kernel(feat, psi, pair, energies, sent, spread):
    sent[:, :D] = feat[...].astype(F32)
    sent[:, D : 2 * D] = psi[...].astype(F32)
    for l in range(2):
        sent[:, 2 * D + l * PAIR : 2 * D + (l + 1) * PAIR] = pair[l].astype(F32)
    spread[...] = jnp.broadcast_to(energies[...], (WALK, WALK))


def forward_kernel(feat, pair, other, weights, x_s, d_s, m_s):
    mp = lax.axis_index("c")
    own_row = pl.multiple_of(D + D * mp, D)
    oth_row = pl.multiple_of(2 * D - D * mp, D)
    x_s[0, :HALF, :D] = feat[...]
    x_s[0, HALF:, :D] = other[:, :D].astype(BF16)
    for l in range(2):
        x_s[l, :HALF, D:] = pair[l]
        x_s[l, HALF:, D:] = other[:, 2 * D + l * PAIR : 2 * D + (l + 1) * PAIR].astype(BF16)
    pick = walker_table()
    for l in range(2):
        means = (dot(pick, x_s[l, :, :D]) * (1.0 / 32.0)).astype(BF16)
        m_s[l] = means
        z_walk = dot(means[:WALK], weights[l, pl.ds(own_row, D), :]) + dot(
            means[WALK:], weights[l, pl.ds(oth_row, D), :]
        )
        z_wide = per_walker(z_walk)
        for half in range(2):
            rows = slice(half * HALF, (half + 1) * HALF)
            z = dot(x_s[l, rows, :D], weights[l, :D, :]) + dot(
                x_s[l, rows, D:], weights[l, 3 * D :, :]
            )
            t = jnp.tanh(z + z_wide)
            d_s[l, rows, :] = 1.0 - t * t
            if l == 0:
                x_s[1, rows, :D] = (x_s[0, rows, :D].astype(F32) + t).astype(BF16)


def factors_kernel(
    x_s, d_s, m_s, psi, other, weights, gathered, energy, multiplicity, keep, to_x, to_y, to_z, s_s, c_s, out
):
    mp = lax.axis_index("c")
    own_row = pl.multiple_of(D + D * mp, D)
    oth_row = pl.multiple_of(2 * D - D * mp, D)
    pick = walker_table()
    s_s[1, :HALF, :] = (psi[...].astype(F32) * d_s[1, :HALF, :]).astype(BF16)
    s_s[1, HALF:, :] = (other[:, D : 2 * D] * d_s[1, HALF:, :]).astype(BF16)
    q_both = dot(pick, s_s[1])
    q_high, q_low = split(q_both[:WALK] + q_both[WALK:])
    for half in range(2):
        rows = slice(half * HALF, (half + 1) * HALF)
        w_spin = weights[1, pl.ds(own_row if half == 0 else oth_row, D), :]
        spin = (dot_nt(q_high, w_spin) + dot_nt(q_low, w_spin)) * (1.0 / 32.0)
        up = psi[...].astype(F32) if half == 0 else other[:, D : 2 * D]
        u = up + dot_nt(s_s[1, rows, :], weights[1, :D, :]) + per_walker(spin)
        s_s[0, rows, :] = (u * d_s[0, rows, :]).astype(BF16)

    l = mp
    mult = multiplicity[0].astype(F32)
    row_scale = mult * (1.0 / 16384.0)
    x = x_s[l]
    s = s_s[l]
    mean = jnp.sum(jnp.sum(gathered[...], axis=0, keepdims=True), axis=1, keepdims=True) * (1.0 / 256.0)
    step = HALF // WALK
    for w in range(WALK):
        centered = energy[0, w] - mean
        for first in (w * step, HALF + w * step):
            rows = slice(first, first + step)
            c_s[rows, :] = (centered * s_s[l, rows, :].astype(F32)).astype(BF16)
    c = c_s[...]
    h, p = x[:, :D], x[:, D:]
    row, col = square_iotas()

    parity = own_parity()

    def put(slot, value):
        first = slot % SLOTS * B
        out[parity ^ (slot // SLOTS), first : first + B, :] = value * row_scale

    lines = {}

    def put_symmetric(slot, line, full):
        low = full[B:, B:]
        put(slot, jnp.where(col >= row, full[:B, :B], low))
        put(slot + 1, full[:B, B:])
        lines[line] = jnp.sum(jnp.where(col == row, low, 0.0), axis=0, keepdims=True) * row_scale

    put_symmetric(0, 0, dot_t(h, h))
    hp = dot_t(h, p)
    put(11, hp[:B])
    put(12, hp[B:])
    put(10, dot_t(p, p))
    hc = dot_t(h, c)
    pc = dot_t(p, c)
    for j in range(2):
        cols = slice(j * B, (j + 1) * B)
        put(19 + j, hc[:B, cols])
        put(21 + j, hc[B:, cols])
        put(31 + j, pc[:, cols])
    put_symmetric(17, 3, dot_t(s, s))

    means = m_s[l]
    up_first = mp == 0
    up = jnp.where(up_first, means[:WALK].astype(F32), means[WALK:].astype(F32)).astype(BF16)
    down = jnp.where(up_first, means[WALK:].astype(F32), means[:WALK].astype(F32)).astype(BF16)
    both = jnp.concatenate([up, down], 1)
    mm = dot_t(both, both) * 64.0
    put_symmetric(2, 1, mm[:D, :D])
    put_symmetric(4, 2, mm[D:, D:])
    for i in range(2):
        for j in range(2):
            put(6 + 2 * i + j, mm[i * B : (i + 1) * B, D + j * B : D + (j + 1) * B])
    totals = dot(pick, jnp.concatenate([p, c], 1))
    t_high, t_low = split(totals[:WALK] + totals[WALK:])
    side = dot_t(jnp.concatenate([both, both], 0), jnp.concatenate([t_high, t_low], 0))
    for i in range(4):
        rows = slice(i * B, (i + 1) * B)
        put(13 + i, side[rows, :B])
        put(23 + 2 * i, side[rows, B : 2 * B])
        put(24 + 2 * i, side[rows, 2 * B :])
    lines[4] = jnp.full((1, B), mult * (1.0 / 16.0), F32)
    last = KEPT - B
    out[parity ^ 1, last:, :] = jnp.zeros((B, B), F32)
    for line, value in lines.items():
        out[parity ^ 1, last + line : last + line + 1, :] = value
    keep[...] = out[0]
    for target, (first, end) in zip((to_x, to_y, to_z), STREAMS):
        target[...] = out[1, first * B : end * B, :]


def add_kernel(keep, from_x, from_y, from_z, total):
    for part, (first, end) in zip((from_x, from_y, from_z), STREAMS):
        rows = slice(first * B, end * B)
        total[rows, :] = keep[rows, :] + part[...]


def cut_kernel(kept, to_x, to_y, to_z):
    for target, (first, end) in zip((to_x, to_y, to_z), STREAMS):
        target[...] = kept[first * B : end * B, :]


def reader(kept, parts):
    parity = own_parity()

    def read(slot, first=0, size=B):
        place = slot % SLOTS
        for part, (begin, end) in zip(parts, STREAMS):
            if begin <= place < end:
                other = part[(place - begin) * B + first : (place - begin) * B + first + size, :]
        own = kept[place * B + first : place * B + first + size, :]
        return jnp.where(parity == slot // SLOTS, own, other)

    return read


def unpack_kernel(kept, from_x, from_y, from_z, a_out, s_out):
    row, col = square_iotas()
    read = reader(kept, (from_x, from_y, from_z))
    lines = read(33, 0, 8)
    inverse = 1.0 / lines[4:5, :]

    def get(slot):
        return read(slot) * inverse

    def symmetric(slot, line):
        tri = get(slot)
        off = get(slot + 1)
        flipped = tri.T
        diag = lines[line : line + 1, :] * inverse
        first = jnp.where(col >= row, tri, flipped)
        second = jnp.where(col < row, tri, flipped)
        second = jnp.where(col == row, jnp.broadcast_to(diag, (B, B)), second)
        return [[first, off], [off.T, second]]

    def place(target, i, j, value):
        target[i * B : (i + 1) * B, j * B : (j + 1) * B] = value

    ss = symmetric(17, 3)
    hh = symmetric(0, 0)
    for i in range(2):
        for j in range(2):
            place(s_out, i, j, ss[i][j])
            place(a_out, i, j, hh[i][j])
    uu = symmetric(2, 1)
    dd = symmetric(4, 2)
    ud = [[get(6 + 2 * i + j) for j in range(2)] for i in range(2)]
    du = [[ud[j][i].T for j in range(2)] for i in range(2)]
    for i in range(2):
        for j in range(2):
            place(a_out, 2 + i, 2 + j, uu[i][j])
            place(a_out, 4 + i, 4 + j, dd[i][j])
            place(a_out, 2 + i, 4 + j, ud[i][j])
            place(a_out, 4 + i, 2 + j, du[i][j])
            place(a_out, i, 2 + j, (uu[i][j] + du[i][j]) * 0.5)
            place(a_out, i, 4 + j, (ud[i][j] + dd[i][j]) * 0.5)
            place(a_out, 2 + i, j, (uu[i][j] + ud[i][j]) * 0.5)
            place(a_out, 4 + i, j, (du[i][j] + dd[i][j]) * 0.5)
    place(a_out, 6, 6, get(10))
    for i in range(6):
        block = get(11 + i)
        place(a_out, i, 6, block)
        place(a_out, 6, i, block.T)


def natural_kernel(kept, from_x, from_y, from_z, a_inverse, s_inverse, natural, curvature):
    get = reader(kept, (from_x, from_y, from_z))

    grad = jnp.concatenate(
        [jnp.concatenate([get(19 + 2 * i), get(20 + 2 * i)], 1) for i in range(7)], 0
    )
    g_high, g_low = split(grad)
    s_high, s_low = split(s_inverse[...])
    half = dot(g_high, s_high) + (dot(g_high, s_low) + dot(g_low, s_high))
    h_high, h_low = split(half)
    total = jnp.zeros((1, D), F32)
    for i in range(7):
        rows = slice(i * B, (i + 1) * B)
        a_high, a_low = split(a_inverse[rows, :])
        part = dot(a_high, h_high) + (dot(a_high, h_low) + dot(a_low, h_high))
        natural[rows, :] = part
        total = total + jnp.sum(part * grad[rows, :], axis=0, keepdims=True)
    curvature[...] = jnp.broadcast_to(jnp.sum(total, axis=1, keepdims=True), (1, B))


def scale_kernel(natural, curvature, other, direction):
    total = curvature[:, :1] + other[:, :1]
    direction[...] = natural[...] * lax.rsqrt(total * (1.0 / ENTRIES))


def call(kernel, out_shapes, in_spaces, limit_mib, name, scratch=(), flops=0, moved=0):
    return pl.pallas_call(
        kernel,
        out_shape=tuple(jax.ShapeDtypeStruct(shape, dtype) for shape, dtype in out_shapes),
        in_specs=[pl.BlockSpec(memory_space=space) for space in in_spaces],
        out_specs=tuple(pl.BlockSpec(memory_space=pltpu.VMEM) for _ in out_shapes),
        scratch_shapes=scratch,
        compiler_params=pltpu.CompilerParams(vmem_limit_bytes=limit_mib * 1024 * 1024),
        cost_estimate=pl.CostEstimate(flops=flops, bytes_accessed=moved, transcendentals=0),
        name=name,
    )


V, S = pltpu.VMEM, pltpu.SMEM


def parity_groups():
    groups = {}
    for place in range(256):
        rest, c = divmod(place, 2)
        rest, x = divmod(rest, 4)
        rest, zh = divmod(rest, 4)
        zl, y = divmod(rest, 4)
        groups.setdefault((zh, c, (x + y + zl) % 2), []).append(place)
    return [groups[key] for key in sorted(groups)]


def same_parity(value):
    axes = ("zl", "y", "zh", "x", "c")
    return lax.all_to_all(value, axes, 0, 0, axis_index_groups=parity_groups(), tiled=True)


def to_neighbours(parts):
    pairs = {"x": [(0, 1), (1, 0), (2, 3), (3, 2)], "zl": [(0, 1), (1, 0)]}
    pairs["y"] = pairs["x"]
    return [lax.ppermute(part, axis, pairs[axis]) for part, axis in zip(parts, ("x", "y", "zl"))]


def body(features, psi_grad, pair_means, energies, multiplicity, weights, a_inverse, s_inverse):
    feat = features.reshape(HALF, D)
    psi = psi_grad.reshape(HALF, D)
    pair = pair_means.reshape(2, HALF, PAIR)
    swap = [(0, 1), (1, 0)]
    streams = [(((end - first) * B, B), F32) for first, end in STREAMS]

    sent, spread = call(
        widen_kernel, [((HALF, 3 * D), F32), ((WALK, WALK), F32)], [V] * 4, 6, "widen", moved=2_400_000
    )(feat, psi, pair, energies)
    other = lax.ppermute(sent, "c", swap)
    gathered = lax.all_to_all(spread, ("zh", "x"), 0, 0, tiled=True)

    x_s, d_s, m_s = call(
        forward_kernel,
        [((2, ROWS, D + PAIR), BF16), ((2, ROWS, D), F32), ((2, 2 * WALK, D), BF16)],
        [V] * 4,
        16,
        "forward",
        flops=1_000_000_000,
        moved=6_000_000,
    )(feat, pair, other, weights)
    keep, *parts = call(
        factors_kernel,
        [((KEPT, B), F32)] + streams,
        [V] * 7 + [S] * 2,
        22,
        "factors",
        scratch=[
            pltpu.VMEM((2, ROWS, D), BF16),
            pltpu.VMEM((ROWS, D), BF16),
            pltpu.VMEM((2, KEPT, B), F32),
        ],
        flops=1_500_000_000,
        moved=8_000_000,
    )(x_s, d_s, m_s, psi, other, weights, gathered, energies, multiplicity)

    parts = to_neighbours(parts)
    (total,) = call(add_kernel, [((KEPT, B), F32)], [V] * 4, 6, "add", moved=3_000_000)(keep, *parts)
    mine = jnp.sum(same_parity(total).reshape(GROUP, CHUNK, B), axis=0)
    one, two, three = (
        lax.ppermute(mine, "zh", [(i, (i + k) % 4) for i in range(4)]) for k in (1, 2, 3)
    )
    mine = (mine + two) + (one + three)
    kept = same_parity(jnp.broadcast_to(mine[None], (GROUP, CHUNK, B)).reshape(KEPT, B))
    parts = call(cut_kernel, streams, [V], 6, "cut", moved=2_200_000)(kept)
    parts = to_neighbours(parts)

    natural, curvature = call(
        natural_kernel,
        [((DIN, D), F32), ((1, B), F32)],
        [V] * 6,
        18,
        "natural",
        flops=1_500_000_000,
        moved=5_000_000,
    )(kept, *parts, a_inverse[0], s_inverse[0])
    other = lax.ppermute(curvature, "c", swap)
    a_sum, s_sum = call(
        unpack_kernel,
        [((DIN, DIN), F32), ((D, D), F32)],
        [V] * 4,
        14,
        "unpack",
        flops=10_000_000,
        moved=6_000_000,
    )(kept, *parts)
    (direction,) = call(
        scale_kernel, [((DIN, D), F32)], [V] * 3, 6, "scale", flops=1_000_000, moved=2_000_000
    )(natural, curvature, other)
    return a_sum[None], s_sum[None], direction[None]


def solution(mesh):
    fine = Mesh(mesh.devices.reshape(2, 4, 4, 4, 2), ("zl", "y", "zh", "x", "c"))
    twist, walker = ("zl", "y"), ("zh", "x")
    return jax.shard_map(
        body,
        mesh=fine,
        in_specs=(
            P(twist, walker, "c", None),
            P(twist, walker, "c", None),
            P(twist, None, walker, "c", None),
            P(twist, walker),
            P(twist),
            P(),
            P("c", None, None),
            P("c", None, None),
        ),
        out_specs=(P("c", None, None),) * 3,
        check_vma=False,
    )
```

```python
import jax
import jax.numpy as jnp
from jax import lax
from jax.experimental import pallas as pl
from jax.experimental.pallas import tpu as pltpu
from jax.sharding import Mesh, PartitionSpec as P

F32, BF16 = jnp.float32, jnp.bfloat16
D, PAIR, DIN = 256, 128, 896
WALK, HALF, ROWS = 16, 512, 1024
B = 128
GROUP = 16
SLOTS = 17
KEPT = SLOTS * B
CHUNK = KEPT // GROUP
GRADS, FACTORS = 7, 10
OUT_STREAMS = ((0, 5), (5, 9), (9, 12), (12, 15), (15, 17))
BACK_STREAMS = ((0, 4), (4, 7), (7, 11), (11, 14), (14, 17))
ENTRIES = 2 * DIN * D


def dot_t(a, b):
    return lax.dot_general(a, b, (((0,), (0,)), ((), ())), preferred_element_type=F32)


def dot_nt(a, b):
    return lax.dot_general(a, b, (((1,), (1,)), ((), ())), preferred_element_type=F32)


def dot(a, b):
    return jnp.dot(a, b, preferred_element_type=F32)


def split(a):
    high = a.astype(BF16)
    return high, (a - high.astype(F32)).astype(BF16)


def per_walker(a):
    n = a.shape[1]
    return jnp.broadcast_to(a[:, None, :], (WALK, HALF // WALK, n)).reshape(HALF, n)


def square_iotas():
    return lax.broadcasted_iota(jnp.int32, (B, B), 0), lax.broadcasted_iota(jnp.int32, (B, B), 1)


def own_parity():
    return lax.rem(lax.axis_index("x") + lax.axis_index("y") + lax.axis_index("zl"), 2)


def walker_table():
    group = lax.broadcasted_iota(jnp.int32, (2 * WALK, ROWS), 1) // (HALF // WALK)
    return (group == lax.broadcasted_iota(jnp.int32, (2 * WALK, ROWS), 0)).astype(BF16)


def place_of(slot):
    if 19 <= slot < 33:
        half, place = divmod(slot - 19, GRADS)
        return half, place
    half, place = divmod(slot if slot < 19 else 19, FACTORS)
    return half, place + GRADS


def factors_kernel(
    feat, pair, psi, other, oth_pair, weights, gathered, energy, multiplicity,
    keep, to_0, to_1, to_2, to_3, to_4, x_s, d_s, m_s, s_s, c_s, out
):
    mp = lax.axis_index("c")
    own_row = pl.multiple_of(D + D * mp, D)
    oth_row = pl.multiple_of(2 * D - D * mp, D)
    x_s[0, :HALF, :D] = feat[...]
    x_s[0, HALF:, :D] = other[:, :D].astype(BF16)
    for l in range(2):
        x_s[l, :HALF, D:] = pair[l]
        x_s[l, HALF:, D:] = oth_pair[l].astype(BF16)
    pick = walker_table()
    for l in range(2):
        means = (dot(pick, x_s[l, :, :D]) * (1.0 / 32.0)).astype(BF16)
        m_s[l] = means
        z_walk = dot(means[:WALK], weights[l, pl.ds(own_row, D), :]) + dot(
            means[WALK:], weights[l, pl.ds(oth_row, D), :]
        )
        z_wide = per_walker(z_walk)
        for half in range(2):
            rows = slice(half * HALF, (half + 1) * HALF)
            z = dot(x_s[l, rows, :D], weights[l, :D, :]) + dot(
                x_s[l, rows, D:], weights[l, 3 * D :, :]
            )
            t = jnp.tanh(z + z_wide)
            d_s[l, rows, :] = 1.0 - t * t
            if l == 0:
                x_s[1, rows, :D] = (x_s[0, rows, :D].astype(F32) + t).astype(BF16)

    s_s[1, :HALF, :] = (psi[...].astype(F32) * d_s[1, :HALF, :]).astype(BF16)
    s_s[1, HALF:, :] = (other[:, D : 2 * D] * d_s[1, HALF:, :]).astype(BF16)
    q_both = dot(pick, s_s[1])
    q_high, q_low = split(q_both[:WALK] + q_both[WALK:])
    for half in range(2):
        rows = slice(half * HALF, (half + 1) * HALF)
        w_spin = weights[1, pl.ds(own_row if half == 0 else oth_row, D), :]
        spin = (dot_nt(q_high, w_spin) + dot_nt(q_low, w_spin)) * (1.0 / 32.0)
        up = psi[...].astype(F32) if half == 0 else other[:, D : 2 * D]
        u = up + dot_nt(s_s[1, rows, :], weights[1, :D, :]) + per_walker(spin)
        s_s[0, rows, :] = (u * d_s[0, rows, :]).astype(BF16)

    l = mp
    mult = multiplicity[0].astype(F32)
    row_scale = mult * (1.0 / 16384.0)
    x = x_s[l]
    s = s_s[l]
    mean = jnp.sum(jnp.sum(gathered[...], axis=0, keepdims=True), axis=1, keepdims=True) * (1.0 / 256.0)
    step = HALF // WALK
    for w in range(WALK):
        centered = energy[0, w] - mean
        for first in (w * step, HALF + w * step):
            rows = slice(first, first + step)
            c_s[rows, :] = (centered * s_s[l, rows, :].astype(F32)).astype(BF16)
    c = c_s[...]
    h, p = x[:, :D], x[:, D:]
    row, col = square_iotas()

    parity = own_parity()

    def put(slot, value):
        half, place = place_of(slot)
        out[parity ^ half, place * B : (place + 1) * B, :] = value * row_scale

    lines = {}

    def put_symmetric(slot, line, full):
        low = full[B:, B:]
        put(slot, jnp.where(col >= row, full[:B, :B], low))
        put(slot + 1, full[:B, B:])
        lines[line] = jnp.sum(jnp.where(col == row, low, 0.0), axis=0, keepdims=True) * row_scale

    put_symmetric(0, 0, dot_t(h, h))
    hp = dot_t(h, p)
    put(11, hp[:B])
    put(12, hp[B:])
    put(10, dot_t(p, p))
    hc = dot_t(h, c)
    pc = dot_t(p, c)
    for j in range(2):
        cols = slice(j * B, (j + 1) * B)
        put(19 + j, hc[:B, cols])
        put(21 + j, hc[B:, cols])
        put(31 + j, pc[:, cols])
    put_symmetric(17, 3, dot_t(s, s))

    means = m_s[l]
    up_first = mp == 0
    up = jnp.where(up_first, means[:WALK].astype(F32), means[WALK:].astype(F32)).astype(BF16)
    down = jnp.where(up_first, means[WALK:].astype(F32), means[:WALK].astype(F32)).astype(BF16)
    both = jnp.concatenate([up, down], 1)
    mm = dot_t(both, both) * 64.0
    put_symmetric(2, 1, mm[:D, :D])
    put_symmetric(4, 2, mm[D:, D:])
    for i in range(2):
        for j in range(2):
            put(6 + 2 * i + j, mm[i * B : (i + 1) * B, D + j * B : D + (j + 1) * B])
    totals = dot(pick, jnp.concatenate([p, c], 1))
    t_high, t_low = split(totals[:WALK] + totals[WALK:])
    side = dot_t(jnp.concatenate([both, both], 0), jnp.concatenate([t_high, t_low], 0))
    for i in range(4):
        rows = slice(i * B, (i + 1) * B)
        put(13 + i, side[rows, :B])
        put(23 + 2 * i, side[rows, B : 2 * B])
        put(24 + 2 * i, side[rows, 2 * B :])
    lines[4] = jnp.full((1, B), mult * (1.0 / 16.0), F32)
    last = KEPT - B
    out[parity ^ 1, last:, :] = jnp.zeros((B, B), F32)
    for line, value in lines.items():
        out[parity ^ 1, last + line : last + line + 1, :] = value
    keep[...] = out[0]
    for target, (first, end) in zip((to_0, to_1, to_2, to_3, to_4), OUT_STREAMS):
        target[...] = out[1, first * B : end * B, :]


def add_kernel(keep, from_0, from_1, from_2, from_3, from_4, total):
    for part, (first, end) in zip((from_0, from_1, from_2, from_3, from_4), OUT_STREAMS):
        rows = slice(first * B, end * B)
        total[rows, :] = keep[rows, :] + part[...]


def cut_kernel(kept, to_0, to_1, to_2, to_3, to_4):
    for target, (first, end) in zip((to_0, to_1, to_2, to_3, to_4), BACK_STREAMS):
        target[...] = kept[first * B : end * B, :]


def reader(kept, parts, streams):
    parity = own_parity()

    def read(slot, size=B):
        half, place = place_of(slot)
        for part, (begin, end) in zip(parts, streams):
            if begin <= place < end:
                other = part[(place - begin) * B : (place - begin) * B + size, :]
        own = kept[place * B : place * B + size, :]
        return jnp.where(parity == half, own, other)

    return read


def unpack_kernel(kept, from_2, from_3, from_4, a_out, s_out):
    row, col = square_iotas()
    read = reader(kept, (from_2, from_3, from_4), BACK_STREAMS[2:])
    lines = read(33, 8)
    inverse = 1.0 / lines[4:5, :]

    def get(slot):
        return read(slot) * inverse

    def symmetric(slot, line):
        tri = get(slot)
        off = get(slot + 1)
        flipped = tri.T
        diag = lines[line : line + 1, :] * inverse
        first = jnp.where(col >= row, tri, flipped)
        second = jnp.where(col < row, tri, flipped)
        second = jnp.where(col == row, jnp.broadcast_to(diag, (B, B)), second)
        return [[first, off], [off.T, second]]

    def place(target, i, j, value):
        target[i * B : (i + 1) * B, j * B : (j + 1) * B] = value

    ss = symmetric(17, 3)
    hh = symmetric(0, 0)
    for i in range(2):
        for j in range(2):
            place(s_out, i, j, ss[i][j])
            place(a_out, i, j, hh[i][j])
    uu = symmetric(2, 1)
    dd = symmetric(4, 2)
    ud = [[get(6 + 2 * i + j) for j in range(2)] for i in range(2)]
    du = [[ud[j][i].T for j in range(2)] for i in range(2)]
    for i in range(2):
        for j in range(2):
            place(a_out, 2 + i, 2 + j, uu[i][j])
            place(a_out, 4 + i, 4 + j, dd[i][j])
            place(a_out, 2 + i, 4 + j, ud[i][j])
            place(a_out, 4 + i, 2 + j, du[i][j])
            place(a_out, i, 2 + j, (uu[i][j] + du[i][j]) * 0.5)
            place(a_out, i, 4 + j, (ud[i][j] + dd[i][j]) * 0.5)
            place(a_out, 2 + i, j, (uu[i][j] + ud[i][j]) * 0.5)
            place(a_out, 4 + i, j, (du[i][j] + dd[i][j]) * 0.5)
    place(a_out, 6, 6, get(10))
    for i in range(6):
        block = get(11 + i)
        place(a_out, i, 6, block)
        place(a_out, 6, i, block.T)


def natural_kernel(kept, from_0, from_1, a_inverse, s_inverse, natural, curvature):
    get = reader(kept, (from_0, from_1), BACK_STREAMS[:2])

    grad = jnp.concatenate(
        [jnp.concatenate([get(19 + 2 * i), get(20 + 2 * i)], 1) for i in range(7)], 0
    )
    g_high, g_low = split(grad)
    s_high, s_low = split(s_inverse[...])
    half = dot(g_high, s_high) + (dot(g_high, s_low) + dot(g_low, s_high))
    h_high, h_low = split(half)
    total = jnp.zeros((1, D), F32)
    for i in range(7):
        rows = slice(i * B, (i + 1) * B)
        a_high, a_low = split(a_inverse[rows, :])
        part = dot(a_high, h_high) + (dot(a_high, h_low) + dot(a_low, h_high))
        natural[rows, :] = part
        total = total + jnp.sum(part * grad[rows, :], axis=0, keepdims=True)
    curvature[...] = jnp.broadcast_to(jnp.sum(total, axis=1, keepdims=True), (1, B))


def scale_kernel(natural, curvature, other, direction):
    total = curvature[:, :1] + other[:, :1]
    direction[...] = natural[...] * lax.rsqrt(total * (1.0 / ENTRIES))


def call(kernel, out_shapes, in_spaces, limit_mib, name, scratch=(), flops=0, moved=0):
    return pl.pallas_call(
        kernel,
        out_shape=tuple(jax.ShapeDtypeStruct(shape, dtype) for shape, dtype in out_shapes),
        in_specs=[pl.BlockSpec(memory_space=space) for space in in_spaces],
        out_specs=tuple(pl.BlockSpec(memory_space=pltpu.VMEM) for _ in out_shapes),
        scratch_shapes=scratch,
        compiler_params=pltpu.CompilerParams(vmem_limit_bytes=limit_mib * 1024 * 1024),
        cost_estimate=pl.CostEstimate(flops=flops, bytes_accessed=moved, transcendentals=0),
        name=name,
    )


V, S = pltpu.VMEM, pltpu.SMEM


def parity_groups():
    groups = {}
    for place in range(256):
        rest, c = divmod(place, 2)
        rest, x = divmod(rest, 4)
        rest, zh = divmod(rest, 4)
        zl, y = divmod(rest, 4)
        groups.setdefault((zh, c, (x + y + zl) % 2), []).append(place)
    return [groups[key] for key in sorted(groups)]


def same_parity(value):
    axes = ("zl", "y", "zh", "x", "c")
    return lax.all_to_all(value, axes, 0, 0, axis_index_groups=parity_groups(), tiled=True)


def to_neighbours(parts):
    low, high = [(0, 1), (1, 0), (2, 3), (3, 2)], [(1, 2), (2, 1), (3, 0), (0, 3)]
    ways = (("x", low), ("y", low), ("zl", [(0, 1), (1, 0)]), ("x", high), ("y", high))
    return [lax.ppermute(part, axis, pairs) for part, (axis, pairs) in zip(parts, ways)]


def streams_of(streams):
    return [(((end - first) * B, B), F32) for first, end in streams]


def body(features, psi_grad, pair_means, energies, multiplicity, weights, a_inverse, s_inverse):
    feat = features.reshape(HALF, D)
    psi = psi_grad.reshape(HALF, D)
    pair = pair_means.reshape(2, HALF, PAIR)
    swap = [(0, 1), (1, 0)]

    other = lax.ppermute(jnp.concatenate([feat, psi], 1).astype(F32), "c", swap)
    oth_pair = lax.ppermute(pair.astype(F32), "c", swap)
    spread = jnp.broadcast_to(energies, (WALK, WALK))
    gathered = lax.all_to_all(spread, ("zh", "x"), 0, 0, tiled=True)

    keep, *parts = call(
        factors_kernel,
        [((KEPT, B), F32)] + streams_of(OUT_STREAMS),
        [V] * 7 + [S] * 2,
        24,
        "factors",
        scratch=[
            pltpu.VMEM((2, ROWS, D + PAIR), BF16),
            pltpu.VMEM((2, ROWS, D), F32),
            pltpu.VMEM((2, 2 * WALK, D), BF16),
            pltpu.VMEM((2, ROWS, D), BF16),
            pltpu.VMEM((ROWS, D), BF16),
            pltpu.VMEM((2, KEPT, B), F32),
        ],
        flops=2_500_000_000,
        moved=8_000_000,
    )(feat, pair, psi, other, oth_pair, weights, gathered, energies, multiplicity)

    parts = to_neighbours(parts)
    (total,) = call(add_kernel, [((KEPT, B), F32)], [V] * 6, 6, "add", moved=3_000_000)(keep, *parts)
    mine = jnp.sum(same_parity(total).reshape(GROUP, CHUNK, B), axis=0)
    one, two, three = (
        lax.ppermute(mine, "zh", [(i, (i + k) % 4) for i in range(4)]) for k in (1, 2, 3)
    )
    mine = (mine + two) + (one + three)
    kept = same_parity(jnp.broadcast_to(mine[None], (GROUP, CHUNK, B)).reshape(KEPT, B))
    parts = call(cut_kernel, streams_of(BACK_STREAMS), [V], 6, "cut", moved=2_200_000)(kept)
    parts = to_neighbours(parts)

    natural, curvature = call(
        natural_kernel,
        [((DIN, D), F32), ((1, B), F32)],
        [V] * 5,
        18,
        "natural",
        flops=1_500_000_000,
        moved=5_000_000,
    )(kept, *parts[:2], a_inverse[0], s_inverse[0])
    other = lax.ppermute(curvature, "c", swap)
    a_sum, s_sum = call(
        unpack_kernel,
        [((DIN, DIN), F32), ((D, D), F32)],
        [V] * 4,
        14,
        "unpack",
        flops=10_000_000,
        moved=6_000_000,
    )(kept, *parts[2:])
    (direction,) = call(
        scale_kernel, [((DIN, D), F32)], [V] * 3, 6, "scale", flops=1_000_000, moved=2_000_000
    )(natural, curvature, other)
    return a_sum[None], s_sum[None], direction[None]


def solution(mesh):
    fine = Mesh(mesh.devices.reshape(2, 4, 4, 4, 2), ("zl", "y", "zh", "x", "c"))
    twist, walker = ("zl", "y"), ("zh", "x")
    return jax.shard_map(
        body,
        mesh=fine,
        in_specs=(
            P(twist, walker, "c", None),
            P(twist, walker, "c", None),
            P(twist, None, walker, "c", None),
            P(twist, walker),
            P(twist),
            P(),
            P("c", None, None),
            P("c", None, None),
        ),
        out_specs=(P("c", None, None),) * 3,
        check_vma=False,
    )
```

```python
import jax
import jax.numpy as jnp
from jax import lax
from jax.experimental import pallas as pl
from jax.experimental.pallas import tpu as pltpu
from jax.sharding import Mesh, PartitionSpec as P

F32, BF16 = jnp.float32, jnp.bfloat16
D, PAIR, DIN = 256, 128, 896
WALK, HALF, ROWS = 16, 512, 1024
B = 128
GROUP = 16
SLOTS = 17
KEPT = SLOTS * B
CHUNK = KEPT // GROUP
GRADS, FACTORS = 7, 10
OUT_STREAMS = ((7, 12), (12, 17))
BACK_STREAMS = ((0, 4), (4, 7), (7, 11), (11, 14), (14, 17))
ENTRIES = 2 * DIN * D
SHIFT = 7.0


def dot_t(a, b):
    return lax.dot_general(a, b, (((0,), (0,)), ((), ())), preferred_element_type=F32)


def dot_nt(a, b):
    return lax.dot_general(a, b, (((1,), (1,)), ((), ())), preferred_element_type=F32)


def dot(a, b):
    return jnp.dot(a, b, preferred_element_type=F32)


def split(a):
    high = a.astype(BF16)
    return high, (a - high.astype(F32)).astype(BF16)


def per_walker(a):
    n = a.shape[1]
    return jnp.broadcast_to(a[:, None, :], (WALK, HALF // WALK, n)).reshape(HALF, n)


def square_iotas():
    return lax.broadcasted_iota(jnp.int32, (B, B), 0), lax.broadcasted_iota(jnp.int32, (B, B), 1)


def own_parity():
    return lax.rem(lax.axis_index("x") + lax.axis_index("y") + lax.axis_index("zl"), 2)


def walker_table():
    group = lax.broadcasted_iota(jnp.int32, (2 * WALK, ROWS), 1) // (HALF // WALK)
    return (group == lax.broadcasted_iota(jnp.int32, (2 * WALK, ROWS), 0)).astype(BF16)


def place_of(slot):
    if 19 <= slot < 33:
        half, place = divmod(slot - 19, GRADS)
        return half, place
    half, place = divmod(slot if slot < 19 else 19, FACTORS)
    return half, place + GRADS


def factors_kernel(
    feat, pair, psi, other, oth_pair, weights, half_sum, half_other, energies, energy, multiplicity,
    keep, keep_0, to_a, to_0, to_2, to_3, row_sum, x_s, d_s, m_s, s_s, c_s, out, out_0
):
    mp = lax.axis_index("c")
    own_row = pl.multiple_of(D + D * mp, D)
    oth_row = pl.multiple_of(2 * D - D * mp, D)
    x_s[0, :HALF, :D] = feat[...]
    x_s[0, HALF:, :D] = other[:, :D].astype(BF16)
    for l in range(2):
        x_s[l, :HALF, D:] = pair[l]
        x_s[l, HALF:, D:] = oth_pair[l].astype(BF16)
    pick = walker_table()
    for l in range(2):
        means = (dot(pick, x_s[l, :, :D]) * (1.0 / 32.0)).astype(BF16)
        m_s[l] = means
        z_walk = dot(means[:WALK], weights[l, pl.ds(own_row, D), :]) + dot(
            means[WALK:], weights[l, pl.ds(oth_row, D), :]
        )
        z_wide = per_walker(z_walk)
        for half in range(2):
            rows = slice(half * HALF, (half + 1) * HALF)
            z = dot(x_s[l, rows, :D], weights[l, :D, :]) + dot(
                x_s[l, rows, D:], weights[l, 3 * D :, :]
            )
            t = jnp.tanh(z + z_wide)
            d_s[l, rows, :] = 1.0 - t * t
            if l == 0:
                x_s[1, rows, :D] = (x_s[0, rows, :D].astype(F32) + t).astype(BF16)

    s_s[1, :HALF, :] = (psi[...].astype(F32) * d_s[1, :HALF, :]).astype(BF16)
    s_s[1, HALF:, :] = (other[:, D : 2 * D] * d_s[1, HALF:, :]).astype(BF16)
    q_both = dot(pick, s_s[1])
    q_high, q_low = split(q_both[:WALK] + q_both[WALK:])
    for half in range(2):
        rows = slice(half * HALF, (half + 1) * HALF)
        w_spin = weights[1, pl.ds(own_row if half == 0 else oth_row, D), :]
        spin = (dot_nt(q_high, w_spin) + dot_nt(q_low, w_spin)) * (1.0 / 32.0)
        up = psi[...].astype(F32) if half == 0 else other[:, D : 2 * D]
        u = up + dot_nt(s_s[1, rows, :], weights[1, :D, :]) + per_walker(spin)
        s_s[0, rows, :] = (u * d_s[0, rows, :]).astype(BF16)

    l = mp
    mult = multiplicity[0].astype(F32)
    row_scale = mult * (1.0 / 16384.0)
    x = x_s[l]
    s = s_s[l]
    mean = jnp.sum(energies[...], axis=1, keepdims=True) * (1.0 / WALK)
    shifted = mean + SHIFT
    zh_sum = jnp.sum(half_sum[...] + half_other[...], axis=1, keepdims=True)
    row_sum[...] = jnp.broadcast_to(zh_sum, (8, B))
    step = HALF // WALK
    for w in range(WALK):
        centered = energy[0, w] - mean
        for first in (w * step, HALF + w * step):
            rows = slice(first, first + step)
            c_s[rows, :] = (centered * s_s[l, rows, :].astype(F32)).astype(BF16)
    c = c_s[...]
    h, p = x[:, :D], x[:, D:]
    row, col = square_iotas()

    parity = own_parity()

    def put(slot, value):
        half, place = place_of(slot)
        out[parity ^ half, place * B : (place + 1) * B, :] = value * row_scale

    def put_grad(slot, centered, plain):
        half, place = place_of(slot)
        rows = slice(place * B, (place + 1) * B)
        out[parity ^ half, rows, :] = (centered + shifted * plain) * row_scale
        out_0[parity ^ half, rows, :] = plain * row_scale

    lines = {}

    def put_symmetric(slot, line, full):
        low = full[B:, B:]
        put(slot, jnp.where(col >= row, full[:B, :B], low))
        put(slot + 1, full[:B, B:])
        lines[line] = jnp.sum(jnp.where(col == row, low, 0.0), axis=0, keepdims=True) * row_scale

    put_symmetric(0, 0, dot_t(h, h))
    hp = dot_t(h, p)
    put(11, hp[:B])
    put(12, hp[B:])
    put(10, dot_t(p, p))
    hc, hs = dot_t(h, c), dot_t(h, s)
    pc, ps = dot_t(p, c), dot_t(p, s)
    for j in range(2):
        cols = slice(j * B, (j + 1) * B)
        put_grad(19 + j, hc[:B, cols], hs[:B, cols])
        put_grad(21 + j, hc[B:, cols], hs[B:, cols])
        put_grad(31 + j, pc[:, cols], ps[:, cols])
    put_symmetric(17, 3, dot_t(s, s))

    means = m_s[l]
    up_first = mp == 0
    up = jnp.where(up_first, means[:WALK].astype(F32), means[WALK:].astype(F32)).astype(BF16)
    down = jnp.where(up_first, means[WALK:].astype(F32), means[:WALK].astype(F32)).astype(BF16)
    both = jnp.concatenate([up, down], 1)
    mm = dot_t(both, both) * 64.0
    put_symmetric(2, 1, mm[:D, :D])
    put_symmetric(4, 2, mm[D:, D:])
    for i in range(2):
        for j in range(2):
            put(6 + 2 * i + j, mm[i * B : (i + 1) * B, D + j * B : D + (j + 1) * B])
    totals = dot(pick, jnp.concatenate([p, c, s], 1))
    t_high, t_low = split(totals[:WALK] + totals[WALK:])
    side = dot_t(jnp.concatenate([both, both], 0), jnp.concatenate([t_high, t_low], 0))
    for i in range(4):
        rows = slice(i * B, (i + 1) * B)
        put(13 + i, side[rows, :B])
        for j in range(2):
            at = (1 + j) * B
            put_grad(23 + 2 * i + j, side[rows, at : at + B], side[rows, at + D : at + D + B])
    lines[4] = jnp.full((1, B), mult * (1.0 / 16.0), F32)
    last = KEPT - B
    out[parity ^ 1, last:, :] = jnp.zeros((B, B), F32)
    for line, value in lines.items():
        out[parity ^ 1, last + line : last + line + 1, :] = value
    keep[...] = out[0]
    keep_0[...] = out_0[0]
    grads = GRADS * B
    to_a[:grads, :] = out[1, :grads, :]
    to_0[:grads, :] = out_0[1]
    to_a[grads:, :] = row_sum[...]
    to_0[grads:, :] = row_sum[...]
    for target, (first, end) in zip((to_2, to_3), OUT_STREAMS):
        target[...] = out[1, first * B : end * B, :]


def add_kernel(keep, keep_0, from_a, from_0, from_2, from_3, row_sum, row_two, total):
    grads = GRADS * B
    energy = (row_sum[...] + row_two[...]) + (from_a[grads:, :] + from_0[grads:, :])
    shifted = energy[:1, :] * (1.0 / 256.0) + SHIFT
    plain = keep_0[...] + from_0[:grads, :]
    total[:grads, :] = (keep[:grads, :] + from_a[:grads, :]) - shifted * plain
    for part, (first, end) in zip((from_2, from_3), OUT_STREAMS):
        rows = slice(first * B, end * B)
        total[rows, :] = keep[rows, :] + part[...]


def cut_kernel(kept, to_0, to_1, to_2, to_3, to_4):
    for target, (first, end) in zip((to_0, to_1, to_2, to_3, to_4), BACK_STREAMS):
        target[...] = kept[first * B : end * B, :]


def reader(kept, parts, streams):
    parity = own_parity()

    def read(slot, size=B):
        half, place = place_of(slot)
        for part, (begin, end) in zip(parts, streams):
            if begin <= place < end:
                other = part[(place - begin) * B : (place - begin) * B + size, :]
        own = kept[place * B : place * B + size, :]
        return jnp.where(parity == half, own, other)

    return read


def unpack_kernel(kept, from_2, from_3, from_4, a_out, s_out):
    row, col = square_iotas()
    read = reader(kept, (from_2, from_3, from_4), BACK_STREAMS[2:])
    lines = read(33, 8)
    inverse = 1.0 / lines[4:5, :]

    def get(slot):
        return read(slot) * inverse

    def symmetric(slot, line):
        tri = get(slot)
        off = get(slot + 1)
        flipped = tri.T
        diag = lines[line : line + 1, :] * inverse
        first = jnp.where(col >= row, tri, flipped)
        second = jnp.where(col < row, tri, flipped)
        second = jnp.where(col == row, jnp.broadcast_to(diag, (B, B)), second)
        return [[first, off], [off.T, second]]

    def place(target, i, j, value):
        target[i * B : (i + 1) * B, j * B : (j + 1) * B] = value

    ss = symmetric(17, 3)
    hh = symmetric(0, 0)
    for i in range(2):
        for j in range(2):
            place(s_out, i, j, ss[i][j])
            place(a_out, i, j, hh[i][j])
    uu = symmetric(2, 1)
    dd = symmetric(4, 2)
    ud = [[get(6 + 2 * i + j) for j in range(2)] for i in range(2)]
    du = [[ud[j][i].T for j in range(2)] for i in range(2)]
    for i in range(2):
        for j in range(2):
            place(a_out, 2 + i, 2 + j, uu[i][j])
            place(a_out, 4 + i, 4 + j, dd[i][j])
            place(a_out, 2 + i, 4 + j, ud[i][j])
            place(a_out, 4 + i, 2 + j, du[i][j])
            place(a_out, i, 2 + j, (uu[i][j] + du[i][j]) * 0.5)
            place(a_out, i, 4 + j, (ud[i][j] + dd[i][j]) * 0.5)
            place(a_out, 2 + i, j, (uu[i][j] + ud[i][j]) * 0.5)
            place(a_out, 4 + i, j, (du[i][j] + dd[i][j]) * 0.5)
    place(a_out, 6, 6, get(10))
    for i in range(6):
        block = get(11 + i)
        place(a_out, i, 6, block)
        place(a_out, 6, i, block.T)


def natural_kernel(kept, from_0, from_1, a_inverse, s_inverse, natural, curvature):
    get = reader(kept, (from_0, from_1), BACK_STREAMS[:2])

    grad = jnp.concatenate(
        [jnp.concatenate([get(19 + 2 * i), get(20 + 2 * i)], 1) for i in range(7)], 0
    )
    g_high, g_low = split(grad)
    s_high, s_low = split(s_inverse[...])
    half = dot(g_high, s_high) + (dot(g_high, s_low) + dot(g_low, s_high))
    h_high, h_low = split(half)
    total = jnp.zeros((1, D), F32)
    for i in range(7):
        rows = slice(i * B, (i + 1) * B)
        a_high, a_low = split(a_inverse[rows, :])
        part = dot(a_high, h_high) + (dot(a_high, h_low) + dot(a_low, h_high))
        natural[rows, :] = part
        total = total + jnp.sum(part * grad[rows, :], axis=0, keepdims=True)
    curvature[...] = jnp.broadcast_to(jnp.sum(total, axis=1, keepdims=True), (1, B))


def scale_kernel(natural, curvature, other, direction):
    total = curvature[:, :1] + other[:, :1]
    direction[...] = natural[...] * lax.rsqrt(total * (1.0 / ENTRIES))


def call(kernel, out_shapes, in_spaces, limit_mib, name, scratch=(), flops=0, moved=0):
    return pl.pallas_call(
        kernel,
        out_shape=tuple(jax.ShapeDtypeStruct(shape, dtype) for shape, dtype in out_shapes),
        in_specs=[pl.BlockSpec(memory_space=space) for space in in_spaces],
        out_specs=tuple(pl.BlockSpec(memory_space=pltpu.VMEM) for _ in out_shapes),
        scratch_shapes=scratch,
        compiler_params=pltpu.CompilerParams(vmem_limit_bytes=limit_mib * 1024 * 1024),
        cost_estimate=pl.CostEstimate(flops=flops, bytes_accessed=moved, transcendentals=0),
        name=name,
    )


V, S = pltpu.VMEM, pltpu.SMEM


def parity_groups():
    groups = {}
    for place in range(256):
        rest, c = divmod(place, 2)
        rest, x = divmod(rest, 4)
        rest, zh = divmod(rest, 4)
        zl, y = divmod(rest, 4)
        groups.setdefault((zh, c, (x + y + zl) % 2), []).append(place)
    return [groups[key] for key in sorted(groups)]


def same_parity(value):
    axes = ("zl", "y", "zh", "x", "c")
    return lax.all_to_all(value, axes, 0, 0, axis_index_groups=parity_groups(), tiled=True)


LOW, HIGH = [(0, 1), (1, 0), (2, 3), (3, 2)], [(1, 2), (2, 1), (3, 0), (0, 3)]


def to_neighbours(parts):
    ways = (("x", LOW), ("y", LOW), ("zl", [(0, 1), (1, 0)]), ("x", HIGH), ("y", HIGH))
    return [lax.ppermute(part, axis, pairs) for part, (axis, pairs) in zip(parts, ways)]


def streams_of(streams):
    return [(((end - first) * B, B), F32) for first, end in streams]


def body(features, psi_grad, pair_means, energies, multiplicity, weights, a_inverse, s_inverse):
    feat = features.reshape(HALF, D)
    psi = psi_grad.reshape(HALF, D)
    pair = pair_means.reshape(2, HALF, PAIR)
    swap = [(0, 1), (1, 0)]

    half_sum = energies + lax.ppermute(energies, "zh", LOW)
    other = lax.ppermute(jnp.concatenate([feat, psi], 1).astype(F32), "c", swap)
    oth_pair = lax.ppermute(pair.astype(F32), "c", swap)
    half_other = lax.ppermute(half_sum, "zh", HIGH)

    grads = GRADS * B
    keep, keep_0, to_a, to_0, to_2, to_3, row_sum = call(
        factors_kernel,
        [((KEPT, B), F32), ((grads, B), F32)]
        + [((grads + 8, B), F32)] * 2
        + streams_of(OUT_STREAMS)
        + [((8, B), F32)],
        [V] * 9 + [S] * 2,
        26,
        "factors",
        scratch=[
            pltpu.VMEM((2, ROWS, D + PAIR), BF16),
            pltpu.VMEM((2, ROWS, D), F32),
            pltpu.VMEM((2, 2 * WALK, D), BF16),
            pltpu.VMEM((2, ROWS, D), BF16),
            pltpu.VMEM((ROWS, D), BF16),
            pltpu.VMEM((2, KEPT, B), F32),
            pltpu.VMEM((2, grads, B), F32),
        ],
        flops=2_500_000_000,
        moved=8_000_000,
    )(feat, pair, psi, other, oth_pair, weights, half_sum, half_other, energies, energies, multiplicity)

    from_a = lax.ppermute(to_a, "x", LOW)
    from_0 = lax.ppermute(to_0, "x", HIGH)
    from_2 = lax.ppermute(to_2, "y", LOW)
    from_3 = lax.ppermute(to_3, "zl", swap)
    row_two = lax.ppermute(row_sum, "x", [(0, 2), (1, 3), (2, 0), (3, 1)])
    (total,) = call(add_kernel, [((KEPT, B), F32)], [V] * 8, 8, "add", moved=3_000_000)(
        keep, keep_0, from_a, from_0, from_2, from_3, row_sum, row_two
    )
    mine = jnp.sum(same_parity(total).reshape(GROUP, CHUNK, B), axis=0)
    one, two, three = (
        lax.ppermute(mine, "zh", [(i, (i + k) % 4) for i in range(4)]) for k in (1, 2, 3)
    )
    mine = (mine + two) + (one + three)
    kept = same_parity(jnp.broadcast_to(mine[None], (GROUP, CHUNK, B)).reshape(KEPT, B))
    parts = call(cut_kernel, streams_of(BACK_STREAMS), [V], 6, "cut", moved=2_200_000)(kept)
    parts = to_neighbours(parts)

    natural, curvature = call(
        natural_kernel,
        [((DIN, D), F32), ((1, B), F32)],
        [V] * 5,
        18,
        "natural",
        flops=1_500_000_000,
        moved=5_000_000,
    )(kept, *parts[:2], a_inverse[0], s_inverse[0])
    other = lax.ppermute(curvature, "c", swap)
    a_sum, s_sum = call(
        unpack_kernel,
        [((DIN, DIN), F32), ((D, D), F32)],
        [V] * 4,
        14,
        "unpack",
        flops=10_000_000,
        moved=6_000_000,
    )(kept, *parts[2:])
    (direction,) = call(
        scale_kernel, [((DIN, D), F32)], [V] * 3, 6, "scale", flops=1_000_000, moved=2_000_000
    )(natural, curvature, other)
    return a_sum[None], s_sum[None], direction[None]


def solution(mesh):
    fine = Mesh(mesh.devices.reshape(2, 4, 4, 4, 2), ("zl", "y", "zh", "x", "c"))
    twist, walker = ("zl", "y"), ("zh", "x")
    return jax.shard_map(
        body,
        mesh=fine,
        in_specs=(
            P(twist, walker, "c", None),
            P(twist, walker, "c", None),
            P(twist, None, walker, "c", None),
            P(twist, walker),
            P(twist),
            P(),
            P("c", None, None),
            P("c", None, None),
        ),
        out_specs=(P("c", None, None),) * 3,
        check_vma=False,
    )
```

```python
import jax
import jax.numpy as jnp
from jax import lax
from jax.experimental import pallas as pl
from jax.experimental.pallas import tpu as pltpu
from jax.sharding import Mesh, PartitionSpec as P

F32, BF16 = jnp.float32, jnp.bfloat16
D, PAIR, DIN = 256, 128, 896
WALK, HALF, ROWS = 16, 512, 1024
B = 128
GROUP = 16
SLOTS = 17
KEPT = SLOTS * B
CHUNK = KEPT // GROUP
GRADS, FACTORS = 7, 10
OUT_STREAMS = ((7, 12), (12, 17))
BACK_STREAMS = ((0, 4), (4, 7), (7, 11), (11, 14), (14, 17))
ENTRIES = 2 * DIN * D
SHIFT = 7.0


def dot_t(a, b):
    return lax.dot_general(a, b, (((0,), (0,)), ((), ())), preferred_element_type=F32)


def dot_nt(a, b):
    return lax.dot_general(a, b, (((1,), (1,)), ((), ())), preferred_element_type=F32)


def dot(a, b):
    return jnp.dot(a, b, preferred_element_type=F32)


def split(a):
    high = a.astype(BF16)
    return high, (a - high.astype(F32)).astype(BF16)


def per_walker(a):
    n = a.shape[1]
    return jnp.broadcast_to(a[:, None, :], (WALK, HALF // WALK, n)).reshape(HALF, n)


def square_iotas():
    return lax.broadcasted_iota(jnp.int32, (B, B), 0), lax.broadcasted_iota(jnp.int32, (B, B), 1)


def own_parity():
    return lax.rem(lax.axis_index("x") + lax.axis_index("y") + lax.axis_index("zl"), 2)


def walker_table():
    group = lax.broadcasted_iota(jnp.int32, (2 * WALK, ROWS), 1) // (HALF // WALK)
    return (group == lax.broadcasted_iota(jnp.int32, (2 * WALK, ROWS), 0)).astype(BF16)


def place_of(slot):
    if 19 <= slot < 33:
        half, place = divmod(slot - 19, GRADS)
        return half, place
    half, place = divmod(slot if slot < 19 else 19, FACTORS)
    return half, place + GRADS


def factors_kernel(
    feat, pair, psi, other, oth_pair, weights, energies, energy, multiplicity,
    keep, keep_0, to_a, to_0, to_2, to_3, x_s, d_s, m_s, s_s, c_s, out, out_0
):
    mp = lax.axis_index("c")
    own_row = pl.multiple_of(D + D * mp, D)
    oth_row = pl.multiple_of(2 * D - D * mp, D)
    x_s[0, :HALF, :D] = feat[...]
    x_s[0, HALF:, :D] = other[:, :D].astype(BF16)
    for l in range(2):
        x_s[l, :HALF, D:] = pair[l]
        x_s[l, HALF:, D:] = oth_pair[l].astype(BF16)
    pick = walker_table()
    for l in range(2):
        means = (dot(pick, x_s[l, :, :D]) * (1.0 / 32.0)).astype(BF16)
        m_s[l] = means
        z_walk = dot(means[:WALK], weights[l, pl.ds(own_row, D), :]) + dot(
            means[WALK:], weights[l, pl.ds(oth_row, D), :]
        )
        z_wide = per_walker(z_walk)
        for half in range(2):
            rows = slice(half * HALF, (half + 1) * HALF)
            z = dot(x_s[l, rows, :D], weights[l, :D, :]) + dot(
                x_s[l, rows, D:], weights[l, 3 * D :, :]
            )
            t = jnp.tanh(z + z_wide)
            d_s[l, rows, :] = 1.0 - t * t
            if l == 0:
                x_s[1, rows, :D] = (x_s[0, rows, :D].astype(F32) + t).astype(BF16)

    s_s[1, :HALF, :] = (psi[...].astype(F32) * d_s[1, :HALF, :]).astype(BF16)
    s_s[1, HALF:, :] = (other[:, D : 2 * D] * d_s[1, HALF:, :]).astype(BF16)
    q_both = dot(pick, s_s[1])
    q_high, q_low = split(q_both[:WALK] + q_both[WALK:])
    for half in range(2):
        rows = slice(half * HALF, (half + 1) * HALF)
        w_spin = weights[1, pl.ds(own_row if half == 0 else oth_row, D), :]
        spin = (dot_nt(q_high, w_spin) + dot_nt(q_low, w_spin)) * (1.0 / 32.0)
        up = psi[...].astype(F32) if half == 0 else other[:, D : 2 * D]
        u = up + dot_nt(s_s[1, rows, :], weights[1, :D, :]) + per_walker(spin)
        s_s[0, rows, :] = (u * d_s[0, rows, :]).astype(BF16)

    l = mp
    mult = multiplicity[0].astype(F32)
    row_scale = mult * (1.0 / 16384.0)
    x = x_s[l]
    s = s_s[l]
    mean = jnp.sum(energies[...], axis=1, keepdims=True) * (1.0 / WALK)
    shifted = mean + SHIFT
    step = HALF // WALK
    for w in range(WALK):
        centered = energy[0, w] - mean
        for first in (w * step, HALF + w * step):
            rows = slice(first, first + step)
            c_s[0, rows, :], c_s[1, rows, :] = split(centered * s_s[l, rows, :].astype(F32))
    c, c_low = c_s[0], c_s[1]
    h, p = x[:, :D], x[:, D:]
    row, col = square_iotas()

    parity = own_parity()

    def put(slot, value):
        half, place = place_of(slot)
        out[parity ^ half, place * B : (place + 1) * B, :] = value * row_scale

    def put_grad(slot, centered, plain):
        half, place = place_of(slot)
        rows = slice(place * B, (place + 1) * B)
        out[parity ^ half, rows, :] = (centered + shifted * plain) * row_scale
        out_0[parity ^ half, rows, :] = plain * row_scale

    lines = {}

    def put_symmetric(slot, line, full):
        low = full[B:, B:]
        put(slot, jnp.where(col >= row, full[:B, :B], low))
        put(slot + 1, full[:B, B:])
        lines[line] = jnp.sum(jnp.where(col == row, low, 0.0), axis=0, keepdims=True) * row_scale

    put_symmetric(0, 0, dot_t(h, h))
    hp = dot_t(h, p)
    put(11, hp[:B])
    put(12, hp[B:])
    put(10, dot_t(p, p))
    hc, hs = dot_t(h, c) + dot_t(h, c_low), dot_t(h, s)
    pc, ps = dot_t(p, c) + dot_t(p, c_low), dot_t(p, s)
    for j in range(2):
        cols = slice(j * B, (j + 1) * B)
        put_grad(19 + j, hc[:B, cols], hs[:B, cols])
        put_grad(21 + j, hc[B:, cols], hs[B:, cols])
        put_grad(31 + j, pc[:, cols], ps[:, cols])
    put_symmetric(17, 3, dot_t(s, s))

    means = m_s[l]
    up_first = mp == 0
    up = jnp.where(up_first, means[:WALK].astype(F32), means[WALK:].astype(F32)).astype(BF16)
    down = jnp.where(up_first, means[WALK:].astype(F32), means[:WALK].astype(F32)).astype(BF16)
    both = jnp.concatenate([up, down], 1)
    mm = dot_t(both, both) * 64.0
    put_symmetric(2, 1, mm[:D, :D])
    put_symmetric(4, 2, mm[D:, D:])
    for i in range(2):
        for j in range(2):
            put(6 + 2 * i + j, mm[i * B : (i + 1) * B, D + j * B : D + (j + 1) * B])
    totals = jnp.concatenate([dot(pick, p), dot(pick, c) + dot(pick, c_low), dot(pick, s)], 1)
    t_high, t_low = split(totals[:WALK] + totals[WALK:])
    side = dot_t(jnp.concatenate([both, both], 0), jnp.concatenate([t_high, t_low], 0))
    for i in range(4):
        rows = slice(i * B, (i + 1) * B)
        put(13 + i, side[rows, :B])
        for j in range(2):
            at = (1 + j) * B
            put_grad(23 + 2 * i + j, side[rows, at : at + B], side[rows, at + D : at + D + B])
    lines[4] = jnp.full((1, B), mult * (1.0 / 16.0), F32)
    last = KEPT - B
    out[parity ^ 1, last:, :] = jnp.zeros((B, B), F32)
    for line, value in lines.items():
        out[parity ^ 1, last + line : last + line + 1, :] = value
    keep[...] = out[0]
    keep_0[...] = out_0[0]
    grads = GRADS * B
    to_a[...] = out[1, :grads, :]
    to_0[...] = out_0[1]
    for target, (first, end) in zip((to_2, to_3), OUT_STREAMS):
        target[...] = out[1, first * B : end * B, :]


def tie_kernel(stream, near, far, same_stream, total):
    total[...] = near[...] + far[...]


def add_kernel(keep, keep_0, from_a, from_0, from_2, from_3, near_sum, far_sum, total):
    grads = GRADS * B
    energy = jnp.sum(near_sum[...] + far_sum[...], axis=1, keepdims=True)
    shifted = energy * (1.0 / 256.0) + SHIFT
    plain = keep_0[...] + from_0[...]
    total[:grads, :] = (keep[:grads, :] + from_a[...]) - shifted * plain
    for part, (first, end) in zip((from_2, from_3), OUT_STREAMS):
        rows = slice(first * B, end * B)
        total[rows, :] = keep[rows, :] + part[...]


def cut_kernel(kept, to_0, to_1, to_2, to_3, to_4):
    for target, (first, end) in zip((to_0, to_1, to_2, to_3, to_4), BACK_STREAMS):
        target[...] = kept[first * B : end * B, :]


def reader(kept, parts, streams):
    parity = own_parity()

    def read(slot, size=B):
        half, place = place_of(slot)
        for part, (begin, end) in zip(parts, streams):
            if begin <= place < end:
                other = part[(place - begin) * B : (place - begin) * B + size, :]
        own = kept[place * B : place * B + size, :]
        return jnp.where(parity == half, own, other)

    return read


def unpack_kernel(kept, from_2, from_3, from_4, a_out, s_out):
    row, col = square_iotas()
    read = reader(kept, (from_2, from_3, from_4), BACK_STREAMS[2:])
    lines = read(33, 8)
    inverse = 1.0 / lines[4:5, :]

    def get(slot):
        return read(slot) * inverse

    def symmetric(slot, line):
        tri = get(slot)
        off = get(slot + 1)
        flipped = tri.T
        diag = lines[line : line + 1, :] * inverse
        first = jnp.where(col >= row, tri, flipped)
        second = jnp.where(col < row, tri, flipped)
        second = jnp.where(col == row, jnp.broadcast_to(diag, (B, B)), second)
        return [[first, off], [off.T, second]]

    def place(target, i, j, value):
        target[i * B : (i + 1) * B, j * B : (j + 1) * B] = value

    ss = symmetric(17, 3)
    hh = symmetric(0, 0)
    for i in range(2):
        for j in range(2):
            place(s_out, i, j, ss[i][j])
            place(a_out, i, j, hh[i][j])
    uu = symmetric(2, 1)
    dd = symmetric(4, 2)
    ud = [[get(6 + 2 * i + j) for j in range(2)] for i in range(2)]
    du = [[ud[j][i].T for j in range(2)] for i in range(2)]
    for i in range(2):
        for j in range(2):
            place(a_out, 2 + i, 2 + j, uu[i][j])
            place(a_out, 4 + i, 4 + j, dd[i][j])
            place(a_out, 2 + i, 4 + j, ud[i][j])
            place(a_out, 4 + i, 2 + j, du[i][j])
            place(a_out, i, 2 + j, (uu[i][j] + du[i][j]) * 0.5)
            place(a_out, i, 4 + j, (ud[i][j] + dd[i][j]) * 0.5)
            place(a_out, 2 + i, j, (uu[i][j] + ud[i][j]) * 0.5)
            place(a_out, 4 + i, j, (du[i][j] + dd[i][j]) * 0.5)
    place(a_out, 6, 6, get(10))
    for i in range(6):
        block = get(11 + i)
        place(a_out, i, 6, block)
        place(a_out, 6, i, block.T)


def natural_kernel(kept, from_0, from_1, a_inverse, s_inverse, natural, curvature):
    get = reader(kept, (from_0, from_1), BACK_STREAMS[:2])

    grad = jnp.concatenate(
        [jnp.concatenate([get(19 + 2 * i), get(20 + 2 * i)], 1) for i in range(7)], 0
    )
    g_high, g_low = split(grad)
    s_high, s_low = split(s_inverse[...])
    half = dot(g_high, s_high) + (dot(g_high, s_low) + dot(g_low, s_high))
    h_high, h_low = split(half)
    total = jnp.zeros((1, D), F32)
    for i in range(7):
        rows = slice(i * B, (i + 1) * B)
        a_high, a_low = split(a_inverse[rows, :])
        part = dot(a_high, h_high) + (dot(a_high, h_low) + dot(a_low, h_high))
        natural[rows, :] = part
        total = total + jnp.sum(part * grad[rows, :], axis=0, keepdims=True)
    curvature[...] = jnp.broadcast_to(jnp.sum(total, axis=1, keepdims=True), (1, B))


def scale_kernel(natural, curvature, other, direction):
    total = curvature[:, :1] + other[:, :1]
    direction[...] = natural[...] * lax.rsqrt(total * (1.0 / ENTRIES))


def call(kernel, out_shapes, in_spaces, limit_mib, name, scratch=(), flops=0, moved=0):
    return pl.pallas_call(
        kernel,
        out_shape=tuple(jax.ShapeDtypeStruct(shape, dtype) for shape, dtype in out_shapes),
        in_specs=[pl.BlockSpec(memory_space=space) for space in in_spaces],
        out_specs=tuple(pl.BlockSpec(memory_space=pltpu.VMEM) for _ in out_shapes),
        scratch_shapes=scratch,
        compiler_params=pltpu.CompilerParams(vmem_limit_bytes=limit_mib * 1024 * 1024),
        cost_estimate=pl.CostEstimate(flops=flops, bytes_accessed=moved, transcendentals=0),
        name=name,
    )


V, S = pltpu.VMEM, pltpu.SMEM


def parity_groups():
    groups = {}
    for place in range(256):
        rest, c = divmod(place, 2)
        rest, x = divmod(rest, 4)
        rest, zh = divmod(rest, 4)
        zl, y = divmod(rest, 4)
        groups.setdefault((zh, c, (x + y + zl) % 2), []).append(place)
    return [groups[key] for key in sorted(groups)]


def same_parity(value):
    axes = ("zl", "y", "zh", "x", "c")
    return lax.all_to_all(value, axes, 0, 0, axis_index_groups=parity_groups(), tiled=True)


LOW, HIGH = [(0, 1), (1, 0), (2, 3), (3, 2)], [(1, 2), (2, 1), (3, 0), (0, 3)]


def to_neighbours(parts):
    ways = (("x", LOW), ("y", LOW), ("zl", [(0, 1), (1, 0)]), ("x", HIGH), ("y", HIGH))
    return [lax.ppermute(part, axis, pairs) for part, (axis, pairs) in zip(parts, ways)]


def streams_of(streams):
    return [(((end - first) * B, B), F32) for first, end in streams]


def body(features, psi_grad, pair_means, energies, multiplicity, weights, a_inverse, s_inverse):
    feat = features.reshape(HALF, D)
    psi = psi_grad.reshape(HALF, D)
    pair = pair_means.reshape(2, HALF, PAIR)
    swap = [(0, 1), (1, 0)]

    two = [(0, 2), (1, 3), (2, 0), (3, 1)]
    sum_2 = energies + lax.ppermute(energies, "x", two)
    other = lax.ppermute(jnp.concatenate([feat, psi], 1).astype(F32), "c", swap)
    oth_pair = lax.ppermute(pair.astype(F32), "c", swap)
    far_2 = lax.ppermute(sum_2, "zh", LOW)

    grads = GRADS * B
    keep, keep_0, to_a, to_0, to_2, to_3 = call(
        factors_kernel,
        [((KEPT, B), F32), ((grads, B), F32)]
        + [((grads, B), F32)] * 2
        + streams_of(OUT_STREAMS),
        [V] * 7 + [S] * 2,
        26,
        "factors",
        scratch=[
            pltpu.VMEM((2, ROWS, D + PAIR), BF16),
            pltpu.VMEM((2, ROWS, D), F32),
            pltpu.VMEM((2, 2 * WALK, D), BF16),
            pltpu.VMEM((2, ROWS, D), BF16),
            pltpu.VMEM((2, ROWS, D), BF16),
            pltpu.VMEM((2, KEPT, B), F32),
            pltpu.VMEM((2, grads, B), F32),
        ],
        flops=2_500_000_000,
        moved=8_000_000,
    )(feat, pair, psi, other, oth_pair, weights, energies, energies, multiplicity)

    to_a, sum_4 = pl.pallas_call(
        tie_kernel,
        out_shape=(jax.ShapeDtypeStruct((grads, B), F32), jax.ShapeDtypeStruct((1, WALK), F32)),
        in_specs=[pl.BlockSpec(memory_space=pl.ANY)] + [pl.BlockSpec(memory_space=V)] * 2,
        out_specs=(pl.BlockSpec(memory_space=pl.ANY), pl.BlockSpec(memory_space=V)),
        input_output_aliases={0: 0},
        name="tie",
    )(to_a, sum_2, far_2)
    from_a = lax.ppermute(to_a, "x", LOW)
    from_0 = lax.ppermute(to_0, "x", HIGH)
    from_2 = lax.ppermute(to_2, "y", LOW)
    from_3 = lax.ppermute(to_3, "zl", swap)
    sum_8 = sum_4 + lax.ppermute(sum_4, "zh", HIGH)
    far_8 = lax.ppermute(sum_8, "x", LOW)
    (total,) = call(add_kernel, [((KEPT, B), F32)], [V] * 8, 8, "add", moved=3_000_000)(
        keep, keep_0, from_a, from_0, from_2, from_3, sum_8, far_8
    )
    mine = jnp.sum(same_parity(total).reshape(GROUP, CHUNK, B), axis=0)
    one, two, three = (
        lax.ppermute(mine, "zh", [(i, (i + k) % 4) for i in range(4)]) for k in (1, 2, 3)
    )
    mine = (mine + two) + (one + three)
    kept = same_parity(jnp.broadcast_to(mine[None], (GROUP, CHUNK, B)).reshape(KEPT, B))
    parts = call(cut_kernel, streams_of(BACK_STREAMS), [V], 6, "cut", moved=2_200_000)(kept)
    parts = to_neighbours(parts)

    natural, curvature = call(
        natural_kernel,
        [((DIN, D), F32), ((1, B), F32)],
        [V] * 5,
        18,
        "natural",
        flops=1_500_000_000,
        moved=5_000_000,
    )(kept, *parts[:2], a_inverse[0], s_inverse[0])
    other = lax.ppermute(curvature, "c", swap)
    a_sum, s_sum = call(
        unpack_kernel,
        [((DIN, DIN), F32), ((D, D), F32)],
        [V] * 4,
        14,
        "unpack",
        flops=10_000_000,
        moved=6_000_000,
    )(kept, *parts[2:])
    (direction,) = call(
        scale_kernel, [((DIN, D), F32)], [V] * 3, 6, "scale", flops=1_000_000, moved=2_000_000
    )(natural, curvature, other)
    return a_sum[None], s_sum[None], direction[None]


def solution(mesh):
    fine = Mesh(mesh.devices.reshape(2, 4, 4, 4, 2), ("zl", "y", "zh", "x", "c"))
    twist, walker = ("zl", "y"), ("zh", "x")
    return jax.shard_map(
        body,
        mesh=fine,
        in_specs=(
            P(twist, walker, "c", None),
            P(twist, walker, "c", None),
            P(twist, None, walker, "c", None),
            P(twist, walker),
            P(twist),
            P(),
            P("c", None, None),
            P("c", None, None),
        ),
        out_specs=(P("c", None, None),) * 3,
        check_vma=False,
    )
```

```python
import jax
import jax.numpy as jnp
from jax import lax
from jax.experimental import pallas as pl
from jax.experimental.pallas import tpu as pltpu
from jax.sharding import Mesh, PartitionSpec as P

F32, BF16 = jnp.float32, jnp.bfloat16
D, PAIR, DIN = 256, 128, 896
WALK, HALF, ROWS = 16, 512, 1024
B = 128
GROUP = 16
SLOTS = 17
KEPT = SLOTS * B
CHUNK = KEPT // GROUP
GRADS, FACTORS = 7, 10
OUT_STREAMS = ((7, 12), (12, 17))
BACK_STREAMS = ((0, 4), (4, 7), (7, 11), (11, 14), (14, 17))
ENTRIES = 2 * DIN * D
SHIFT = 7.0


def dot_t(a, b):
    return lax.dot_general(a, b, (((0,), (0,)), ((), ())), preferred_element_type=F32)


def dot_nt(a, b):
    return lax.dot_general(a, b, (((1,), (1,)), ((), ())), preferred_element_type=F32)


def dot(a, b):
    return jnp.dot(a, b, preferred_element_type=F32)


def split(a):
    high = a.astype(BF16)
    return high, (a - high.astype(F32)).astype(BF16)


def per_walker(a):
    n = a.shape[1]
    return jnp.broadcast_to(a[:, None, :], (WALK, HALF // WALK, n)).reshape(HALF, n)


def square_iotas():
    return lax.broadcasted_iota(jnp.int32, (B, B), 0), lax.broadcasted_iota(jnp.int32, (B, B), 1)


def own_parity():
    return lax.rem(lax.axis_index("x") + lax.axis_index("y") + lax.axis_index("zl"), 2)


def walker_table():
    group = lax.broadcasted_iota(jnp.int32, (2 * WALK, ROWS), 1) // (HALF // WALK)
    return (group == lax.broadcasted_iota(jnp.int32, (2 * WALK, ROWS), 0)).astype(BF16)


def place_of(slot):
    if 19 <= slot < 33:
        half, place = divmod(slot - 19, GRADS)
        return half, place
    half, place = divmod(slot if slot < 19 else 19, FACTORS)
    return half, place + GRADS


def factors_kernel(
    feat, pair, psi, other, oth_pair, weights, energies, energy, multiplicity,
    keep, keep_0, to_a, to_0, to_2, to_3, x_s, d_s, m_s, s_s, w_s, out, out_0
):
    mp = lax.axis_index("c")
    own_row = pl.multiple_of(D + D * mp, D)
    oth_row = pl.multiple_of(2 * D - D * mp, D)
    x_s[0, :HALF, :D] = feat[...]
    x_s[0, HALF:, :D] = other[:, :D].astype(BF16)
    for l in range(2):
        x_s[l, :HALF, D:] = pair[l]
        x_s[l, HALF:, D:] = oth_pair[l].astype(BF16)
    pick = walker_table()
    for l in range(2):
        means = (dot(pick, x_s[l, :, :D]) * (1.0 / 32.0)).astype(BF16)
        m_s[l] = means
        z_walk = dot(means[:WALK], weights[l, pl.ds(own_row, D), :]) + dot(
            means[WALK:], weights[l, pl.ds(oth_row, D), :]
        )
        z_wide = per_walker(z_walk)
        for half in range(2):
            rows = slice(half * HALF, (half + 1) * HALF)
            z = dot(x_s[l, rows, :D], weights[l, :D, :]) + dot(
                x_s[l, rows, D:], weights[l, 3 * D :, :]
            )
            t = jnp.tanh(z + z_wide)
            d_s[l, rows, :] = 1.0 - t * t
            if l == 0:
                x_s[1, rows, :D] = (x_s[0, rows, :D].astype(F32) + t).astype(BF16)

    s_s[1, :HALF, :] = (psi[...].astype(F32) * d_s[1, :HALF, :]).astype(BF16)
    s_s[1, HALF:, :] = (other[:, D : 2 * D] * d_s[1, HALF:, :]).astype(BF16)
    q_both = dot(pick, s_s[1])
    q_high, q_low = split(q_both[:WALK] + q_both[WALK:])
    for half in range(2):
        rows = slice(half * HALF, (half + 1) * HALF)
        w_spin = weights[1, pl.ds(own_row if half == 0 else oth_row, D), :]
        spin = (dot_nt(q_high, w_spin) + dot_nt(q_low, w_spin)) * (1.0 / 32.0)
        up = psi[...].astype(F32) if half == 0 else other[:, D : 2 * D]
        u = up + dot_nt(s_s[1, rows, :], weights[1, :D, :]) + per_walker(spin)
        s_s[0, rows, :] = (u * d_s[0, rows, :]).astype(BF16)

    l = mp
    mult = multiplicity[0].astype(F32)
    row_scale = mult * (1.0 / 16384.0)
    mean = jnp.sum(energies[...], axis=1, keepdims=True) * (1.0 / WALK)
    shifted = mean + SHIFT
    at_p, at_c, at_low, at_s = D, D + PAIR, 2 * D + PAIR, 3 * D + PAIR
    w_s[:, :at_c] = x_s[l]
    w_s[:, at_s:] = s_s[l]
    step = HALF // WALK
    for w in range(WALK):
        centered = energy[0, w] - mean
        for first in (w * step, HALF + w * step):
            rows = slice(first, first + step)
            high, low = split(centered * w_s[rows, at_s:].astype(F32))
            w_s[rows, at_c:at_low] = high
            w_s[rows, at_low:at_s] = low
    with_h = dot_t(w_s[:, :D], w_s[...])
    with_p = dot_t(w_s[:, at_p:at_c], w_s[:, at_p:])
    with_s = dot_t(w_s[:, at_s:], w_s[:, at_s:])
    totals = dot(pick, w_s[:, at_p:])
    totals = totals[:WALK] + totals[WALK:]
    row, col = square_iotas()

    parity = own_parity()

    def put(slot, value):
        half, place = place_of(slot)
        out[parity ^ half, place * B : (place + 1) * B, :] = value * row_scale

    def put_grad(slot, centered, plain):
        half, place = place_of(slot)
        rows = slice(place * B, (place + 1) * B)
        out[parity ^ half, rows, :] = (centered + shifted * plain) * row_scale
        out_0[parity ^ half, rows, :] = plain * row_scale

    lines = {}

    def put_symmetric(slot, line, full):
        low = full[B:, B:]
        put(slot, jnp.where(col >= row, full[:B, :B], low))
        put(slot + 1, full[:B, B:])
        lines[line] = jnp.sum(jnp.where(col == row, low, 0.0), axis=0, keepdims=True) * row_scale

    put_symmetric(0, 0, with_h[:, :D])
    hp = with_h[:, at_p:at_c]
    put(11, hp[:B])
    put(12, hp[B:])
    put(10, with_p[:, :PAIR])
    hc, hs = with_h[:, at_c:at_low] + with_h[:, at_low:at_s], with_h[:, at_s:]
    pc = with_p[:, PAIR : PAIR + D] + with_p[:, PAIR + D : PAIR + 2 * D]
    ps = with_p[:, PAIR + 2 * D :]
    for j in range(2):
        cols = slice(j * B, (j + 1) * B)
        put_grad(19 + j, hc[:B, cols], hs[:B, cols])
        put_grad(21 + j, hc[B:, cols], hs[B:, cols])
        put_grad(31 + j, pc[:, cols], ps[:, cols])
    put_symmetric(17, 3, with_s)

    means = m_s[l]
    up_first = mp == 0
    up = jnp.where(up_first, means[:WALK].astype(F32), means[WALK:].astype(F32)).astype(BF16)
    down = jnp.where(up_first, means[WALK:].astype(F32), means[:WALK].astype(F32)).astype(BF16)
    both = jnp.concatenate([up, down], 1)
    mm = dot_t(both, both) * 64.0
    put_symmetric(2, 1, mm[:D, :D])
    put_symmetric(4, 2, mm[D:, D:])
    for i in range(2):
        for j in range(2):
            put(6 + 2 * i + j, mm[i * B : (i + 1) * B, D + j * B : D + (j + 1) * B])
    totals = jnp.concatenate(
        [totals[:, :PAIR], totals[:, PAIR : PAIR + D] + totals[:, PAIR + D : PAIR + 2 * D], totals[:, PAIR + 2 * D :]], 1
    )
    t_high, t_low = split(totals)
    side = dot_t(jnp.concatenate([both, both], 0), jnp.concatenate([t_high, t_low], 0))
    for i in range(4):
        rows = slice(i * B, (i + 1) * B)
        put(13 + i, side[rows, :B])
        for j in range(2):
            at = (1 + j) * B
            put_grad(23 + 2 * i + j, side[rows, at : at + B], side[rows, at + D : at + D + B])
    lines[4] = jnp.full((1, B), mult * (1.0 / 16.0), F32)
    last = KEPT - B
    out[parity ^ 1, last:, :] = jnp.zeros((B, B), F32)
    for line, value in lines.items():
        out[parity ^ 1, last + line : last + line + 1, :] = value
    keep[...] = out[0]
    keep_0[...] = out_0[0]
    grads = GRADS * B
    to_a[...] = out[1, :grads, :]
    to_0[...] = out_0[1]
    for target, (first, end) in zip((to_2, to_3), OUT_STREAMS):
        target[...] = out[1, first * B : end * B, :]


def tie_kernel(plain_a, plain_0, near, far, to_a, to_0, row_sum):
    zh_sum = jnp.sum(near[...] + far[...], axis=1, keepdims=True)
    row_sum[...] = jnp.broadcast_to(zh_sum, (8, B))
    grads = GRADS * B
    for source, target in ((plain_a, to_a), (plain_0, to_0)):
        target[:grads, :] = source[...]
        target[grads:, :] = row_sum[...]


def add_kernel(keep, keep_0, from_a, from_0, from_2, from_3, row_sum, row_two, total):
    grads = GRADS * B
    energy = (row_sum[...] + row_two[...]) + (from_a[grads:, :] + from_0[grads:, :])
    shifted = energy[:1, :] * (1.0 / 256.0) + SHIFT
    plain = keep_0[...] + from_0[:grads, :]
    total[:grads, :] = (keep[:grads, :] + from_a[:grads, :]) - shifted * plain
    for part, (first, end) in zip((from_2, from_3), OUT_STREAMS):
        rows = slice(first * B, end * B)
        total[rows, :] = keep[rows, :] + part[...]


def cut_kernel(kept, to_0, to_1, to_2, to_3, to_4):
    for target, (first, end) in zip((to_0, to_1, to_2, to_3, to_4), BACK_STREAMS):
        target[...] = kept[first * B : end * B, :]


def reader(kept, parts, streams):
    parity = own_parity()

    def read(slot, size=B):
        half, place = place_of(slot)
        for part, (begin, end) in zip(parts, streams):
            if begin <= place < end:
                other = part[(place - begin) * B : (place - begin) * B + size, :]
        own = kept[place * B : place * B + size, :]
        return jnp.where(parity == half, own, other)

    return read


def unpack_kernel(kept, from_2, from_3, from_4, a_out, s_out, a_v, s_v, sems):
    row, col = square_iotas()
    read = reader(kept, (from_2, from_3, from_4), BACK_STREAMS[2:])
    lines = read(33, 8)
    inverse = 1.0 / lines[4:5, :]
    copies = []

    def get(slot):
        return read(slot) * inverse

    def symmetric(slot, line):
        tri = get(slot)
        off = get(slot + 1)
        flipped = tri.T
        diag = lines[line : line + 1, :] * inverse
        first = jnp.where(col >= row, tri, flipped)
        second = jnp.where(col < row, tri, flipped)
        second = jnp.where(col == row, jnp.broadcast_to(diag, (B, B)), second)
        return [[first, off], [off.T, second]]

    def place(target, i, j, value):
        target[i * B : (i + 1) * B, j * B : (j + 1) * B] = value

    def send(source, target, first, end):
        rows = slice(first * B, end * B)
        copy = pltpu.make_async_copy(source.at[rows], target.at[rows], sems.at[len(copies)])
        copy.start()
        copies.append(copy)

    ss = symmetric(17, 3)
    for i in range(2):
        for j in range(2):
            place(s_v, i, j, ss[i][j])
    send(s_v, s_out, 0, 2)
    uu = symmetric(2, 1)
    dd = symmetric(4, 2)
    ud = [[get(6 + 2 * i + j) for j in range(2)] for i in range(2)]
    du = [[ud[j][i].T for j in range(2)] for i in range(2)]
    sides = [get(11 + i) for i in range(6)]
    for i in range(2):
        for j in range(2):
            place(a_v, 2 + i, j, (uu[i][j] + ud[i][j]) * 0.5)
            place(a_v, 2 + i, 2 + j, uu[i][j])
            place(a_v, 2 + i, 4 + j, ud[i][j])
        place(a_v, 2 + i, 6, sides[2 + i])
    send(a_v, a_out, 2, 4)
    for i in range(2):
        for j in range(2):
            place(a_v, 4 + i, j, (du[i][j] + dd[i][j]) * 0.5)
            place(a_v, 4 + i, 2 + j, du[i][j])
            place(a_v, 4 + i, 4 + j, dd[i][j])
        place(a_v, 4 + i, 6, sides[4 + i])
    send(a_v, a_out, 4, 6)
    hh = symmetric(0, 0)
    for i in range(2):
        for j in range(2):
            place(a_v, i, j, hh[i][j])
            place(a_v, i, 2 + j, (uu[i][j] + du[i][j]) * 0.5)
            place(a_v, i, 4 + j, (ud[i][j] + dd[i][j]) * 0.5)
        place(a_v, i, 6, sides[i])
    send(a_v, a_out, 0, 2)
    for i in range(6):
        place(a_v, 6, i, sides[i].T)
    place(a_v, 6, 6, get(10))
    send(a_v, a_out, 6, 7)
    for copy in copies:
        copy.wait()


def natural_kernel(kept, from_0, from_1, a_inverse, s_inverse, natural, curvature):
    get = reader(kept, (from_0, from_1), BACK_STREAMS[:2])

    grad = jnp.concatenate(
        [jnp.concatenate([get(19 + 2 * i), get(20 + 2 * i)], 1) for i in range(7)], 0
    )
    g_high, g_low = split(grad)
    s_high, s_low = split(s_inverse[...])
    half = dot(g_high, s_high) + (dot(g_high, s_low) + dot(g_low, s_high))
    h_high, h_low = split(half)
    total = jnp.zeros((1, D), F32)
    for i in range(7):
        rows = slice(i * B, (i + 1) * B)
        a_high, a_low = split(a_inverse[rows, :])
        part = dot(a_high, h_high) + (dot(a_high, h_low) + dot(a_low, h_high))
        natural[rows, :] = part
        total = total + jnp.sum(part * grad[rows, :], axis=0, keepdims=True)
    curvature[...] = jnp.broadcast_to(jnp.sum(total, axis=1, keepdims=True), (1, B))


def scale_kernel(natural, curvature, other, direction):
    total = curvature[:, :1] + other[:, :1]
    direction[...] = natural[...] * lax.rsqrt(total * (1.0 / ENTRIES))


def call(kernel, out_shapes, in_spaces, limit_mib, name, scratch=(), flops=0, moved=0, out_space=pltpu.VMEM):
    return pl.pallas_call(
        kernel,
        out_shape=tuple(jax.ShapeDtypeStruct(shape, dtype) for shape, dtype in out_shapes),
        in_specs=[pl.BlockSpec(memory_space=space) for space in in_spaces],
        out_specs=tuple(pl.BlockSpec(memory_space=out_space) for _ in out_shapes),
        scratch_shapes=scratch,
        compiler_params=pltpu.CompilerParams(vmem_limit_bytes=limit_mib * 1024 * 1024),
        cost_estimate=pl.CostEstimate(flops=flops, bytes_accessed=moved, transcendentals=0),
        name=name,
    )


V, S = pltpu.VMEM, pltpu.SMEM


def parity_groups():
    groups = {}
    for place in range(256):
        rest, c = divmod(place, 2)
        rest, x = divmod(rest, 4)
        rest, zh = divmod(rest, 4)
        zl, y = divmod(rest, 4)
        groups.setdefault((zh, c, (x + y + zl) % 2), []).append(place)
    return [groups[key] for key in sorted(groups)]


def same_parity(value):
    axes = ("zl", "y", "zh", "x", "c")
    return lax.all_to_all(value, axes, 0, 0, axis_index_groups=parity_groups(), tiled=True)


LOW, HIGH = [(0, 1), (1, 0), (2, 3), (3, 2)], [(1, 2), (2, 1), (3, 0), (0, 3)]


def to_neighbours(parts):
    ways = (("x", LOW), ("y", LOW), ("zl", [(0, 1), (1, 0)]), ("x", HIGH), ("y", HIGH))
    return [lax.ppermute(part, axis, pairs) for part, (axis, pairs) in zip(parts, ways)]


def streams_of(streams):
    return [(((end - first) * B, B), F32) for first, end in streams]


def body(features, psi_grad, pair_means, energies, multiplicity, weights, a_inverse, s_inverse):
    feat = features.reshape(HALF, D)
    psi = psi_grad.reshape(HALF, D)
    pair = pair_means.reshape(2, HALF, PAIR)
    swap = [(0, 1), (1, 0)]

    sum_2 = energies + lax.ppermute(energies, "zh", LOW)
    other = lax.ppermute(jnp.concatenate([feat, psi], 1).astype(F32), "c", swap)
    oth_pair = lax.ppermute(pair.astype(F32), "c", swap)
    far_2 = lax.ppermute(sum_2, "zh", HIGH)

    grads = GRADS * B
    keep, keep_0, to_a, to_0, to_2, to_3 = call(
        factors_kernel,
        [((KEPT, B), F32), ((grads, B), F32)]
        + [((grads, B), F32)] * 2
        + streams_of(OUT_STREAMS),
        [V] * 7 + [S] * 2,
        26,
        "factors",
        scratch=[
            pltpu.VMEM((2, ROWS, D + PAIR), BF16),
            pltpu.VMEM((2, ROWS, D), F32),
            pltpu.VMEM((2, 2 * WALK, D), BF16),
            pltpu.VMEM((2, ROWS, D), BF16),
            pltpu.VMEM((ROWS, 4 * D + PAIR), BF16),
            pltpu.VMEM((2, KEPT, B), F32),
            pltpu.VMEM((2, grads, B), F32),
        ],
        flops=2_500_000_000,
        moved=8_000_000,
    )(feat, pair, psi, other, oth_pair, weights, energies, energies, multiplicity)

    to_a, to_0, row_sum = call(
        tie_kernel, [((grads + 8, B), F32)] * 2 + [((8, B), F32)], [V] * 4, 6, "tie", moved=2_000_000
    )(to_a, to_0, sum_2, far_2)
    from_a = lax.ppermute(to_a, "x", LOW)
    from_0 = lax.ppermute(to_0, "x", HIGH)
    from_2 = lax.ppermute(to_2, "y", LOW)
    from_3 = lax.ppermute(to_3, "zl", swap)
    row_two = lax.ppermute(row_sum, "x", [(0, 2), (1, 3), (2, 0), (3, 1)])
    (total,) = call(add_kernel, [((KEPT, B), F32)], [V] * 8, 8, "add", moved=3_000_000)(
        keep, keep_0, from_a, from_0, from_2, from_3, row_sum, row_two
    )
    mine = jnp.sum(same_parity(total).reshape(GROUP, CHUNK, B), axis=0)
    one, two, three = (
        lax.ppermute(mine, "zh", [(i, (i + k) % 4) for i in range(4)]) for k in (1, 2, 3)
    )
    mine = (mine + two) + (one + three)
    kept = same_parity(jnp.broadcast_to(mine[None], (GROUP, CHUNK, B)).reshape(KEPT, B))
    parts = call(cut_kernel, streams_of(BACK_STREAMS), [V], 6, "cut", moved=2_200_000)(kept)
    parts = to_neighbours(parts)

    natural, curvature = call(
        natural_kernel,
        [((DIN, D), F32), ((1, B), F32)],
        [V] * 5,
        18,
        "natural",
        flops=1_500_000_000,
        moved=5_000_000,
    )(kept, *parts[:2], a_inverse[0], s_inverse[0])
    other = lax.ppermute(curvature, "c", swap)
    a_sum, s_sum = call(
        unpack_kernel,
        [((DIN, DIN), F32), ((D, D), F32)],
        [V] * 4,
        14,
        "unpack",
        scratch=[pltpu.VMEM((DIN, DIN), F32), pltpu.VMEM((D, D), F32), pltpu.SemaphoreType.DMA((5,))],
        out_space=pl.ANY,
        flops=10_000_000,
        moved=6_000_000,
    )(kept, *parts[2:])
    (direction,) = call(
        scale_kernel, [((DIN, D), F32)], [V] * 3, 6, "scale", flops=1_000_000, moved=2_000_000
    )(natural, curvature, other)
    return a_sum[None], s_sum[None], direction[None]


def solution(mesh):
    fine = Mesh(mesh.devices.reshape(2, 4, 4, 4, 2), ("zl", "y", "zh", "x", "c"))
    twist, walker = ("zl", "y"), ("zh", "x")
    return jax.shard_map(
        body,
        mesh=fine,
        in_specs=(
            P(twist, walker, "c", None),
            P(twist, walker, "c", None),
            P(twist, None, walker, "c", None),
            P(twist, walker),
            P(twist),
            P(),
            P("c", None, None),
            P("c", None, None),
        ),
        out_specs=(P("c", None, None),) * 3,
        check_vma=False,
    )
```

```python
import jax
import jax.numpy as jnp
from jax import lax
from jax.experimental import pallas as pl
from jax.experimental.pallas import tpu as pltpu
from jax.sharding import Mesh, PartitionSpec as P

F32, BF16 = jnp.float32, jnp.bfloat16
D, PAIR, DIN = 256, 128, 896
WALK, HALF, ROWS = 16, 512, 1024
B = 128
GROUP = 16
SLOTS = 17
KEPT = SLOTS * B
CHUNK = KEPT // GROUP
GRADS, FACTORS = 7, 10
OUT_STREAMS = ((0, 6), (6, 12), (12, 17))
BACK_STREAMS = ((0, 4), (4, 7), (7, 12), (12, 15), (15, 17))
ENTRIES = 2 * DIN * D
SHIFT = 7.0


def dot_t(a, b):
    return lax.dot_general(a, b, (((0,), (0,)), ((), ())), preferred_element_type=F32)


def dot_nt(a, b):
    return lax.dot_general(a, b, (((1,), (1,)), ((), ())), preferred_element_type=F32)


def dot(a, b):
    return jnp.dot(a, b, preferred_element_type=F32)


def split(a):
    high = a.astype(BF16)
    return high, (a - high.astype(F32)).astype(BF16)


def per_walker(a):
    n = a.shape[1]
    return jnp.broadcast_to(a[:, None, :], (WALK, HALF // WALK, n)).reshape(HALF, n)


def square_iotas():
    return lax.broadcasted_iota(jnp.int32, (B, B), 0), lax.broadcasted_iota(jnp.int32, (B, B), 1)


def own_parity():
    return lax.rem(lax.axis_index("x") + lax.axis_index("y") + lax.axis_index("zl"), 2)


def walker_table():
    group = lax.broadcasted_iota(jnp.int32, (2 * WALK, ROWS), 1) // (HALF // WALK)
    return (group == lax.broadcasted_iota(jnp.int32, (2 * WALK, ROWS), 0)).astype(BF16)


def place_of(slot):
    if 19 <= slot < 33:
        half, place = divmod(slot - 19, GRADS)
        return half, place
    half, place = divmod(slot if slot < 19 else 19, FACTORS)
    return half, place + GRADS


def factors_kernel(
    feat, pair, psi, other, oth_pair, weights, energies, energy, multiplicity,
    out, out_0, x_s, d_s, m_s, s_s, w_s
):
    mp = lax.axis_index("c")
    own_row = pl.multiple_of(D + D * mp, D)
    oth_row = pl.multiple_of(2 * D - D * mp, D)
    x_s[0, :HALF, :D] = feat[...]
    x_s[0, HALF:, :D] = other[:, :D].astype(BF16)
    for l in range(2):
        x_s[l, :HALF, D:] = pair[l]
        x_s[l, HALF:, D:] = oth_pair[l].astype(BF16)
    pick = walker_table()
    for l in range(2):
        means = (dot(pick, x_s[l, :, :D]) * (1.0 / 32.0)).astype(BF16)
        m_s[l] = means
        z_walk = dot(means[:WALK], weights[l, pl.ds(own_row, D), :]) + dot(
            means[WALK:], weights[l, pl.ds(oth_row, D), :]
        )
        z_wide = per_walker(z_walk)
        for half in range(2):
            rows = slice(half * HALF, (half + 1) * HALF)
            z = dot(x_s[l, rows, :D], weights[l, :D, :]) + dot(
                x_s[l, rows, D:], weights[l, 3 * D :, :]
            )
            t = jnp.tanh(z + z_wide)
            d_s[l, rows, :] = 1.0 - t * t
            if l == 0:
                x_s[1, rows, :D] = (x_s[0, rows, :D].astype(F32) + t).astype(BF16)

    s_s[1, :HALF, :] = (psi[...].astype(F32) * d_s[1, :HALF, :]).astype(BF16)
    s_s[1, HALF:, :] = (other[:, D : 2 * D] * d_s[1, HALF:, :]).astype(BF16)
    q_both = dot(pick, s_s[1])
    q_high, q_low = split(q_both[:WALK] + q_both[WALK:])
    for half in range(2):
        rows = slice(half * HALF, (half + 1) * HALF)
        w_spin = weights[1, pl.ds(own_row if half == 0 else oth_row, D), :]
        spin = (dot_nt(q_high, w_spin) + dot_nt(q_low, w_spin)) * (1.0 / 32.0)
        up = psi[...].astype(F32) if half == 0 else other[:, D : 2 * D]
        u = up + dot_nt(s_s[1, rows, :], weights[1, :D, :]) + per_walker(spin)
        s_s[0, rows, :] = (u * d_s[0, rows, :]).astype(BF16)

    l = mp
    mult = multiplicity[0].astype(F32)
    row_scale = mult * (1.0 / 16384.0)
    mean = jnp.sum(energies[...], axis=1, keepdims=True) * (1.0 / WALK)
    shifted = mean + SHIFT
    at_p, at_c, at_low, at_s = D, D + PAIR, 2 * D + PAIR, 3 * D + PAIR
    w_s[:, :at_c] = x_s[l]
    w_s[:, at_s:] = s_s[l]
    step = HALF // WALK
    for w in range(WALK):
        centered = energy[0, w] - mean
        for first in (w * step, HALF + w * step):
            rows = slice(first, first + step)
            high, low = split(centered * w_s[rows, at_s:].astype(F32))
            w_s[rows, at_c:at_low] = high
            w_s[rows, at_low:at_s] = low
    with_h = dot_t(w_s[:, :D], w_s[...])
    with_p = dot_t(w_s[:, at_p:at_c], w_s[:, at_p:])
    with_s = dot_t(w_s[:, at_s:], w_s[:, at_s:])
    totals = dot(pick, w_s[:, at_p:])
    totals = totals[:WALK] + totals[WALK:]
    row, col = square_iotas()

    parity = own_parity()

    def put(slot, value):
        half, place = place_of(slot)
        out[parity ^ half, place * B : (place + 1) * B, :] = value * row_scale

    def put_grad(slot, centered, plain):
        half, place = place_of(slot)
        rows = slice(place * B, (place + 1) * B)
        out[parity ^ half, rows, :] = (centered + shifted * plain) * row_scale
        out_0[parity ^ half, rows, :] = plain * row_scale

    lines = {}

    def put_symmetric(slot, line, full):
        low = full[B:, B:]
        put(slot, jnp.where(col >= row, full[:B, :B], low))
        put(slot + 1, full[:B, B:])
        lines[line] = jnp.sum(jnp.where(col == row, low, 0.0), axis=0, keepdims=True) * row_scale

    put_symmetric(0, 0, with_h[:, :D])
    hp = with_h[:, at_p:at_c]
    put(11, hp[:B])
    put(12, hp[B:])
    put(10, with_p[:, :PAIR])
    hc, hs = with_h[:, at_c:at_low] + with_h[:, at_low:at_s], with_h[:, at_s:]
    pc = with_p[:, PAIR : PAIR + D] + with_p[:, PAIR + D : PAIR + 2 * D]
    ps = with_p[:, PAIR + 2 * D :]
    for j in range(2):
        cols = slice(j * B, (j + 1) * B)
        put_grad(19 + j, hc[:B, cols], hs[:B, cols])
        put_grad(21 + j, hc[B:, cols], hs[B:, cols])
        put_grad(31 + j, pc[:, cols], ps[:, cols])
    put_symmetric(17, 3, with_s)

    means = m_s[l]
    up_first = mp == 0
    up = jnp.where(up_first, means[:WALK].astype(F32), means[WALK:].astype(F32)).astype(BF16)
    down = jnp.where(up_first, means[WALK:].astype(F32), means[:WALK].astype(F32)).astype(BF16)
    both = jnp.concatenate([up, down], 1)
    mm = dot_t(both, both) * 64.0
    put_symmetric(2, 1, mm[:D, :D])
    put_symmetric(4, 2, mm[D:, D:])
    for i in range(2):
        for j in range(2):
            put(6 + 2 * i + j, mm[i * B : (i + 1) * B, D + j * B : D + (j + 1) * B])
    totals = jnp.concatenate(
        [totals[:, :PAIR], totals[:, PAIR : PAIR + D] + totals[:, PAIR + D : PAIR + 2 * D], totals[:, PAIR + 2 * D :]], 1
    )
    t_high, t_low = split(totals)
    side = dot_t(jnp.concatenate([both, both], 0), jnp.concatenate([t_high, t_low], 0))
    for i in range(4):
        rows = slice(i * B, (i + 1) * B)
        put(13 + i, side[rows, :B])
        for j in range(2):
            at = (1 + j) * B
            put_grad(23 + 2 * i + j, side[rows, at : at + B], side[rows, at + D : at + D + B])
    lines[4] = jnp.full((1, B), mult * (1.0 / 16.0), F32)
    last = KEPT - B
    out[parity ^ 1, last:, :] = jnp.zeros((B, B), F32)
    for line, value in lines.items():
        out[parity ^ 1, last + line : last + line + 1, :] = value


def tie_kernel(out, out_0, near, far, to_0, to_1, to_2, to_3, row_sum):
    zh_sum = jnp.sum(near[...] + far[...], axis=1, keepdims=True)
    row_sum[...] = jnp.broadcast_to(zh_sum, (8, B))
    grads = GRADS * B
    to_0[:grads, :] = out_0[1]
    to_0[grads:, :] = row_sum[...]
    for target, (first, end) in zip((to_1, to_2, to_3), OUT_STREAMS):
        target[: (end - first) * B, :] = out[1, first * B : end * B, :]
    to_1[OUT_STREAMS[0][1] * B :, :] = row_sum[...]


def add_kernel(out, out_0, from_0, from_1, from_2, from_3, row_sum, row_two, total):
    grads = GRADS * B
    near, far = from_0[grads:, :], from_1[OUT_STREAMS[0][1] * B :, :]
    energy = (row_sum[...] + row_two[...]) + (near + far)
    shifted = energy[:1, :] * (1.0 / 256.0) + SHIFT
    for part, (first, end) in zip((from_1, from_2, from_3), OUT_STREAMS):
        for place in range(first, end):
            rows = slice(place * B, (place + 1) * B)
            value = out[0, rows, :] + part[(place - first) * B : (place - first + 1) * B, :]
            if place < GRADS:
                value = value - shifted * (out_0[0, rows, :] + from_0[rows, :])
            total[rows, :] = value


def cut_kernel(kept, to_0, to_1, to_2, to_3, to_4):
    for target, (first, end) in zip((to_0, to_1, to_2, to_3, to_4), BACK_STREAMS):
        target[...] = kept[first * B : end * B, :]


def reader(kept, parts, streams):
    parity = own_parity()

    def read(slot, size=B):
        half, place = place_of(slot)
        for part, (begin, end) in zip(parts, streams):
            if begin <= place < end:
                other = part[(place - begin) * B : (place - begin) * B + size, :]
        own = kept[place * B : place * B + size, :]
        return jnp.where(parity == half, own, other)

    return read


def unpack_kernel(kept, from_2, from_3, from_4, a_out, s_out, a_v, s_v, sems):
    row, col = square_iotas()
    read = reader(kept, (from_2, from_3, from_4), BACK_STREAMS[2:])
    lines = read(33, 8)
    inverse = 1.0 / lines[4:5, :]
    copies = []

    def get(slot):
        return read(slot) * inverse

    def symmetric(slot, line):
        tri = get(slot)
        off = get(slot + 1)
        flipped = tri.T
        diag = lines[line : line + 1, :] * inverse
        first = jnp.where(col >= row, tri, flipped)
        second = jnp.where(col < row, tri, flipped)
        second = jnp.where(col == row, jnp.broadcast_to(diag, (B, B)), second)
        return [[first, off], [off.T, second]]

    def place(target, i, j, value):
        target[i * B : (i + 1) * B, j * B : (j + 1) * B] = value

    def send(source, target, first, end):
        rows = slice(first * B, end * B)
        copy = pltpu.make_async_copy(source.at[rows], target.at[rows], sems.at[len(copies)])
        copy.start()
        copies.append(copy)

    ss = symmetric(17, 3)
    for i in range(2):
        for j in range(2):
            place(s_v, i, j, ss[i][j])
    send(s_v, s_out, 0, 2)
    uu = symmetric(2, 1)
    dd = symmetric(4, 2)
    ud = [[get(6 + 2 * i + j) for j in range(2)] for i in range(2)]
    du = [[ud[j][i].T for j in range(2)] for i in range(2)]
    sides = [get(11 + i) for i in range(6)]
    for i in range(2):
        for j in range(2):
            place(a_v, 2 + i, j, (uu[i][j] + ud[i][j]) * 0.5)
            place(a_v, 2 + i, 2 + j, uu[i][j])
            place(a_v, 2 + i, 4 + j, ud[i][j])
        place(a_v, 2 + i, 6, sides[2 + i])
    send(a_v, a_out, 2, 4)
    for i in range(2):
        for j in range(2):
            place(a_v, 4 + i, j, (du[i][j] + dd[i][j]) * 0.5)
            place(a_v, 4 + i, 2 + j, du[i][j])
            place(a_v, 4 + i, 4 + j, dd[i][j])
        place(a_v, 4 + i, 6, sides[4 + i])
    send(a_v, a_out, 4, 6)
    hh = symmetric(0, 0)
    for i in range(2):
        for j in range(2):
            place(a_v, i, j, hh[i][j])
            place(a_v, i, 2 + j, (uu[i][j] + du[i][j]) * 0.5)
            place(a_v, i, 4 + j, (ud[i][j] + dd[i][j]) * 0.5)
        place(a_v, i, 6, sides[i])
    send(a_v, a_out, 0, 2)
    for i in range(6):
        place(a_v, 6, i, sides[i].T)
    place(a_v, 6, 6, get(10))
    send(a_v, a_out, 6, 7)
    for copy in copies:
        copy.wait()


def natural_kernel(kept, from_0, from_1, a_inverse, s_inverse, natural, curvature):
    get = reader(kept, (from_0, from_1), BACK_STREAMS[:2])

    grad = jnp.concatenate(
        [jnp.concatenate([get(19 + 2 * i), get(20 + 2 * i)], 1) for i in range(7)], 0
    )
    g_high, g_low = split(grad)
    s_high, s_low = split(s_inverse[...])
    half = dot(g_high, s_high) + (dot(g_high, s_low) + dot(g_low, s_high))
    h_high, h_low = split(half)
    total = jnp.zeros((1, D), F32)
    for i in range(7):
        rows = slice(i * B, (i + 1) * B)
        a_high, a_low = split(a_inverse[rows, :])
        part = dot(a_high, h_high) + (dot(a_high, h_low) + dot(a_low, h_high))
        natural[rows, :] = part
        total = total + jnp.sum(part * grad[rows, :], axis=0, keepdims=True)
    curvature[...] = jnp.broadcast_to(jnp.sum(total, axis=1, keepdims=True), (1, B))


def scale_kernel(natural, curvature, other, direction):
    total = curvature[:, :1] + other[:, :1]
    direction[...] = natural[...] * lax.rsqrt(total * (1.0 / ENTRIES))


def call(kernel, out_shapes, in_spaces, limit_mib, name, scratch=(), flops=0, moved=0, out_space=pltpu.VMEM):
    return pl.pallas_call(
        kernel,
        out_shape=tuple(jax.ShapeDtypeStruct(shape, dtype) for shape, dtype in out_shapes),
        in_specs=[pl.BlockSpec(memory_space=space) for space in in_spaces],
        out_specs=tuple(pl.BlockSpec(memory_space=out_space) for _ in out_shapes),
        scratch_shapes=scratch,
        compiler_params=pltpu.CompilerParams(vmem_limit_bytes=limit_mib * 1024 * 1024),
        cost_estimate=pl.CostEstimate(flops=flops, bytes_accessed=moved, transcendentals=0),
        name=name,
    )


V, S = pltpu.VMEM, pltpu.SMEM


def parity_groups():
    groups = {}
    for place in range(256):
        rest, c = divmod(place, 2)
        rest, x = divmod(rest, 4)
        rest, zh = divmod(rest, 4)
        zl, y = divmod(rest, 4)
        groups.setdefault((zh, c, (x + y + zl) % 2), []).append(place)
    return [groups[key] for key in sorted(groups)]


def same_parity(value):
    axes = ("zl", "y", "zh", "x", "c")
    return lax.all_to_all(value, axes, 0, 0, axis_index_groups=parity_groups(), tiled=True)


LOW, HIGH = [(0, 1), (1, 0), (2, 3), (3, 2)], [(1, 2), (2, 1), (3, 0), (0, 3)]


def to_neighbours(parts):
    ways = (("x", LOW), ("y", LOW), ("zl", [(0, 1), (1, 0)]), ("x", HIGH), ("y", HIGH))
    return [lax.ppermute(part, axis, pairs) for part, (axis, pairs) in zip(parts, ways)]


def streams_of(streams):
    return [(((end - first) * B, B), F32) for first, end in streams]


def body(features, psi_grad, pair_means, energies, multiplicity, weights, a_inverse, s_inverse):
    feat = features.reshape(HALF, D)
    psi = psi_grad.reshape(HALF, D)
    pair = pair_means.reshape(2, HALF, PAIR)
    swap = [(0, 1), (1, 0)]

    sum_2 = energies + lax.ppermute(energies, "zh", LOW)
    other = lax.ppermute(jnp.concatenate([feat, psi], 1).astype(F32), "c", swap)
    oth_pair = lax.ppermute(pair.astype(F32), "c", swap)
    far_2 = lax.ppermute(sum_2, "zh", HIGH)

    grads = GRADS * B
    out, out_0 = call(
        factors_kernel,
        [((2, KEPT, B), F32), ((2, grads, B), F32)],
        [V] * 7 + [S] * 2,
        26,
        "factors",
        scratch=[
            pltpu.VMEM((2, ROWS, D + PAIR), BF16),
            pltpu.VMEM((2, ROWS, D), F32),
            pltpu.VMEM((2, 2 * WALK, D), BF16),
            pltpu.VMEM((2, ROWS, D), BF16),
            pltpu.VMEM((ROWS, 4 * D + PAIR), BF16),
        ],
        flops=2_500_000_000,
        moved=8_000_000,
    )(feat, pair, psi, other, oth_pair, weights, energies, energies, multiplicity)

    sizes = [((end - first) * B, B) for first, end in OUT_STREAMS]
    to_0, to_1, to_2, to_3, row_sum = call(
        tie_kernel,
        [((grads + 8, B), F32), ((sizes[0][0] + 8, B), F32), (sizes[1], F32), (sizes[2], F32), ((8, B), F32)],
        [V] * 4,
        8,
        "tie",
        moved=3_000_000,
    )(out, out_0, sum_2, far_2)
    from_0 = lax.ppermute(to_0, "x", LOW)
    from_1 = lax.ppermute(to_1, "x", HIGH)
    from_2 = lax.ppermute(to_2, "y", LOW)
    from_3 = lax.ppermute(to_3, "zl", swap)
    row_two = lax.ppermute(row_sum, "x", [(0, 2), (1, 3), (2, 0), (3, 1)])
    (total,) = call(add_kernel, [((KEPT, B), F32)], [V] * 8, 10, "add", moved=3_000_000)(
        out, out_0, from_0, from_1, from_2, from_3, row_sum, row_two
    )
    mine = jnp.sum(same_parity(total).reshape(GROUP, CHUNK, B), axis=0)
    one, two, three = (
        lax.ppermute(mine, "zh", [(i, (i + k) % 4) for i in range(4)]) for k in (1, 2, 3)
    )
    mine = (mine + two) + (one + three)
    kept = same_parity(jnp.broadcast_to(mine[None], (GROUP, CHUNK, B)).reshape(KEPT, B))
    parts = call(cut_kernel, streams_of(BACK_STREAMS), [V], 6, "cut", moved=2_200_000)(kept)
    parts = to_neighbours(parts)

    natural, curvature = call(
        natural_kernel,
        [((DIN, D), F32), ((1, B), F32)],
        [V] * 5,
        18,
        "natural",
        flops=1_500_000_000,
        moved=5_000_000,
    )(kept, *parts[:2], a_inverse[0], s_inverse[0])
    other = lax.ppermute(curvature, "c", swap)
    a_sum, s_sum = call(
        unpack_kernel,
        [((DIN, DIN), F32), ((D, D), F32)],
        [V] * 4,
        14,
        "unpack",
        scratch=[pltpu.VMEM((DIN, DIN), F32), pltpu.VMEM((D, D), F32), pltpu.SemaphoreType.DMA((5,))],
        out_space=pl.ANY,
        flops=10_000_000,
        moved=6_000_000,
    )(kept, *parts[2:])
    (direction,) = call(
        scale_kernel, [((DIN, D), F32)], [V] * 3, 6, "scale", flops=1_000_000, moved=2_000_000
    )(natural, curvature, other)
    return a_sum[None], s_sum[None], direction[None]


def solution(mesh):
    fine = Mesh(mesh.devices.reshape(2, 4, 4, 4, 2), ("zl", "y", "zh", "x", "c"))
    twist, walker = ("zl", "y"), ("zh", "x")
    return jax.shard_map(
        body,
        mesh=fine,
        in_specs=(
            P(twist, walker, "c", None),
            P(twist, walker, "c", None),
            P(twist, None, walker, "c", None),
            P(twist, walker),
            P(twist),
            P(),
            P("c", None, None),
            P("c", None, None),
        ),
        out_specs=(P("c", None, None),) * 3,
        check_vma=False,
    )
```

```python
import jax
import jax.numpy as jnp
from jax import lax
from jax.experimental import pallas as pl
from jax.experimental.pallas import tpu as pltpu
from jax.sharding import Mesh, PartitionSpec as P

F32, BF16 = jnp.float32, jnp.bfloat16
D, PAIR, DIN = 256, 128, 896
WALK, HALF, ROWS = 16, 512, 1024
B = 128
GROUP = 16
SLOTS = 17
KEPT = SLOTS * B
CHUNK = KEPT // GROUP
GRADS, FACTORS = 7, 10
OUT_STREAMS = ((0, 6), (6, 12), (12, 17))
BACK_STREAMS = ((0, 4), (4, 7), (7, 12), (12, 15), (15, 17))
ENTRIES = 2 * DIN * D
SHIFT = 7.0


def dot_t(a, b):
    return lax.dot_general(a, b, (((0,), (0,)), ((), ())), preferred_element_type=F32)


def dot_nt(a, b):
    return lax.dot_general(a, b, (((1,), (1,)), ((), ())), preferred_element_type=F32)


def dot(a, b):
    return jnp.dot(a, b, preferred_element_type=F32)


def split(a):
    high = a.astype(BF16)
    return high, (a - high.astype(F32)).astype(BF16)


def per_walker(a):
    n = a.shape[1]
    return jnp.broadcast_to(a[:, None, :], (WALK, HALF // WALK, n)).reshape(HALF, n)


def square_iotas():
    return lax.broadcasted_iota(jnp.int32, (B, B), 0), lax.broadcasted_iota(jnp.int32, (B, B), 1)


def own_parity():
    return lax.rem(lax.axis_index("x") + lax.axis_index("y") + lax.axis_index("zl"), 2)


def walker_table():
    group = lax.broadcasted_iota(jnp.int32, (2 * WALK, ROWS), 1) // (HALF // WALK)
    return (group == lax.broadcasted_iota(jnp.int32, (2 * WALK, ROWS), 0)).astype(BF16)


def place_of(slot):
    if 19 <= slot < 33:
        half, place = divmod(slot - 19, GRADS)
        return half, place
    half, place = divmod(slot if slot < 19 else 19, FACTORS)
    return half, place + GRADS


def factors_kernel(
    feat, pair, psi, other, oth_pair, weights, energies, energy, multiplicity,
    out, out_0, x_s, d_s, m_s, s_s, w_s
):
    mp = lax.axis_index("c")
    own_row = pl.multiple_of(D + D * mp, D)
    oth_row = pl.multiple_of(2 * D - D * mp, D)
    x_s[0, :HALF, :D] = feat[...]
    x_s[0, HALF:, :D] = other[:, :D].astype(BF16)
    for l in range(2):
        x_s[l, :HALF, D:] = pair[l]
        x_s[l, HALF:, D:] = oth_pair[l].astype(BF16)
    pick = walker_table()
    for l in range(2):
        means = (dot(pick, x_s[l, :, :D]) * (1.0 / 32.0)).astype(BF16)
        m_s[l] = means
        z_walk = dot(means[:WALK], weights[l, pl.ds(own_row, D), :]) + dot(
            means[WALK:], weights[l, pl.ds(oth_row, D), :]
        )
        z_wide = per_walker(z_walk)
        for half in range(2):
            rows = slice(half * HALF, (half + 1) * HALF)
            z = dot(x_s[l, rows, :D], weights[l, :D, :]) + dot(
                x_s[l, rows, D:], weights[l, 3 * D :, :]
            )
            t = jnp.tanh(z + z_wide)
            d_s[l, rows, :] = 1.0 - t * t
            if l == 0:
                x_s[1, rows, :D] = (x_s[0, rows, :D].astype(F32) + t).astype(BF16)

    s_s[1, :HALF, :] = (psi[...].astype(F32) * d_s[1, :HALF, :]).astype(BF16)
    s_s[1, HALF:, :] = (other[:, D : 2 * D] * d_s[1, HALF:, :]).astype(BF16)
    q_both = dot(pick, s_s[1])
    q_high, q_low = split(q_both[:WALK] + q_both[WALK:])
    for half in range(2):
        rows = slice(half * HALF, (half + 1) * HALF)
        w_spin = weights[1, pl.ds(own_row if half == 0 else oth_row, D), :]
        spin = (dot_nt(q_high, w_spin) + dot_nt(q_low, w_spin)) * (1.0 / 32.0)
        up = psi[...].astype(F32) if half == 0 else other[:, D : 2 * D]
        u = up + dot_nt(s_s[1, rows, :], weights[1, :D, :]) + per_walker(spin)
        s_s[0, rows, :] = (u * d_s[0, rows, :]).astype(BF16)

    l = mp
    mult = multiplicity[0].astype(F32)
    row_scale = mult * (1.0 / 16384.0)
    mean = jnp.sum(energies[...], axis=1, keepdims=True) * (1.0 / WALK)
    shifted = mean + SHIFT
    at_p, at_c, at_low, at_s = D, D + PAIR, 2 * D + PAIR, 3 * D + PAIR
    w_s[:, :at_c] = x_s[l]
    w_s[:, at_s:] = s_s[l]
    step = HALF // WALK
    for w in range(WALK):
        centered = energy[0, w] - mean
        for first in (w * step, HALF + w * step):
            rows = slice(first, first + step)
            high, low = split(centered * w_s[rows, at_s:].astype(F32))
            w_s[rows, at_c:at_low] = high
            w_s[rows, at_low:at_s] = low
    with_h = dot_t(w_s[:, :D], w_s[...])
    with_p = dot_t(w_s[:, at_p:at_c], w_s[:, at_p:])
    with_s = dot_t(w_s[:, at_s:], w_s[:, at_s:])
    totals = dot(pick, w_s[:, at_p:])
    totals = totals[:WALK] + totals[WALK:]
    row, col = square_iotas()

    parity = own_parity()

    def put(slot, value):
        half, place = place_of(slot)
        out[parity ^ half, place * B : (place + 1) * B, :] = value * row_scale

    def put_grad(slot, centered, plain):
        half, place = place_of(slot)
        rows = slice(place * B, (place + 1) * B)
        out[parity ^ half, rows, :] = (centered + shifted * plain) * row_scale
        out_0[parity ^ half, rows, :] = plain * row_scale

    lines = {}

    def put_symmetric(slot, line, full):
        low = full[B:, B:]
        put(slot, jnp.where(col >= row, full[:B, :B], low))
        put(slot + 1, full[:B, B:])
        lines[line] = jnp.sum(jnp.where(col == row, low, 0.0), axis=0, keepdims=True) * row_scale

    put_symmetric(0, 0, with_h[:, :D])
    hp = with_h[:, at_p:at_c]
    put(11, hp[:B])
    put(12, hp[B:])
    put(10, with_p[:, :PAIR])
    hc, hs = with_h[:, at_c:at_low] + with_h[:, at_low:at_s], with_h[:, at_s:]
    pc = with_p[:, PAIR : PAIR + D] + with_p[:, PAIR + D : PAIR + 2 * D]
    ps = with_p[:, PAIR + 2 * D :]
    for j in range(2):
        cols = slice(j * B, (j + 1) * B)
        put_grad(19 + j, hc[:B, cols], hs[:B, cols])
        put_grad(21 + j, hc[B:, cols], hs[B:, cols])
        put_grad(31 + j, pc[:, cols], ps[:, cols])
    put_symmetric(17, 3, with_s)

    means = m_s[l]
    up_first = mp == 0
    up = jnp.where(up_first, means[:WALK].astype(F32), means[WALK:].astype(F32)).astype(BF16)
    down = jnp.where(up_first, means[WALK:].astype(F32), means[:WALK].astype(F32)).astype(BF16)
    both = jnp.concatenate([up, down], 1)
    mm = dot_t(both, both) * 64.0
    put_symmetric(2, 1, mm[:D, :D])
    put_symmetric(4, 2, mm[D:, D:])
    for i in range(2):
        for j in range(2):
            put(6 + 2 * i + j, mm[i * B : (i + 1) * B, D + j * B : D + (j + 1) * B])
    totals = jnp.concatenate(
        [totals[:, :PAIR], totals[:, PAIR : PAIR + D] + totals[:, PAIR + D : PAIR + 2 * D], totals[:, PAIR + 2 * D :]], 1
    )
    t_high, t_low = split(totals)
    side = dot_t(jnp.concatenate([both, both], 0), jnp.concatenate([t_high, t_low], 0))
    for i in range(4):
        rows = slice(i * B, (i + 1) * B)
        put(13 + i, side[rows, :B])
        for j in range(2):
            at = (1 + j) * B
            put_grad(23 + 2 * i + j, side[rows, at : at + B], side[rows, at + D : at + D + B])
    lines[4] = jnp.full((1, B), mult * (1.0 / 16.0), F32)
    last = KEPT - B
    out[parity ^ 1, last:, :] = jnp.zeros((B, B), F32)
    for line, value in lines.items():
        out[parity ^ 1, last + line : last + line + 1, :] = value


def tie_kernel(out, out_0, near, far, to_0, to_1, to_2, to_3, sums):
    sums[...] = near[...] + far[...]
    to_0[...] = out_0[1]
    for target, (first, end) in zip((to_1, to_2, to_3), OUT_STREAMS):
        target[...] = out[1, first * B : end * B, :]


def add_kernel(out, out_0, from_0, from_1, from_2, from_3, sums, sums_1, total):
    known = jnp.where(lax.axis_index("c") == 0, sums_1[...], sums[...])
    shifted = jnp.sum(known, axis=1, keepdims=True) * (1.0 / 256.0) + SHIFT
    for part, (first, end) in zip((from_1, from_2, from_3), OUT_STREAMS):
        for place in range(first, end):
            rows = slice(place * B, (place + 1) * B)
            value = out[0, rows, :] + part[(place - first) * B : (place - first + 1) * B, :]
            if place < GRADS:
                value = value - shifted * (out_0[0, rows, :] + from_0[rows, :])
            total[rows, :] = value


def cut_kernel(kept, to_0, to_1, to_2, to_3, to_4):
    for target, (first, end) in zip((to_0, to_1, to_2, to_3, to_4), BACK_STREAMS):
        target[...] = kept[first * B : end * B, :]


def reader(kept, parts, streams):
    parity = own_parity()

    def read(slot, size=B):
        half, place = place_of(slot)
        for part, (begin, end) in zip(parts, streams):
            if begin <= place < end:
                other = part[(place - begin) * B : (place - begin) * B + size, :]
        own = kept[place * B : place * B + size, :]
        return jnp.where(parity == half, own, other)

    return read


def unpack_kernel(kept, from_2, from_3, from_4, a_out, s_out, a_v, s_v, sems):
    row, col = square_iotas()
    read = reader(kept, (from_2, from_3, from_4), BACK_STREAMS[2:])
    lines = read(33, 8)
    inverse = 1.0 / lines[4:5, :]
    copies = []

    def get(slot):
        return read(slot) * inverse

    def symmetric(slot, line):
        tri = get(slot)
        off = get(slot + 1)
        flipped = tri.T
        diag = lines[line : line + 1, :] * inverse
        first = jnp.where(col >= row, tri, flipped)
        second = jnp.where(col < row, tri, flipped)
        second = jnp.where(col == row, jnp.broadcast_to(diag, (B, B)), second)
        return [[first, off], [off.T, second]]

    def place(target, i, j, value):
        target[i * B : (i + 1) * B, j * B : (j + 1) * B] = value

    def send(source, target, first, end):
        rows = slice(first * B, end * B)
        copy = pltpu.make_async_copy(source.at[rows], target.at[rows], sems.at[len(copies)])
        copy.start()
        copies.append(copy)

    ss = symmetric(17, 3)
    for i in range(2):
        for j in range(2):
            place(s_v, i, j, ss[i][j])
    send(s_v, s_out, 0, 2)
    uu = symmetric(2, 1)
    dd = symmetric(4, 2)
    ud = [[get(6 + 2 * i + j) for j in range(2)] for i in range(2)]
    du = [[ud[j][i].T for j in range(2)] for i in range(2)]
    sides = [get(11 + i) for i in range(6)]
    for i in range(2):
        for j in range(2):
            place(a_v, 2 + i, j, (uu[i][j] + ud[i][j]) * 0.5)
            place(a_v, 2 + i, 2 + j, uu[i][j])
            place(a_v, 2 + i, 4 + j, ud[i][j])
        place(a_v, 2 + i, 6, sides[2 + i])
    send(a_v, a_out, 2, 4)
    for i in range(2):
        for j in range(2):
            place(a_v, 4 + i, j, (du[i][j] + dd[i][j]) * 0.5)
            place(a_v, 4 + i, 2 + j, du[i][j])
            place(a_v, 4 + i, 4 + j, dd[i][j])
        place(a_v, 4 + i, 6, sides[4 + i])
    send(a_v, a_out, 4, 6)
    hh = symmetric(0, 0)
    for i in range(2):
        for j in range(2):
            place(a_v, i, j, hh[i][j])
            place(a_v, i, 2 + j, (uu[i][j] + du[i][j]) * 0.5)
            place(a_v, i, 4 + j, (ud[i][j] + dd[i][j]) * 0.5)
        place(a_v, i, 6, sides[i])
    send(a_v, a_out, 0, 2)
    for i in range(6):
        place(a_v, 6, i, sides[i].T)
    place(a_v, 6, 6, get(10))
    send(a_v, a_out, 6, 7)
    for copy in copies:
        copy.wait()


def natural_kernel(kept, from_0, from_1, a_inverse, s_inverse, natural, curvature):
    get = reader(kept, (from_0, from_1), BACK_STREAMS[:2])

    grad = jnp.concatenate(
        [jnp.concatenate([get(19 + 2 * i), get(20 + 2 * i)], 1) for i in range(7)], 0
    )
    g_high, g_low = split(grad)
    s_high, s_low = split(s_inverse[...])
    half = dot(g_high, s_high) + (dot(g_high, s_low) + dot(g_low, s_high))
    h_high, h_low = split(half)
    total = jnp.zeros((1, D), F32)
    for i in range(7):
        rows = slice(i * B, (i + 1) * B)
        a_high, a_low = split(a_inverse[rows, :])
        part = dot(a_high, h_high) + (dot(a_high, h_low) + dot(a_low, h_high))
        natural[rows, :] = part
        total = total + jnp.sum(part * grad[rows, :], axis=0, keepdims=True)
    curvature[...] = jnp.broadcast_to(jnp.sum(total, axis=1, keepdims=True), (1, B))


def scale_kernel(natural, curvature, other, direction):
    total = curvature[:, :1] + other[:, :1]
    direction[...] = natural[...] * lax.rsqrt(total * (1.0 / ENTRIES))


def call(kernel, out_shapes, in_spaces, limit_mib, name, scratch=(), flops=0, moved=0, out_space=pltpu.VMEM):
    return pl.pallas_call(
        kernel,
        out_shape=tuple(jax.ShapeDtypeStruct(shape, dtype) for shape, dtype in out_shapes),
        in_specs=[pl.BlockSpec(memory_space=space) for space in in_spaces],
        out_specs=tuple(pl.BlockSpec(memory_space=out_space) for _ in out_shapes),
        scratch_shapes=scratch,
        compiler_params=pltpu.CompilerParams(vmem_limit_bytes=limit_mib * 1024 * 1024),
        cost_estimate=pl.CostEstimate(flops=flops, bytes_accessed=moved, transcendentals=0),
        name=name,
    )


V, S = pltpu.VMEM, pltpu.SMEM


def parity_groups():
    groups = {}
    for place in range(256):
        rest, c = divmod(place, 2)
        rest, x = divmod(rest, 4)
        rest, zh = divmod(rest, 4)
        zl, y = divmod(rest, 4)
        groups.setdefault((zh, c, (x + y + zl) % 2), []).append(place)
    return [groups[key] for key in sorted(groups)]


def same_parity(value):
    axes = ("zl", "y", "zh", "x", "c")
    return lax.all_to_all(value, axes, 0, 0, axis_index_groups=parity_groups(), tiled=True)


LOW, HIGH = [(0, 1), (1, 0), (2, 3), (3, 2)], [(1, 2), (2, 1), (3, 0), (0, 3)]


def to_neighbours(parts):
    ways = (("x", LOW), ("y", LOW), ("zl", [(0, 1), (1, 0)]), ("x", HIGH), ("y", HIGH))
    return [lax.ppermute(part, axis, pairs) for part, (axis, pairs) in zip(parts, ways)]


def core_1(value, axis, pairs):
    return lax.ppermute(value, (axis, "c"), [(2 * a + 1, 2 * b + 1) for a, b in pairs])


def streams_of(streams):
    return [(((end - first) * B, B), F32) for first, end in streams]


def body(features, psi_grad, pair_means, energies, multiplicity, weights, a_inverse, s_inverse):
    feat = features.reshape(HALF, D)
    psi = psi_grad.reshape(HALF, D)
    pair = pair_means.reshape(2, HALF, PAIR)
    swap = [(0, 1), (1, 0)]

    sums = energies
    for axis, pairs in (("zh", LOW), ("x", LOW), ("x", HIGH)):
        sums = sums + core_1(sums, axis, pairs)
    other = lax.ppermute(jnp.concatenate([feat, psi], 1).astype(F32), "c", swap)
    oth_pair = lax.ppermute(pair.astype(F32), "c", swap)
    far = core_1(sums, "zh", HIGH)

    grads = GRADS * B
    out, out_0 = call(
        factors_kernel,
        [((2, KEPT, B), F32), ((2, grads, B), F32)],
        [V] * 7 + [S] * 2,
        26,
        "factors",
        scratch=[
            pltpu.VMEM((2, ROWS, D + PAIR), BF16),
            pltpu.VMEM((2, ROWS, D), F32),
            pltpu.VMEM((2, 2 * WALK, D), BF16),
            pltpu.VMEM((2, ROWS, D), BF16),
            pltpu.VMEM((ROWS, 4 * D + PAIR), BF16),
        ],
        flops=2_500_000_000,
        moved=8_000_000,
    )(feat, pair, psi, other, oth_pair, weights, energies, energies, multiplicity)

    to_0, to_1, to_2, to_3, sums = call(
        tie_kernel,
        [((grads, B), F32)] + streams_of(OUT_STREAMS) + [((1, WALK), F32)],
        [V] * 4,
        8,
        "tie",
        moved=3_000_000,
    )(out, out_0, sums, far)
    from_0 = lax.ppermute(to_0, "x", LOW)
    from_1 = lax.ppermute(to_1, "x", HIGH)
    from_2 = lax.ppermute(to_2, "y", LOW)
    from_3 = lax.ppermute(to_3, "zl", swap)
    sums_1 = lax.ppermute(sums, "c", [(1, 0)])
    (total,) = call(add_kernel, [((KEPT, B), F32)], [V] * 8, 10, "add", moved=3_000_000)(
        out, out_0, from_0, from_1, from_2, from_3, sums, sums_1
    )
    mine = jnp.sum(same_parity(total).reshape(GROUP, CHUNK, B), axis=0)
    one, two, three = (
        lax.ppermute(mine, "zh", [(i, (i + k) % 4) for i in range(4)]) for k in (1, 2, 3)
    )
    mine = (mine + two) + (one + three)
    kept = same_parity(jnp.broadcast_to(mine[None], (GROUP, CHUNK, B)).reshape(KEPT, B))
    parts = call(cut_kernel, streams_of(BACK_STREAMS), [V], 6, "cut", moved=2_200_000)(kept)
    parts = to_neighbours(parts)

    natural, curvature = call(
        natural_kernel,
        [((DIN, D), F32), ((1, B), F32)],
        [V] * 5,
        18,
        "natural",
        flops=1_500_000_000,
        moved=5_000_000,
    )(kept, *parts[:2], a_inverse[0], s_inverse[0])
    other = lax.ppermute(curvature, "c", swap)
    a_sum, s_sum = call(
        unpack_kernel,
        [((DIN, DIN), F32), ((D, D), F32)],
        [V] * 4,
        14,
        "unpack",
        scratch=[pltpu.VMEM((DIN, DIN), F32), pltpu.VMEM((D, D), F32), pltpu.SemaphoreType.DMA((5,))],
        out_space=pl.ANY,
        flops=10_000_000,
        moved=6_000_000,
    )(kept, *parts[2:])
    (direction,) = call(
        scale_kernel, [((DIN, D), F32)], [V] * 3, 6, "scale", flops=1_000_000, moved=2_000_000
    )(natural, curvature, other)
    return a_sum[None], s_sum[None], direction[None]


def solution(mesh):
    fine = Mesh(mesh.devices.reshape(2, 4, 4, 4, 2), ("zl", "y", "zh", "x", "c"))
    twist, walker = ("zl", "y"), ("zh", "x")
    return jax.shard_map(
        body,
        mesh=fine,
        in_specs=(
            P(twist, walker, "c", None),
            P(twist, walker, "c", None),
            P(twist, None, walker, "c", None),
            P(twist, walker),
            P(twist),
            P(),
            P("c", None, None),
            P("c", None, None),
        ),
        out_specs=(P("c", None, None),) * 3,
        check_vma=False,
    )
```

```python
import jax
import jax.numpy as jnp
from jax import lax
from jax.experimental import pallas as pl
from jax.experimental.pallas import tpu as pltpu
from jax.sharding import Mesh, PartitionSpec as P

F32, BF16 = jnp.float32, jnp.bfloat16
D, PAIR, DIN = 256, 128, 896
WALK, HALF, ROWS = 16, 512, 1024
B = 128
GROUP = 16
SLOTS = 17
KEPT = SLOTS * B
CHUNK = KEPT // GROUP
GRADS, FACTORS = 7, 10
OUT_STREAMS = ((0, 6), (6, 12), (12, 17))
BACK_STREAMS = ((0, 4), (4, 7), (7, 12), (12, 15), (15, 17))
ENTRIES = 2 * DIN * D
SHIFT = 7.0


def dot_t(a, b):
    return lax.dot_general(a, b, (((0,), (0,)), ((), ())), preferred_element_type=F32)


def dot_nt(a, b):
    return lax.dot_general(a, b, (((1,), (1,)), ((), ())), preferred_element_type=F32)


def dot(a, b):
    return jnp.dot(a, b, preferred_element_type=F32)


def split(a):
    high = a.astype(BF16)
    return high, (a - high.astype(F32)).astype(BF16)


def per_walker(a):
    n = a.shape[1]
    return jnp.broadcast_to(a[:, None, :], (WALK, HALF // WALK, n)).reshape(HALF, n)


def square_iotas():
    return lax.broadcasted_iota(jnp.int32, (B, B), 0), lax.broadcasted_iota(jnp.int32, (B, B), 1)


def own_parity():
    return lax.rem(lax.axis_index("x") + lax.axis_index("y") + lax.axis_index("zl"), 2)


def walker_table():
    group = lax.broadcasted_iota(jnp.int32, (2 * WALK, ROWS), 1) // (HALF // WALK)
    return (group == lax.broadcasted_iota(jnp.int32, (2 * WALK, ROWS), 0)).astype(BF16)


def place_of(slot):
    if 19 <= slot < 33:
        half, place = divmod(slot - 19, GRADS)
        return half, place
    half, place = divmod(slot if slot < 19 else 19, FACTORS)
    return half, place + GRADS


def forward_kernel(feat, pair, oth_feat, oth_pair, weights, x_s, d_s, m_s):
    mp = lax.axis_index("c")
    own_row = pl.multiple_of(D + D * mp, D)
    oth_row = pl.multiple_of(2 * D - D * mp, D)
    x_s[0, :HALF, :D] = feat[...]
    x_s[0, HALF:, :D] = oth_feat[...].astype(BF16)
    for l in range(2):
        x_s[l, :HALF, D:] = pair[l]
        x_s[l, HALF:, D:] = oth_pair[l].astype(BF16)
    pick = walker_table()
    for l in range(2):
        means = (dot(pick, x_s[l, :, :D]) * (1.0 / 32.0)).astype(BF16)
        m_s[l] = means
        z_walk = dot(means[:WALK], weights[l, pl.ds(own_row, D), :]) + dot(
            means[WALK:], weights[l, pl.ds(oth_row, D), :]
        )
        z_wide = per_walker(z_walk)
        for half in range(2):
            rows = slice(half * HALF, (half + 1) * HALF)
            z = dot(x_s[l, rows, :D], weights[l, :D, :]) + dot(
                x_s[l, rows, D:], weights[l, 3 * D :, :]
            )
            t = jnp.tanh(z + z_wide)
            d_s[l, rows, :] = 1.0 - t * t
            if l == 0:
                x_s[1, rows, :D] = (x_s[0, rows, :D].astype(F32) + t).astype(BF16)


def pair_kernel(after, near, far, sums):
    sums[...] = near[...] + far[...]


def factors_kernel(x_s, d_s, m_s, psi, oth_psi, weights, energies, energy, multiplicity, out, out_0, s_s, w_s):
    mp = lax.axis_index("c")
    own_row = pl.multiple_of(D + D * mp, D)
    oth_row = pl.multiple_of(2 * D - D * mp, D)
    pick = walker_table()
    s_s[1, :HALF, :] = (psi[...].astype(F32) * d_s[1, :HALF, :]).astype(BF16)
    s_s[1, HALF:, :] = (oth_psi[...] * d_s[1, HALF:, :]).astype(BF16)
    q_both = dot(pick, s_s[1])
    q_high, q_low = split(q_both[:WALK] + q_both[WALK:])
    for half in range(2):
        rows = slice(half * HALF, (half + 1) * HALF)
        w_spin = weights[1, pl.ds(own_row if half == 0 else oth_row, D), :]
        spin = (dot_nt(q_high, w_spin) + dot_nt(q_low, w_spin)) * (1.0 / 32.0)
        up = psi[...].astype(F32) if half == 0 else oth_psi[...]
        u = up + dot_nt(s_s[1, rows, :], weights[1, :D, :]) + per_walker(spin)
        s_s[0, rows, :] = (u * d_s[0, rows, :]).astype(BF16)

    l = mp
    mult = multiplicity[0].astype(F32)
    row_scale = mult * (1.0 / 16384.0)
    mean = jnp.sum(energies[...], axis=1, keepdims=True) * (1.0 / WALK)
    shifted = mean + SHIFT
    at_p, at_c, at_low, at_s = D, D + PAIR, 2 * D + PAIR, 3 * D + PAIR
    w_s[:, :at_c] = x_s[l]
    w_s[:, at_s:] = s_s[l]
    step = HALF // WALK
    for w in range(WALK):
        centered = energy[0, w] - mean
        for first in (w * step, HALF + w * step):
            rows = slice(first, first + step)
            high, low = split(centered * w_s[rows, at_s:].astype(F32))
            w_s[rows, at_c:at_low] = high
            w_s[rows, at_low:at_s] = low
    with_h = dot_t(w_s[:, :D], w_s[...])
    with_p = dot_t(w_s[:, at_p:at_c], w_s[:, at_p:])
    with_s = dot_t(w_s[:, at_s:], w_s[:, at_s:])
    totals = dot(pick, w_s[:, at_p:])
    totals = totals[:WALK] + totals[WALK:]
    row, col = square_iotas()

    parity = own_parity()

    def put(slot, value):
        half, place = place_of(slot)
        out[parity ^ half, place * B : (place + 1) * B, :] = value * row_scale

    def put_grad(slot, centered, plain):
        half, place = place_of(slot)
        rows = slice(place * B, (place + 1) * B)
        out[parity ^ half, rows, :] = (centered + shifted * plain) * row_scale
        out_0[parity ^ half, rows, :] = plain * row_scale

    lines = {}

    def put_symmetric(slot, line, full):
        low = full[B:, B:]
        put(slot, jnp.where(col >= row, full[:B, :B], low))
        put(slot + 1, full[:B, B:])
        lines[line] = jnp.sum(jnp.where(col == row, low, 0.0), axis=0, keepdims=True) * row_scale

    put_symmetric(0, 0, with_h[:, :D])
    hp = with_h[:, at_p:at_c]
    put(11, hp[:B])
    put(12, hp[B:])
    put(10, with_p[:, :PAIR])
    hc, hs = with_h[:, at_c:at_low] + with_h[:, at_low:at_s], with_h[:, at_s:]
    pc = with_p[:, PAIR : PAIR + D] + with_p[:, PAIR + D : PAIR + 2 * D]
    ps = with_p[:, PAIR + 2 * D :]
    for j in range(2):
        cols = slice(j * B, (j + 1) * B)
        put_grad(19 + j, hc[:B, cols], hs[:B, cols])
        put_grad(21 + j, hc[B:, cols], hs[B:, cols])
        put_grad(31 + j, pc[:, cols], ps[:, cols])
    put_symmetric(17, 3, with_s)

    means = m_s[l]
    up_first = mp == 0
    up = jnp.where(up_first, means[:WALK].astype(F32), means[WALK:].astype(F32)).astype(BF16)
    down = jnp.where(up_first, means[WALK:].astype(F32), means[:WALK].astype(F32)).astype(BF16)
    both = jnp.concatenate([up, down], 1)
    mm = dot_t(both, both) * 64.0
    put_symmetric(2, 1, mm[:D, :D])
    put_symmetric(4, 2, mm[D:, D:])
    for i in range(2):
        for j in range(2):
            put(6 + 2 * i + j, mm[i * B : (i + 1) * B, D + j * B : D + (j + 1) * B])
    totals = jnp.concatenate(
        [totals[:, :PAIR], totals[:, PAIR : PAIR + D] + totals[:, PAIR + D : PAIR + 2 * D], totals[:, PAIR + 2 * D :]], 1
    )
    t_high, t_low = split(totals)
    side = dot_t(jnp.concatenate([both, both], 0), jnp.concatenate([t_high, t_low], 0))
    for i in range(4):
        rows = slice(i * B, (i + 1) * B)
        put(13 + i, side[rows, :B])
        for j in range(2):
            at = (1 + j) * B
            put_grad(23 + 2 * i + j, side[rows, at : at + B], side[rows, at + D : at + D + B])
    lines[4] = jnp.full((1, B), mult * (1.0 / 16.0), F32)
    last = KEPT - B
    out[parity ^ 1, last:, :] = jnp.zeros((B, B), F32)
    for line, value in lines.items():
        out[parity ^ 1, last + line : last + line + 1, :] = value


def tie_kernel(out, out_0, near, far, to_0, to_1, to_2, to_3, row_sum):
    zh_sum = jnp.sum(near[...] + far[...], axis=1, keepdims=True)
    row_sum[...] = jnp.broadcast_to(zh_sum, (8, B))
    grads = GRADS * B
    to_0[:grads, :] = out_0[1]
    to_0[grads:, :] = row_sum[...]
    for target, (first, end) in zip((to_1, to_2, to_3), OUT_STREAMS):
        target[: (end - first) * B, :] = out[1, first * B : end * B, :]
    to_1[OUT_STREAMS[0][1] * B :, :] = row_sum[...]


def add_kernel(out, out_0, from_0, from_1, from_2, from_3, row_sum, row_two, total):
    grads = GRADS * B
    near, far = from_0[grads:, :], from_1[OUT_STREAMS[0][1] * B :, :]
    energy = (row_sum[...] + row_two[...]) + (near + far)
    shifted = energy[:1, :] * (1.0 / 256.0) + SHIFT
    for part, (first, end) in zip((from_1, from_2, from_3), OUT_STREAMS):
        for place in range(first, end):
            rows = slice(place * B, (place + 1) * B)
            value = out[0, rows, :] + part[(place - first) * B : (place - first + 1) * B, :]
            if place < GRADS:
                value = value - shifted * (out_0[0, rows, :] + from_0[rows, :])
            total[rows, :] = value


def cut_kernel(kept, to_0, to_1, to_2, to_3, to_4):
    for target, (first, end) in zip((to_0, to_1, to_2, to_3, to_4), BACK_STREAMS):
        target[...] = kept[first * B : end * B, :]


def reader(kept, parts, streams):
    parity = own_parity()

    def read(slot, size=B):
        half, place = place_of(slot)
        for part, (begin, end) in zip(parts, streams):
            if begin <= place < end:
                other = part[(place - begin) * B : (place - begin) * B + size, :]
        own = kept[place * B : place * B + size, :]
        return jnp.where(parity == half, own, other)

    return read


def unpack_kernel(kept, from_2, from_3, from_4, a_out, s_out, done, a_v, s_v, sems):
    row, col = square_iotas()
    read = reader(kept, (from_2, from_3, from_4), BACK_STREAMS[2:])
    lines = read(33, 8)
    inverse = 1.0 / lines[4:5, :]
    copies = []

    def get(slot):
        return read(slot) * inverse

    def symmetric(slot, line):
        tri = get(slot)
        off = get(slot + 1)
        flipped = tri.T
        diag = lines[line : line + 1, :] * inverse
        first = jnp.where(col >= row, tri, flipped)
        second = jnp.where(col < row, tri, flipped)
        second = jnp.where(col == row, jnp.broadcast_to(diag, (B, B)), second)
        return [[first, off], [off.T, second]]

    def place(target, i, j, value):
        target[i * B : (i + 1) * B, j * B : (j + 1) * B] = value

    def send(source, target, first, end):
        rows = slice(first * B, end * B)
        copy = pltpu.make_async_copy(source.at[rows], target.at[rows], sems.at[len(copies)])
        copy.start()
        copies.append(copy)

    ss = symmetric(17, 3)
    for i in range(2):
        for j in range(2):
            place(s_v, i, j, ss[i][j])
    send(s_v, s_out, 0, 2)
    uu = symmetric(2, 1)
    dd = symmetric(4, 2)
    ud = [[get(6 + 2 * i + j) for j in range(2)] for i in range(2)]
    du = [[ud[j][i].T for j in range(2)] for i in range(2)]
    sides = [get(11 + i) for i in range(6)]
    for i in range(2):
        for j in range(2):
            place(a_v, 2 + i, j, (uu[i][j] + ud[i][j]) * 0.5)
            place(a_v, 2 + i, 2 + j, uu[i][j])
            place(a_v, 2 + i, 4 + j, ud[i][j])
        place(a_v, 2 + i, 6, sides[2 + i])
    send(a_v, a_out, 2, 4)
    for i in range(2):
        for j in range(2):
            place(a_v, 4 + i, j, (du[i][j] + dd[i][j]) * 0.5)
            place(a_v, 4 + i, 2 + j, du[i][j])
            place(a_v, 4 + i, 4 + j, dd[i][j])
        place(a_v, 4 + i, 6, sides[4 + i])
    send(a_v, a_out, 4, 6)
    hh = symmetric(0, 0)
    for i in range(2):
        for j in range(2):
            place(a_v, i, j, hh[i][j])
            place(a_v, i, 2 + j, (uu[i][j] + du[i][j]) * 0.5)
            place(a_v, i, 4 + j, (ud[i][j] + dd[i][j]) * 0.5)
        place(a_v, i, 6, sides[i])
    send(a_v, a_out, 0, 2)
    for i in range(6):
        place(a_v, 6, i, sides[i].T)
    place(a_v, 6, 6, get(10))
    send(a_v, a_out, 6, 7)
    for copy in copies:
        copy.wait()
    done[...] = inverse


def natural_kernel(kept, from_0, from_1, a_inverse, s_inverse, natural, curvature):
    get = reader(kept, (from_0, from_1), BACK_STREAMS[:2])

    grad = jnp.concatenate(
        [jnp.concatenate([get(19 + 2 * i), get(20 + 2 * i)], 1) for i in range(7)], 0
    )
    g_high, g_low = split(grad)
    s_high, s_low = split(s_inverse[...])
    half = dot(g_high, s_high) + (dot(g_high, s_low) + dot(g_low, s_high))
    h_high, h_low = split(half)
    total = jnp.zeros((1, D), F32)
    for i in range(7):
        rows = slice(i * B, (i + 1) * B)
        a_high, a_low = split(a_inverse[rows, :])
        part = dot(a_high, h_high) + (dot(a_high, h_low) + dot(a_low, h_high))
        natural[rows, :] = part
        total = total + jnp.sum(part * grad[rows, :], axis=0, keepdims=True)
    curvature[...] = jnp.broadcast_to(jnp.sum(total, axis=1, keepdims=True), (1, B))


def scale_kernel(natural, curvature, other, after, direction):
    total = curvature[:, :1] + other[:, :1]
    direction[...] = natural[...] * lax.rsqrt(total * (1.0 / ENTRIES))


def call(kernel, out_shapes, in_spaces, limit_mib, name, scratch=(), flops=0, moved=0, out_spaces=None):
    return pl.pallas_call(
        kernel,
        out_shape=tuple(jax.ShapeDtypeStruct(shape, dtype) for shape, dtype in out_shapes),
        in_specs=[pl.BlockSpec(memory_space=space) for space in in_spaces],
        out_specs=tuple(pl.BlockSpec(memory_space=space) for space in out_spaces or [V] * len(out_shapes)),
        scratch_shapes=scratch,
        compiler_params=pltpu.CompilerParams(vmem_limit_bytes=limit_mib * 1024 * 1024),
        cost_estimate=pl.CostEstimate(flops=flops, bytes_accessed=moved, transcendentals=0),
        name=name,
    )


V, S = pltpu.VMEM, pltpu.SMEM


def parity_groups():
    groups = {}
    for place in range(256):
        rest, c = divmod(place, 2)
        rest, x = divmod(rest, 4)
        rest, zh = divmod(rest, 4)
        zl, y = divmod(rest, 4)
        groups.setdefault((zh, c, (x + y + zl) % 2), []).append(place)
    return [groups[key] for key in sorted(groups)]


def same_parity(value):
    axes = ("zl", "y", "zh", "x", "c")
    return lax.all_to_all(value, axes, 0, 0, axis_index_groups=parity_groups(), tiled=True)


LOW, HIGH = [(0, 1), (1, 0), (2, 3), (3, 2)], [(1, 2), (2, 1), (3, 0), (0, 3)]


def to_neighbours(parts):
    ways = (("x", LOW), ("y", LOW), ("zl", [(0, 1), (1, 0)]), ("x", HIGH), ("y", HIGH))
    return [lax.ppermute(part, axis, pairs) for part, (axis, pairs) in zip(parts, ways)]


def streams_of(streams):
    return [(((end - first) * B, B), F32) for first, end in streams]


def body(features, psi_grad, pair_means, energies, multiplicity, weights, a_inverse, s_inverse):
    feat = features.reshape(HALF, D)
    psi = psi_grad.reshape(HALF, D)
    pair = pair_means.reshape(2, HALF, PAIR)
    swap = [(0, 1), (1, 0)]

    oth_feat = lax.ppermute(feat.astype(F32), "c", swap)
    oth_pair = lax.ppermute(pair.astype(F32), "c", swap)
    far_1 = lax.ppermute(energies, "zh", LOW)
    oth_psi = lax.ppermute(psi.astype(F32), "c", swap)

    x_s, d_s, m_s = call(
        forward_kernel,
        [((2, ROWS, D + PAIR), BF16), ((2, ROWS, D), F32), ((2, 2 * WALK, D), BF16)],
        [V] * 5,
        16,
        "forward",
        flops=1_000_000_000,
        moved=6_000_000,
    )(feat, pair, oth_feat, oth_pair, weights)
    (sum_2,) = call(pair_kernel, [((1, WALK), F32)], [V] * 3, 4, "pair")(m_s, energies, far_1)
    far_2 = lax.ppermute(sum_2, "zh", HIGH)

    grads = GRADS * B
    out, out_0 = call(
        factors_kernel,
        [((2, KEPT, B), F32), ((2, grads, B), F32)],
        [V] * 7 + [S] * 2,
        24,
        "factors",
        scratch=[
            pltpu.VMEM((2, ROWS, D), BF16),
            pltpu.VMEM((ROWS, 4 * D + PAIR), BF16),
        ],
        flops=2_500_000_000,
        moved=8_000_000,
    )(x_s, d_s, m_s, psi, oth_psi, weights, energies, energies, multiplicity)

    sizes = [((end - first) * B, B) for first, end in OUT_STREAMS]
    to_0, to_1, to_2, to_3, row_sum = call(
        tie_kernel,
        [((grads + 8, B), F32), ((sizes[0][0] + 8, B), F32), (sizes[1], F32), (sizes[2], F32), ((8, B), F32)],
        [V] * 4,
        8,
        "tie",
        moved=3_000_000,
    )(out, out_0, sum_2, far_2)
    from_0 = lax.ppermute(to_0, "x", LOW)
    from_1 = lax.ppermute(to_1, "x", HIGH)
    from_2 = lax.ppermute(to_2, "y", LOW)
    from_3 = lax.ppermute(to_3, "zl", swap)
    row_two = lax.ppermute(row_sum, "x", [(0, 2), (1, 3), (2, 0), (3, 1)])
    (total,) = call(add_kernel, [((KEPT, B), F32)], [V] * 8, 10, "add", moved=3_000_000)(
        out, out_0, from_0, from_1, from_2, from_3, row_sum, row_two
    )
    mine = jnp.sum(same_parity(total).reshape(GROUP, CHUNK, B), axis=0)
    one, two, three = (
        lax.ppermute(mine, "zh", [(i, (i + k) % 4) for i in range(4)]) for k in (1, 2, 3)
    )
    mine = (mine + two) + (one + three)
    kept = same_parity(jnp.broadcast_to(mine[None], (GROUP, CHUNK, B)).reshape(KEPT, B))
    parts = call(cut_kernel, streams_of(BACK_STREAMS), [V], 6, "cut", moved=2_200_000)(kept)
    parts = to_neighbours(parts)

    natural, curvature = call(
        natural_kernel,
        [((DIN, D), F32), ((1, B), F32)],
        [V] * 5,
        18,
        "natural",
        flops=1_500_000_000,
        moved=5_000_000,
    )(kept, *parts[:2], a_inverse[0], s_inverse[0])
    other = lax.ppermute(curvature, "c", swap)
    a_sum, s_sum, done = call(
        unpack_kernel,
        [((DIN, DIN), F32), ((D, D), F32), ((1, B), F32)],
        [V] * 4,
        14,
        "unpack",
        scratch=[pltpu.VMEM((DIN, DIN), F32), pltpu.VMEM((D, D), F32), pltpu.SemaphoreType.DMA((5,))],
        out_spaces=(pl.ANY, pl.ANY, V),
        flops=10_000_000,
        moved=6_000_000,
    )(kept, *parts[2:])
    (direction,) = call(
        scale_kernel, [((DIN, D), F32)], [V] * 4, 6, "scale", flops=1_000_000, moved=2_000_000
    )(natural, curvature, other, done)
    return a_sum[None], s_sum[None], direction[None]


def solution(mesh):
    fine = Mesh(mesh.devices.reshape(2, 4, 4, 4, 2), ("zl", "y", "zh", "x", "c"))
    twist, walker = ("zl", "y"), ("zh", "x")
    return jax.shard_map(
        body,
        mesh=fine,
        in_specs=(
            P(twist, walker, "c", None),
            P(twist, walker, "c", None),
            P(twist, None, walker, "c", None),
            P(twist, walker),
            P(twist),
            P(),
            P("c", None, None),
            P("c", None, None),
        ),
        out_specs=(P("c", None, None),) * 3,
        check_vma=False,
    )
```

```python
import jax
import jax.numpy as jnp
from jax import lax
from jax.experimental import pallas as pl
from jax.experimental.pallas import tpu as pltpu
from jax.sharding import Mesh, PartitionSpec as P

F32, BF16 = jnp.float32, jnp.bfloat16
D, PAIR, DIN = 256, 128, 896
WALK, HALF, ROWS = 16, 512, 1024
B = 128
GROUP = 16
SLOTS = 17
KEPT = SLOTS * B
CHUNK = KEPT // GROUP
GRADS, FACTORS = 7, 10
OUT_STREAMS = ((0, 6), (6, 12), (12, 17))
BACK_STREAMS = ((0, 4), (4, 7), (7, 12), (12, 15), (15, 17))
ENTRIES = 2 * DIN * D
SHIFT = 7.0


def dot_t(a, b):
    return lax.dot_general(a, b, (((0,), (0,)), ((), ())), preferred_element_type=F32)


def dot_nt(a, b):
    return lax.dot_general(a, b, (((1,), (1,)), ((), ())), preferred_element_type=F32)


def dot(a, b):
    return jnp.dot(a, b, preferred_element_type=F32)


def split(a):
    high = a.astype(BF16)
    return high, (a - high.astype(F32)).astype(BF16)


def per_walker(a):
    n = a.shape[1]
    return jnp.broadcast_to(a[:, None, :], (WALK, HALF // WALK, n)).reshape(HALF, n)


def square_iotas():
    return lax.broadcasted_iota(jnp.int32, (B, B), 0), lax.broadcasted_iota(jnp.int32, (B, B), 1)


def own_parity():
    return lax.rem(lax.axis_index("x") + lax.axis_index("y") + lax.axis_index("zl"), 2)


def walker_table():
    group = lax.broadcasted_iota(jnp.int32, (2 * WALK, ROWS), 1) // (HALF // WALK)
    return (group == lax.broadcasted_iota(jnp.int32, (2 * WALK, ROWS), 0)).astype(BF16)


def place_of(slot):
    if 19 <= slot < 33:
        half, place = divmod(slot - 19, GRADS)
        return half, place
    half, place = divmod(slot if slot < 19 else 19, FACTORS)
    return half, place + GRADS


def factors_kernel(
    feat, pair, psi, other, oth_pair, weights, energies, energy, multiplicity,
    out, out_0, x_s, d_s, m_s, s_s, w_s
):
    mp = lax.axis_index("c")
    own_row = pl.multiple_of(D + D * mp, D)
    oth_row = pl.multiple_of(2 * D - D * mp, D)
    x_s[0, :HALF, :D] = feat[...]
    x_s[0, HALF:, :D] = other[:, :D].astype(BF16)
    for l in range(2):
        x_s[l, :HALF, D:] = pair[l]
        x_s[l, HALF:, D:] = oth_pair[l].astype(BF16)
    pick = walker_table()
    for l in range(2):
        means = (dot(pick, x_s[l, :, :D]) * (1.0 / 32.0)).astype(BF16)
        m_s[l] = means
        z_walk = dot(means[:WALK], weights[l, pl.ds(own_row, D), :]) + dot(
            means[WALK:], weights[l, pl.ds(oth_row, D), :]
        )
        z_wide = per_walker(z_walk)
        for half in range(2):
            rows = slice(half * HALF, (half + 1) * HALF)
            z = dot(x_s[l, rows, :D], weights[l, :D, :]) + dot(
                x_s[l, rows, D:], weights[l, 3 * D :, :]
            )
            t = jnp.tanh(z + z_wide)
            d_s[l, rows, :] = 1.0 - t * t
            if l == 0:
                x_s[1, rows, :D] = (x_s[0, rows, :D].astype(F32) + t).astype(BF16)

    s_s[1, :HALF, :] = (psi[...].astype(F32) * d_s[1, :HALF, :]).astype(BF16)
    s_s[1, HALF:, :] = (other[:, D : 2 * D] * d_s[1, HALF:, :]).astype(BF16)
    q_both = dot(pick, s_s[1])
    q_high, q_low = split(q_both[:WALK] + q_both[WALK:])
    for half in range(2):
        rows = slice(half * HALF, (half + 1) * HALF)
        w_spin = weights[1, pl.ds(own_row if half == 0 else oth_row, D), :]
        spin = (dot_nt(q_high, w_spin) + dot_nt(q_low, w_spin)) * (1.0 / 32.0)
        up = psi[...].astype(F32) if half == 0 else other[:, D : 2 * D]
        u = up + dot_nt(s_s[1, rows, :], weights[1, :D, :]) + per_walker(spin)
        s_s[0, rows, :] = (u * d_s[0, rows, :]).astype(BF16)

    l = mp
    mult = multiplicity[0].astype(F32)
    row_scale = mult * (1.0 / 16384.0)
    mean = jnp.sum(energies[...], axis=1, keepdims=True) * (1.0 / WALK)
    shifted = mean + SHIFT
    at_p, at_c, at_low, at_s = D, D + PAIR, 2 * D + PAIR, 3 * D + PAIR
    w_s[:, :at_c] = x_s[l]
    w_s[:, at_s:] = s_s[l]
    step = HALF // WALK
    for w in range(WALK):
        centered = energy[0, w] - mean
        for first in (w * step, HALF + w * step):
            rows = slice(first, first + step)
            high, low = split(centered * w_s[rows, at_s:].astype(F32))
            w_s[rows, at_c:at_low] = high
            w_s[rows, at_low:at_s] = low
    with_h = dot_t(w_s[:, :D], w_s[...])
    with_p = dot_t(w_s[:, at_p:at_c], w_s[:, at_p:])
    with_s = dot_t(w_s[:, at_s:], w_s[:, at_s:])
    totals = dot(pick, w_s[:, at_p:])
    totals = totals[:WALK] + totals[WALK:]
    row, col = square_iotas()

    parity = own_parity()

    def put(slot, value):
        half, place = place_of(slot)
        out[parity ^ half, place * B : (place + 1) * B, :] = value * row_scale

    def put_grad(slot, centered, plain):
        half, place = place_of(slot)
        rows = slice(place * B, (place + 1) * B)
        out[parity ^ half, rows, :] = (centered + shifted * plain) * row_scale
        out_0[parity ^ half, rows, :] = plain * row_scale

    lines = {}

    def put_symmetric(slot, line, full):
        low = full[B:, B:]
        put(slot, jnp.where(col >= row, full[:B, :B], low))
        put(slot + 1, full[:B, B:])
        lines[line] = jnp.sum(jnp.where(col == row, low, 0.0), axis=0, keepdims=True) * row_scale

    put_symmetric(0, 0, with_h[:, :D])
    hp = with_h[:, at_p:at_c]
    put(11, hp[:B])
    put(12, hp[B:])
    put(10, with_p[:, :PAIR])
    hc, hs = with_h[:, at_c:at_low] + with_h[:, at_low:at_s], with_h[:, at_s:]
    pc = with_p[:, PAIR : PAIR + D] + with_p[:, PAIR + D : PAIR + 2 * D]
    ps = with_p[:, PAIR + 2 * D :]
    for j in range(2):
        cols = slice(j * B, (j + 1) * B)
        put_grad(19 + j, hc[:B, cols], hs[:B, cols])
        put_grad(21 + j, hc[B:, cols], hs[B:, cols])
        put_grad(31 + j, pc[:, cols], ps[:, cols])
    put_symmetric(17, 3, with_s)

    means = m_s[l]
    up_first = mp == 0
    up = jnp.where(up_first, means[:WALK].astype(F32), means[WALK:].astype(F32)).astype(BF16)
    down = jnp.where(up_first, means[WALK:].astype(F32), means[:WALK].astype(F32)).astype(BF16)
    both = jnp.concatenate([up, down], 1)
    mm = dot_t(both, both) * 64.0
    put_symmetric(2, 1, mm[:D, :D])
    put_symmetric(4, 2, mm[D:, D:])
    for i in range(2):
        for j in range(2):
            put(6 + 2 * i + j, mm[i * B : (i + 1) * B, D + j * B : D + (j + 1) * B])
    totals = jnp.concatenate(
        [totals[:, :PAIR], totals[:, PAIR : PAIR + D] + totals[:, PAIR + D : PAIR + 2 * D], totals[:, PAIR + 2 * D :]], 1
    )
    t_high, t_low = split(totals)
    side = dot_t(jnp.concatenate([both, both], 0), jnp.concatenate([t_high, t_low], 0))
    for i in range(4):
        rows = slice(i * B, (i + 1) * B)
        put(13 + i, side[rows, :B])
        for j in range(2):
            at = (1 + j) * B
            put_grad(23 + 2 * i + j, side[rows, at : at + B], side[rows, at + D : at + D + B])
    lines[4] = jnp.full((1, B), mult * (1.0 / 16.0), F32)
    last = KEPT - B
    out[parity ^ 1, last:, :] = jnp.zeros((B, B), F32)
    for line, value in lines.items():
        out[parity ^ 1, last + line : last + line + 1, :] = value


def tie_kernel(out, out_0, own, one, two, three, to_0, to_1, to_2, to_3, row_sum):
    four = (own[...] + two[...]) + (one[...] + three[...])
    zh_sum = jnp.sum(four, axis=1, keepdims=True)
    row_sum[...] = jnp.broadcast_to(zh_sum, (8, B))
    grads = GRADS * B
    to_0[:grads, :] = out_0[1]
    to_0[grads:, :] = row_sum[...]
    for target, (first, end) in zip((to_1, to_2, to_3), OUT_STREAMS):
        target[: (end - first) * B, :] = out[1, first * B : end * B, :]
    to_1[OUT_STREAMS[0][1] * B :, :] = row_sum[...]


def add_kernel(out, out_0, from_0, from_1, from_2, from_3, row_sum, row_two, total):
    grads = GRADS * B
    near, far = from_0[grads:, :], from_1[OUT_STREAMS[0][1] * B :, :]
    energy = (row_sum[...] + row_two[...]) + (near + far)
    shifted = energy[:1, :] * (1.0 / 256.0) + SHIFT
    for part, (first, end) in zip((from_1, from_2, from_3), OUT_STREAMS):
        for place in range(first, end):
            rows = slice(place * B, (place + 1) * B)
            value = out[0, rows, :] + part[(place - first) * B : (place - first + 1) * B, :]
            if place < GRADS:
                value = value - shifted * (out_0[0, rows, :] + from_0[rows, :])
            total[rows, :] = value


def cut_kernel(kept, to_0, to_1, to_2, to_3, to_4):
    for target, (first, end) in zip((to_0, to_1, to_2, to_3, to_4), BACK_STREAMS):
        target[...] = kept[first * B : end * B, :]


def reader(kept, parts, streams):
    parity = own_parity()

    def read(slot, size=B):
        half, place = place_of(slot)
        for part, (begin, end) in zip(parts, streams):
            if begin <= place < end:
                other = part[(place - begin) * B : (place - begin) * B + size, :]
        own = kept[place * B : place * B + size, :]
        return jnp.where(parity == half, own, other)

    return read


def unpack_kernel(kept, from_2, from_3, from_4, a_out, s_out, done, a_v, s_v, sems):
    row, col = square_iotas()
    read = reader(kept, (from_2, from_3, from_4), BACK_STREAMS[2:])
    lines = read(33, 8)
    inverse = 1.0 / lines[4:5, :]
    copies = []

    def get(slot):
        return read(slot) * inverse

    def symmetric(slot, line):
        tri = get(slot)
        off = get(slot + 1)
        flipped = tri.T
        diag = lines[line : line + 1, :] * inverse
        first = jnp.where(col >= row, tri, flipped)
        second = jnp.where(col < row, tri, flipped)
        second = jnp.where(col == row, jnp.broadcast_to(diag, (B, B)), second)
        return [[first, off], [off.T, second]]

    def place(target, i, j, value):
        target[i * B : (i + 1) * B, j * B : (j + 1) * B] = value

    def send(source, target, first, end):
        rows = slice(first * B, end * B)
        copy = pltpu.make_async_copy(source.at[rows], target.at[rows], sems.at[len(copies)])
        copy.start()
        copies.append(copy)

    ss = symmetric(17, 3)
    for i in range(2):
        for j in range(2):
            place(s_v, i, j, ss[i][j])
    send(s_v, s_out, 0, 2)
    uu = symmetric(2, 1)
    dd = symmetric(4, 2)
    ud = [[get(6 + 2 * i + j) for j in range(2)] for i in range(2)]
    du = [[ud[j][i].T for j in range(2)] for i in range(2)]
    sides = [get(11 + i) for i in range(6)]
    for i in range(2):
        for j in range(2):
            place(a_v, 2 + i, j, (uu[i][j] + ud[i][j]) * 0.5)
            place(a_v, 2 + i, 2 + j, uu[i][j])
            place(a_v, 2 + i, 4 + j, ud[i][j])
        place(a_v, 2 + i, 6, sides[2 + i])
    send(a_v, a_out, 2, 4)
    for i in range(2):
        for j in range(2):
            place(a_v, 4 + i, j, (du[i][j] + dd[i][j]) * 0.5)
            place(a_v, 4 + i, 2 + j, du[i][j])
            place(a_v, 4 + i, 4 + j, dd[i][j])
        place(a_v, 4 + i, 6, sides[4 + i])
    send(a_v, a_out, 4, 6)
    hh = symmetric(0, 0)
    for i in range(2):
        for j in range(2):
            place(a_v, i, j, hh[i][j])
            place(a_v, i, 2 + j, (uu[i][j] + du[i][j]) * 0.5)
            place(a_v, i, 4 + j, (ud[i][j] + dd[i][j]) * 0.5)
        place(a_v, i, 6, sides[i])
    send(a_v, a_out, 0, 2)
    for i in range(6):
        place(a_v, 6, i, sides[i].T)
    place(a_v, 6, 6, get(10))
    send(a_v, a_out, 6, 7)
    for copy in copies:
        copy.wait()
    done[...] = inverse


def natural_kernel(kept, from_0, from_1, a_inverse, s_inverse, natural, curvature):
    get = reader(kept, (from_0, from_1), BACK_STREAMS[:2])

    grad = jnp.concatenate(
        [jnp.concatenate([get(19 + 2 * i), get(20 + 2 * i)], 1) for i in range(7)], 0
    )
    g_high, g_low = split(grad)
    s_high, s_low = split(s_inverse[...])
    half = dot(g_high, s_high) + (dot(g_high, s_low) + dot(g_low, s_high))
    h_high, h_low = split(half)
    total = jnp.zeros((1, D), F32)
    for i in range(7):
        rows = slice(i * B, (i + 1) * B)
        a_high, a_low = split(a_inverse[rows, :])
        part = dot(a_high, h_high) + (dot(a_high, h_low) + dot(a_low, h_high))
        natural[rows, :] = part
        total = total + jnp.sum(part * grad[rows, :], axis=0, keepdims=True)
    curvature[...] = jnp.broadcast_to(jnp.sum(total, axis=1, keepdims=True), (1, B))


def scale_kernel(natural, curvature, other, after, direction):
    total = curvature[:, :1] + other[:, :1]
    direction[...] = natural[...] * lax.rsqrt(total * (1.0 / ENTRIES))


def call(kernel, out_shapes, in_spaces, limit_mib, name, scratch=(), flops=0, moved=0, out_spaces=None):
    return pl.pallas_call(
        kernel,
        out_shape=tuple(jax.ShapeDtypeStruct(shape, dtype) for shape, dtype in out_shapes),
        in_specs=[pl.BlockSpec(memory_space=space) for space in in_spaces],
        out_specs=tuple(pl.BlockSpec(memory_space=space) for space in out_spaces or [V] * len(out_shapes)),
        scratch_shapes=scratch,
        compiler_params=pltpu.CompilerParams(vmem_limit_bytes=limit_mib * 1024 * 1024),
        cost_estimate=pl.CostEstimate(flops=flops, bytes_accessed=moved, transcendentals=0),
        name=name,
    )


V, S = pltpu.VMEM, pltpu.SMEM


def parity_groups():
    groups = {}
    for place in range(256):
        rest, c = divmod(place, 2)
        rest, x = divmod(rest, 4)
        rest, zh = divmod(rest, 4)
        zl, y = divmod(rest, 4)
        groups.setdefault((zh, c, (x + y + zl) % 2), []).append(place)
    return [groups[key] for key in sorted(groups)]


def same_parity(value):
    axes = ("zl", "y", "zh", "x", "c")
    return lax.all_to_all(value, axes, 0, 0, axis_index_groups=parity_groups(), tiled=True)


LOW, HIGH = [(0, 1), (1, 0), (2, 3), (3, 2)], [(1, 2), (2, 1), (3, 0), (0, 3)]


def to_neighbours(parts):
    ways = (("x", LOW), ("y", LOW), ("zl", [(0, 1), (1, 0)]), ("x", HIGH), ("y", HIGH))
    return [lax.ppermute(part, axis, pairs) for part, (axis, pairs) in zip(parts, ways)]


def turned(value):
    return [lax.ppermute(value, "zh", [(i, (i + k) % 4) for i in range(4)]) for k in (1, 2, 3)]


def streams_of(streams):
    return [(((end - first) * B, B), F32) for first, end in streams]


def body(features, psi_grad, pair_means, energies, multiplicity, weights, a_inverse, s_inverse):
    feat = features.reshape(HALF, D)
    psi = psi_grad.reshape(HALF, D)
    pair = pair_means.reshape(2, HALF, PAIR)
    swap = [(0, 1), (1, 0)]

    other = lax.ppermute(jnp.concatenate([feat, psi], 1).astype(F32), "c", swap)
    oth_pair = lax.ppermute(pair.astype(F32), "c", swap)
    row = turned(energies)

    grads = GRADS * B
    out, out_0 = call(
        factors_kernel,
        [((2, KEPT, B), F32), ((2, grads, B), F32)],
        [V] * 7 + [S] * 2,
        26,
        "factors",
        scratch=[
            pltpu.VMEM((2, ROWS, D + PAIR), BF16),
            pltpu.VMEM((2, ROWS, D), F32),
            pltpu.VMEM((2, 2 * WALK, D), BF16),
            pltpu.VMEM((2, ROWS, D), BF16),
            pltpu.VMEM((ROWS, 4 * D + PAIR), BF16),
        ],
        flops=2_500_000_000,
        moved=8_000_000,
    )(feat, pair, psi, other, oth_pair, weights, energies, energies, multiplicity)

    sizes = [((end - first) * B, B) for first, end in OUT_STREAMS]
    to_0, to_1, to_2, to_3, row_sum = call(
        tie_kernel,
        [((grads + 8, B), F32), ((sizes[0][0] + 8, B), F32), (sizes[1], F32), (sizes[2], F32), ((8, B), F32)],
        [V] * 6,
        8,
        "tie",
        moved=3_000_000,
    )(out, out_0, energies, *row)
    from_0 = lax.ppermute(to_0, "x", LOW)
    from_1 = lax.ppermute(to_1, "x", HIGH)
    from_2 = lax.ppermute(to_2, "y", LOW)
    from_3 = lax.ppermute(to_3, "zl", swap)
    row_two = lax.ppermute(row_sum, "x", [(0, 2), (1, 3), (2, 0), (3, 1)])
    (total,) = call(add_kernel, [((KEPT, B), F32)], [V] * 8, 10, "add", moved=3_000_000)(
        out, out_0, from_0, from_1, from_2, from_3, row_sum, row_two
    )
    mine = jnp.sum(same_parity(total).reshape(GROUP, CHUNK, B), axis=0)
    one, two, three = turned(mine)
    mine = (mine + two) + (one + three)
    kept = same_parity(jnp.broadcast_to(mine[None], (GROUP, CHUNK, B)).reshape(KEPT, B))
    parts = call(cut_kernel, streams_of(BACK_STREAMS), [V], 6, "cut", moved=2_200_000)(kept)
    parts = to_neighbours(parts)

    natural, curvature = call(
        natural_kernel,
        [((DIN, D), F32), ((1, B), F32)],
        [V] * 5,
        18,
        "natural",
        flops=1_500_000_000,
        moved=5_000_000,
    )(kept, *parts[:2], a_inverse[0], s_inverse[0])
    other = lax.ppermute(curvature, "c", swap)
    a_sum, s_sum, done = call(
        unpack_kernel,
        [((DIN, DIN), F32), ((D, D), F32), ((1, B), F32)],
        [V] * 4,
        14,
        "unpack",
        scratch=[pltpu.VMEM((DIN, DIN), F32), pltpu.VMEM((D, D), F32), pltpu.SemaphoreType.DMA((5,))],
        out_spaces=(pl.ANY, pl.ANY, V),
        flops=10_000_000,
        moved=6_000_000,
    )(kept, *parts[2:])
    (direction,) = call(
        scale_kernel, [((DIN, D), F32)], [V] * 4, 6, "scale", flops=1_000_000, moved=2_000_000
    )(natural, curvature, other, done)
    return a_sum[None], s_sum[None], direction[None]


def solution(mesh):
    fine = Mesh(mesh.devices.reshape(2, 4, 4, 4, 2), ("zl", "y", "zh", "x", "c"))
    twist, walker = ("zl", "y"), ("zh", "x")
    return jax.shard_map(
        body,
        mesh=fine,
        in_specs=(
            P(twist, walker, "c", None),
            P(twist, walker, "c", None),
            P(twist, None, walker, "c", None),
            P(twist, walker),
            P(twist),
            P(),
            P("c", None, None),
            P("c", None, None),
        ),
        out_specs=(P("c", None, None),) * 3,
        check_vma=False,
    )
```

```python
import jax
import jax.numpy as jnp
from jax import lax
from jax.experimental import pallas as pl
from jax.experimental.pallas import tpu as pltpu
from jax.sharding import Mesh, PartitionSpec as P

F32, BF16 = jnp.float32, jnp.bfloat16
D, PAIR, DIN = 256, 128, 896
WALK, HALF, ROWS = 16, 512, 1024
B = 128
GROUP = 16
SLOTS = 17
KEPT = SLOTS * B
CHUNK = KEPT // GROUP
GRADS, FACTORS = 7, 10
OUT_STREAMS = ((0, 9), (9, 17))
PLAIN_STREAMS = ((0, 4), (4, 7))
BACK_STREAMS = ((0, 6), (6, 11), (11, 14), (14, 17))
ENTRIES = 2 * DIN * D
SHIFT = 7.0


def dot_t(a, b):
    return lax.dot_general(a, b, (((0,), (0,)), ((), ())), preferred_element_type=F32)


def dot_nt(a, b):
    return lax.dot_general(a, b, (((1,), (1,)), ((), ())), preferred_element_type=F32)


def dot(a, b):
    return jnp.dot(a, b, preferred_element_type=F32)


def split(a):
    high = a.astype(BF16)
    return high, (a - high.astype(F32)).astype(BF16)


def per_walker(a):
    n = a.shape[1]
    return jnp.broadcast_to(a[:, None, :], (WALK, HALF // WALK, n)).reshape(HALF, n)


def square_iotas():
    return lax.broadcasted_iota(jnp.int32, (B, B), 0), lax.broadcasted_iota(jnp.int32, (B, B), 1)


def own_parity():
    return lax.rem(lax.axis_index("x") + lax.axis_index("y") + lax.axis_index("zl"), 2)


def walker_table():
    group = lax.broadcasted_iota(jnp.int32, (2 * WALK, ROWS), 1) // (HALF // WALK)
    return (group == lax.broadcasted_iota(jnp.int32, (2 * WALK, ROWS), 0)).astype(BF16)


def place_of(slot):
    if 19 <= slot < 33:
        half, place = divmod(slot - 19, GRADS)
        return half, place
    half, place = divmod(slot if slot < 19 else 19, FACTORS)
    return half, place + GRADS


def forward_kernel(feat, pair, oth_feat, oth_pair, weights, x_s, d_s, m_s):
    mp = lax.axis_index("c")
    own_row = pl.multiple_of(D + D * mp, D)
    oth_row = pl.multiple_of(2 * D - D * mp, D)
    x_s[0, :HALF, :D] = feat[...]
    x_s[0, HALF:, :D] = oth_feat[...].astype(BF16)
    for l in range(2):
        x_s[l, :HALF, D:] = pair[l]
        x_s[l, HALF:, D:] = oth_pair[l].astype(BF16)
    pick = walker_table()
    for l in range(2):
        means = (dot(pick, x_s[l, :, :D]) * (1.0 / 32.0)).astype(BF16)
        m_s[l] = means
        z_walk = dot(means[:WALK], weights[l, pl.ds(own_row, D), :]) + dot(
            means[WALK:], weights[l, pl.ds(oth_row, D), :]
        )
        z_wide = per_walker(z_walk)
        for half in range(2):
            rows = slice(half * HALF, (half + 1) * HALF)
            z = dot(x_s[l, rows, :D], weights[l, :D, :]) + dot(
                x_s[l, rows, D:], weights[l, 3 * D :, :]
            )
            t = jnp.tanh(z + z_wide)
            d_s[l, rows, :] = 1.0 - t * t
            if l == 0:
                x_s[1, rows, :D] = (x_s[0, rows, :D].astype(F32) + t).astype(BF16)


def pair_kernel(after, near, far, sums):
    sums[...] = near[...] + far[...]


def factors_kernel(x_s, d_s, m_s, psi, oth_psi, weights, energies, energy, multiplicity, out, out_0, s_s, w_s):
    mp = lax.axis_index("c")
    own_row = pl.multiple_of(D + D * mp, D)
    oth_row = pl.multiple_of(2 * D - D * mp, D)
    pick = walker_table()
    s_s[1, :HALF, :] = (psi[...].astype(F32) * d_s[1, :HALF, :]).astype(BF16)
    s_s[1, HALF:, :] = (oth_psi[...] * d_s[1, HALF:, :]).astype(BF16)
    q_both = dot(pick, s_s[1])
    q_high, q_low = split(q_both[:WALK] + q_both[WALK:])
    for half in range(2):
        rows = slice(half * HALF, (half + 1) * HALF)
        w_spin = weights[1, pl.ds(own_row if half == 0 else oth_row, D), :]
        spin = (dot_nt(q_high, w_spin) + dot_nt(q_low, w_spin)) * (1.0 / 32.0)
        up = psi[...].astype(F32) if half == 0 else oth_psi[...]
        u = up + dot_nt(s_s[1, rows, :], weights[1, :D, :]) + per_walker(spin)
        s_s[0, rows, :] = (u * d_s[0, rows, :]).astype(BF16)

    l = mp
    mult = multiplicity[0].astype(F32)
    row_scale = mult * (1.0 / 16384.0)
    mean = jnp.sum(energies[...], axis=1, keepdims=True) * (1.0 / WALK)
    shifted = mean + SHIFT
    at_p, at_c, at_low, at_s = D, D + PAIR, 2 * D + PAIR, 3 * D + PAIR
    w_s[:, :at_c] = x_s[l]
    w_s[:, at_s:] = s_s[l]
    step = HALF // WALK
    for w in range(WALK):
        centered = energy[0, w] - mean
        for first in (w * step, HALF + w * step):
            rows = slice(first, first + step)
            high, low = split(centered * w_s[rows, at_s:].astype(F32))
            w_s[rows, at_c:at_low] = high
            w_s[rows, at_low:at_s] = low
    with_h = dot_t(w_s[:, :D], w_s[...])
    with_p = dot_t(w_s[:, at_p:at_c], w_s[:, at_p:])
    with_s = dot_t(w_s[:, at_s:], w_s[:, at_s:])
    totals = dot(pick, w_s[:, at_p:])
    totals = totals[:WALK] + totals[WALK:]
    row, col = square_iotas()

    parity = own_parity()

    def put(slot, value):
        half, place = place_of(slot)
        out[parity ^ half, place * B : (place + 1) * B, :] = value * row_scale

    def put_grad(slot, centered, plain):
        half, place = place_of(slot)
        rows = slice(place * B, (place + 1) * B)
        out[parity ^ half, rows, :] = (centered + shifted * plain) * row_scale
        out_0[parity ^ half, rows, :] = plain * row_scale

    lines = {}

    def put_symmetric(slot, line, full):
        low = full[B:, B:]
        put(slot, jnp.where(col >= row, full[:B, :B], low))
        put(slot + 1, full[:B, B:])
        lines[line] = jnp.sum(jnp.where(col == row, low, 0.0), axis=0, keepdims=True) * row_scale

    put_symmetric(0, 0, with_h[:, :D])
    hp = with_h[:, at_p:at_c]
    put(11, hp[:B])
    put(12, hp[B:])
    put(10, with_p[:, :PAIR])
    hc, hs = with_h[:, at_c:at_low] + with_h[:, at_low:at_s], with_h[:, at_s:]
    pc = with_p[:, PAIR : PAIR + D] + with_p[:, PAIR + D : PAIR + 2 * D]
    ps = with_p[:, PAIR + 2 * D :]
    for j in range(2):
        cols = slice(j * B, (j + 1) * B)
        put_grad(19 + j, hc[:B, cols], hs[:B, cols])
        put_grad(21 + j, hc[B:, cols], hs[B:, cols])
        put_grad(31 + j, pc[:, cols], ps[:, cols])
    put_symmetric(17, 3, with_s)

    means = m_s[l]
    up_first = mp == 0
    up = jnp.where(up_first, means[:WALK].astype(F32), means[WALK:].astype(F32)).astype(BF16)
    down = jnp.where(up_first, means[WALK:].astype(F32), means[:WALK].astype(F32)).astype(BF16)
    both = jnp.concatenate([up, down], 1)
    mm = dot_t(both, both) * 64.0
    put_symmetric(2, 1, mm[:D, :D])
    put_symmetric(4, 2, mm[D:, D:])
    for i in range(2):
        for j in range(2):
            put(6 + 2 * i + j, mm[i * B : (i + 1) * B, D + j * B : D + (j + 1) * B])
    totals = jnp.concatenate(
        [totals[:, :PAIR], totals[:, PAIR : PAIR + D] + totals[:, PAIR + D : PAIR + 2 * D], totals[:, PAIR + 2 * D :]], 1
    )
    t_high, t_low = split(totals)
    side = dot_t(jnp.concatenate([both, both], 0), jnp.concatenate([t_high, t_low], 0))
    for i in range(4):
        rows = slice(i * B, (i + 1) * B)
        put(13 + i, side[rows, :B])
        for j in range(2):
            at = (1 + j) * B
            put_grad(23 + 2 * i + j, side[rows, at : at + B], side[rows, at + D : at + D + B])
    lines[4] = jnp.full((1, B), mult * (1.0 / 16.0), F32)
    last = KEPT - B
    out[parity ^ 1, last:, :] = jnp.zeros((B, B), F32)
    for line, value in lines.items():
        out[parity ^ 1, last + line : last + line + 1, :] = value


def tie_kernel(out, out_0, near, far, to_0, to_1, to_2, to_3, row_sum):
    zh_sum = jnp.sum(near[...] + far[...], axis=1, keepdims=True)
    row_sum[...] = jnp.broadcast_to(zh_sum, (8, B))
    for target, (first, end) in zip((to_0, to_1), OUT_STREAMS):
        target[...] = out[1, first * B : end * B, :]
    for target, (first, end) in zip((to_2, to_3), PLAIN_STREAMS):
        rows = (end - first) * B
        target[:rows, :] = out_0[1, first * B : end * B, :]
        target[rows:, :] = row_sum[...]


def add_kernel(out, out_0, from_0, from_1, from_2, from_3, row_sum, row_two, total):
    energy = row_sum[...] + row_two[...]
    near = [
        part[(end - first) * B :, :] for part, (first, end) in zip((from_2, from_3), PLAIN_STREAMS)
    ]
    energy = energy + (near[0] + near[1])
    shifted = energy[:1, :] * (1.0 / 256.0) + SHIFT
    plain = [None] * GRADS
    for part, (first, end) in zip((from_2, from_3), PLAIN_STREAMS):
        for place in range(first, end):
            plain[place] = part[(place - first) * B : (place - first + 1) * B, :]
    for part, (first, end) in zip((from_0, from_1), OUT_STREAMS):
        for place in range(first, end):
            rows = slice(place * B, (place + 1) * B)
            value = out[0, rows, :] + part[(place - first) * B : (place - first + 1) * B, :]
            if place < GRADS:
                value = value - shifted * (out_0[0, rows, :] + plain[place])
            total[rows, :] = value


def cut_kernel(kept, to_0, to_1, to_2, to_3):
    for target, (first, end) in zip((to_0, to_1, to_2, to_3), BACK_STREAMS):
        target[...] = kept[first * B : end * B, :]


def reader(kept, parts, streams):
    parity = own_parity()

    def read(slot, size=B):
        half, place = place_of(slot)
        for part, (begin, end) in zip(parts, streams):
            if begin <= place < end:
                other = part[(place - begin) * B : (place - begin) * B + size, :]
        own = kept[place * B : place * B + size, :]
        return jnp.where(parity == half, own, other)

    return read


def unpack_kernel(kept, from_1, from_2, from_3, a_out, s_out, done, a_v, s_v, sems):
    row, col = square_iotas()
    read = reader(kept, (from_1, from_2, from_3), BACK_STREAMS[1:])
    lines = read(33, 8)
    inverse = 1.0 / lines[4:5, :]
    copies = []

    def get(slot):
        return read(slot) * inverse

    def symmetric(slot, line):
        tri = get(slot)
        off = get(slot + 1)
        flipped = tri.T
        diag = lines[line : line + 1, :] * inverse
        first = jnp.where(col >= row, tri, flipped)
        second = jnp.where(col < row, tri, flipped)
        second = jnp.where(col == row, jnp.broadcast_to(diag, (B, B)), second)
        return [[first, off], [off.T, second]]

    def place(target, i, j, value):
        target[i * B : (i + 1) * B, j * B : (j + 1) * B] = value

    def send(source, target, first, end):
        rows = slice(first * B, end * B)
        copy = pltpu.make_async_copy(source.at[rows], target.at[rows], sems.at[len(copies)])
        copy.start()
        copies.append(copy)

    ss = symmetric(17, 3)
    for i in range(2):
        for j in range(2):
            place(s_v, i, j, ss[i][j])
    send(s_v, s_out, 0, 2)
    uu = symmetric(2, 1)
    dd = symmetric(4, 2)
    ud = [[get(6 + 2 * i + j) for j in range(2)] for i in range(2)]
    du = [[ud[j][i].T for j in range(2)] for i in range(2)]
    sides = [get(11 + i) for i in range(6)]
    for i in range(2):
        for j in range(2):
            place(a_v, 2 + i, j, (uu[i][j] + ud[i][j]) * 0.5)
            place(a_v, 2 + i, 2 + j, uu[i][j])
            place(a_v, 2 + i, 4 + j, ud[i][j])
        place(a_v, 2 + i, 6, sides[2 + i])
    send(a_v, a_out, 2, 4)
    for i in range(2):
        for j in range(2):
            place(a_v, 4 + i, j, (du[i][j] + dd[i][j]) * 0.5)
            place(a_v, 4 + i, 2 + j, du[i][j])
            place(a_v, 4 + i, 4 + j, dd[i][j])
        place(a_v, 4 + i, 6, sides[4 + i])
    send(a_v, a_out, 4, 6)
    hh = symmetric(0, 0)
    for i in range(2):
        for j in range(2):
            place(a_v, i, j, hh[i][j])
            place(a_v, i, 2 + j, (uu[i][j] + du[i][j]) * 0.5)
            place(a_v, i, 4 + j, (ud[i][j] + dd[i][j]) * 0.5)
        place(a_v, i, 6, sides[i])
    send(a_v, a_out, 0, 2)
    for i in range(6):
        place(a_v, 6, i, sides[i].T)
    place(a_v, 6, 6, get(10))
    send(a_v, a_out, 6, 7)
    for copy in copies:
        copy.wait()
    done[...] = inverse


def natural_kernel(kept, from_0, from_1, a_inverse, s_inverse, natural, curvature):
    get = reader(kept, (from_0, from_1), BACK_STREAMS[:2])

    grad = jnp.concatenate(
        [jnp.concatenate([get(19 + 2 * i), get(20 + 2 * i)], 1) for i in range(7)], 0
    )
    g_high, g_low = split(grad)
    s_high, s_low = split(s_inverse[...])
    half = dot(g_high, s_high) + (dot(g_high, s_low) + dot(g_low, s_high))
    h_high, h_low = split(half)
    total = jnp.zeros((1, D), F32)
    for i in range(7):
        rows = slice(i * B, (i + 1) * B)
        a_high, a_low = split(a_inverse[rows, :])
        part = dot(a_high, h_high) + (dot(a_high, h_low) + dot(a_low, h_high))
        natural[rows, :] = part
        total = total + jnp.sum(part * grad[rows, :], axis=0, keepdims=True)
    curvature[...] = jnp.broadcast_to(jnp.sum(total, axis=1, keepdims=True), (1, B))


def scale_kernel(natural, curvature, other, after, direction):
    total = curvature[:, :1] + other[:, :1]
    direction[...] = natural[...] * lax.rsqrt(total * (1.0 / ENTRIES))


def call(kernel, out_shapes, in_spaces, limit_mib, name, scratch=(), flops=0, moved=0, out_spaces=None):
    return pl.pallas_call(
        kernel,
        out_shape=tuple(jax.ShapeDtypeStruct(shape, dtype) for shape, dtype in out_shapes),
        in_specs=[pl.BlockSpec(memory_space=space) for space in in_spaces],
        out_specs=tuple(pl.BlockSpec(memory_space=space) for space in out_spaces or [V] * len(out_shapes)),
        scratch_shapes=scratch,
        compiler_params=pltpu.CompilerParams(vmem_limit_bytes=limit_mib * 1024 * 1024),
        cost_estimate=pl.CostEstimate(flops=flops, bytes_accessed=moved, transcendentals=0),
        name=name,
    )


V, S = pltpu.VMEM, pltpu.SMEM


def parity_groups():
    groups = {}
    for place in range(256):
        rest, c = divmod(place, 2)
        rest, x = divmod(rest, 4)
        rest, zh = divmod(rest, 4)
        zl, y = divmod(rest, 4)
        groups.setdefault((zh, c, (x + y + zl) % 2), []).append(place)
    return [groups[key] for key in sorted(groups)]


def same_parity(value):
    axes = ("zl", "y", "zh", "x", "c")
    return lax.all_to_all(value, axes, 0, 0, axis_index_groups=parity_groups(), tiled=True)


LOW, HIGH = [(0, 1), (1, 0), (2, 3), (3, 2)], [(1, 2), (2, 1), (3, 0), (0, 3)]


def over_y(part):
    pairs = [(2 * a, 2 * b) for a, b in LOW] + [(2 * a + 1, 2 * b + 1) for a, b in HIGH]
    return lax.ppermute(part, ("y", "c"), pairs)


def over_z(part):
    def index(z, c):
        return (z % 2 * 4 + z // 2) * 2 + c

    pairs = [(index(z, 0), index(z ^ 1, 0)) for z in range(8)]
    pairs += [(index(z, 1), index((z + (1 if z % 2 else -1)) % 8, 1)) for z in range(8)]
    return lax.ppermute(part, ("zl", "zh", "c"), pairs)


def streams_of(streams):
    return [(((end - first) * B, B), F32) for first, end in streams]


def body(features, psi_grad, pair_means, energies, multiplicity, weights, a_inverse, s_inverse):
    feat = features.reshape(HALF, D)
    psi = psi_grad.reshape(HALF, D)
    pair = pair_means.reshape(2, HALF, PAIR)
    swap = [(0, 1), (1, 0)]

    oth_feat = lax.ppermute(feat.astype(F32), "c", swap)
    oth_pair = lax.ppermute(pair.astype(F32), "c", swap)
    far_1 = lax.ppermute(energies, "zh", LOW)
    oth_psi = lax.ppermute(psi.astype(F32), "c", swap)

    x_s, d_s, m_s = call(
        forward_kernel,
        [((2, ROWS, D + PAIR), BF16), ((2, ROWS, D), F32), ((2, 2 * WALK, D), BF16)],
        [V] * 5,
        16,
        "forward",
        flops=1_000_000_000,
        moved=6_000_000,
    )(feat, pair, oth_feat, oth_pair, weights)
    (sum_2,) = call(pair_kernel, [((1, WALK), F32)], [V] * 3, 4, "pair")(m_s, energies, far_1)
    far_2 = lax.ppermute(sum_2, "zh", HIGH)

    grads = GRADS * B
    out, out_0 = call(
        factors_kernel,
        [((2, KEPT, B), F32), ((2, grads, B), F32)],
        [V] * 7 + [S] * 2,
        24,
        "factors",
        scratch=[
            pltpu.VMEM((2, ROWS, D), BF16),
            pltpu.VMEM((ROWS, 4 * D + PAIR), BF16),
        ],
        flops=2_500_000_000,
        moved=8_000_000,
    )(x_s, d_s, m_s, psi, oth_psi, weights, energies, energies, multiplicity)

    sizes = [((end - first) * B + 8, B) for first, end in PLAIN_STREAMS]
    to_0, to_1, to_2, to_3, row_sum = call(
        tie_kernel,
        streams_of(OUT_STREAMS) + [(sizes[0], F32), (sizes[1], F32), ((8, B), F32)],
        [V] * 4,
        8,
        "tie",
        moved=3_000_000,
    )(out, out_0, sum_2, far_2)
    from_0, from_1 = over_y(to_0), over_z(to_1)
    from_2 = lax.ppermute(to_2, "x", LOW)
    from_3 = lax.ppermute(to_3, "x", HIGH)
    row_two = lax.ppermute(row_sum, "x", [(0, 2), (1, 3), (2, 0), (3, 1)])
    (total,) = call(add_kernel, [((KEPT, B), F32)], [V] * 8, 10, "add", moved=3_000_000)(
        out, out_0, from_0, from_1, from_2, from_3, row_sum, row_two
    )
    mine = jnp.sum(same_parity(total).reshape(GROUP, CHUNK, B), axis=0)
    one, two, three = (
        lax.ppermute(mine, "zh", [(i, (i + k) % 4) for i in range(4)]) for k in (1, 2, 3)
    )
    mine = (mine + two) + (one + three)
    kept = same_parity(jnp.broadcast_to(mine[None], (GROUP, CHUNK, B)).reshape(KEPT, B))
    parts = call(cut_kernel, streams_of(BACK_STREAMS), [V], 6, "cut", moved=2_200_000)(kept)
    parts = over_y(parts[0]), over_z(parts[1]), lax.ppermute(parts[2], "x", LOW), lax.ppermute(parts[3], "x", HIGH)

    natural, curvature = call(
        natural_kernel,
        [((DIN, D), F32), ((1, B), F32)],
        [V] * 5,
        18,
        "natural",
        flops=1_500_000_000,
        moved=5_000_000,
    )(kept, *parts[:2], a_inverse[0], s_inverse[0])
    other = lax.ppermute(curvature, "c", swap)
    a_sum, s_sum, done = call(
        unpack_kernel,
        [((DIN, DIN), F32), ((D, D), F32), ((1, B), F32)],
        [V] * 4,
        14,
        "unpack",
        scratch=[pltpu.VMEM((DIN, DIN), F32), pltpu.VMEM((D, D), F32), pltpu.SemaphoreType.DMA((5,))],
        out_spaces=(pl.ANY, pl.ANY, V),
        flops=10_000_000,
        moved=6_000_000,
    )(kept, *parts[1:])
    (direction,) = call(
        scale_kernel, [((DIN, D), F32)], [V] * 4, 6, "scale", flops=1_000_000, moved=2_000_000
    )(natural, curvature, other, done)
    return a_sum[None], s_sum[None], direction[None]


def solution(mesh):
    fine = Mesh(mesh.devices.reshape(2, 4, 4, 4, 2), ("zl", "y", "zh", "x", "c"))
    twist, walker = ("zl", "y"), ("zh", "x")
    return jax.shard_map(
        body,
        mesh=fine,
        in_specs=(
            P(twist, walker, "c", None),
            P(twist, walker, "c", None),
            P(twist, None, walker, "c", None),
            P(twist, walker),
            P(twist),
            P(),
            P("c", None, None),
            P("c", None, None),
        ),
        out_specs=(P("c", None, None),) * 3,
        check_vma=False,
    )
```

```python
import jax
import jax.numpy as jnp
from jax import lax
from jax.experimental import pallas as pl
from jax.experimental.pallas import tpu as pltpu
from jax.sharding import Mesh, PartitionSpec as P

F32, BF16 = jnp.float32, jnp.bfloat16
D, PAIR, DIN = 256, 128, 896
WALK, HALF, ROWS = 16, 512, 1024
B = 128
GROUP = 16
SLOTS = 17
KEPT = SLOTS * B
CHUNK = KEPT // GROUP
GRADS, FACTORS = 7, 10
OUT_STREAMS = ((0, 6), (6, 12), (12, 17))
BACK_STREAMS = ((0, 4), (4, 7), (7, 12), (12, 15), (15, 17))
ENTRIES = 2 * DIN * D
SHIFT = 7.0


def dot_t(a, b):
    return lax.dot_general(a, b, (((0,), (0,)), ((), ())), preferred_element_type=F32)


def dot_nt(a, b):
    return lax.dot_general(a, b, (((1,), (1,)), ((), ())), preferred_element_type=F32)


def dot(a, b):
    return jnp.dot(a, b, preferred_element_type=F32)


def split(a):
    high = a.astype(BF16)
    return high, (a - high.astype(F32)).astype(BF16)


def per_walker(a):
    n = a.shape[1]
    return jnp.broadcast_to(a[:, None, :], (WALK, HALF // WALK, n)).reshape(HALF, n)


def square_iotas():
    return lax.broadcasted_iota(jnp.int32, (B, B), 0), lax.broadcasted_iota(jnp.int32, (B, B), 1)


def own_parity():
    return lax.rem(lax.axis_index("x") + lax.axis_index("y") + lax.axis_index("zl"), 2)


def walker_table():
    group = lax.broadcasted_iota(jnp.int32, (2 * WALK, ROWS), 1) // (HALF // WALK)
    return (group == lax.broadcasted_iota(jnp.int32, (2 * WALK, ROWS), 0)).astype(BF16)


def place_of(slot):
    if 19 <= slot < 33:
        half, place = divmod(slot - 19, GRADS)
        return half, place
    half, place = divmod(slot if slot < 19 else 19, FACTORS)
    return half, place + GRADS


def forward_kernel(feat, pair, oth_feat, oth_pair, weights, x_s, d_s, m_s):
    mp = lax.axis_index("c")
    own_row = pl.multiple_of(D + D * mp, D)
    oth_row = pl.multiple_of(2 * D - D * mp, D)
    x_s[0, :HALF, :D] = feat[...]
    x_s[0, HALF:, :D] = oth_feat[...].astype(BF16)
    for l in range(2):
        x_s[l, :HALF, D:] = pair[l]
        x_s[l, HALF:, D:] = oth_pair[l].astype(BF16)
    pick = walker_table()
    for l in range(2):
        means = (dot(pick, x_s[l, :, :D]) * (1.0 / 32.0)).astype(BF16)
        m_s[l] = means
        z_walk = dot(means[:WALK], weights[l, pl.ds(own_row, D), :]) + dot(
            means[WALK:], weights[l, pl.ds(oth_row, D), :]
        )
        z_wide = per_walker(z_walk)
        for half in range(2):
            rows = slice(half * HALF, (half + 1) * HALF)
            z = dot(x_s[l, rows, :D], weights[l, :D, :]) + dot(
                x_s[l, rows, D:], weights[l, 3 * D :, :]
            )
            t = jnp.tanh(z + z_wide)
            d_s[l, rows, :] = 1.0 - t * t
            if l == 0:
                x_s[1, rows, :D] = (x_s[0, rows, :D].astype(F32) + t).astype(BF16)


def pair_kernel(after, near, far, sums):
    sums[...] = near[...] + far[...]


def factors_kernel(x_s, d_s, m_s, psi, oth_psi, weights, energies, energy, multiplicity, out, out_0, s_s, w_s):
    mp = lax.axis_index("c")
    own_row = pl.multiple_of(D + D * mp, D)
    oth_row = pl.multiple_of(2 * D - D * mp, D)
    pick = walker_table()
    s_s[1, :HALF, :] = (psi[...].astype(F32) * d_s[1, :HALF, :]).astype(BF16)
    s_s[1, HALF:, :] = (oth_psi[...] * d_s[1, HALF:, :]).astype(BF16)
    q_both = dot(pick, s_s[1])
    q_high, q_low = split(q_both[:WALK] + q_both[WALK:])
    for half in range(2):
        rows = slice(half * HALF, (half + 1) * HALF)
        w_spin = weights[1, pl.ds(own_row if half == 0 else oth_row, D), :]
        spin = (dot_nt(q_high, w_spin) + dot_nt(q_low, w_spin)) * (1.0 / 32.0)
        up = psi[...].astype(F32) if half == 0 else oth_psi[...]
        u = up + dot_nt(s_s[1, rows, :], weights[1, :D, :]) + per_walker(spin)
        s_s[0, rows, :] = (u * d_s[0, rows, :]).astype(BF16)

    l = mp
    mult = multiplicity[0].astype(F32)
    row_scale = mult * (1.0 / 16384.0)
    mean = jnp.sum(energies[...], axis=1, keepdims=True) * (1.0 / WALK)
    shifted = mean + SHIFT
    at_p, at_c, at_low, at_s = D, D + PAIR, 2 * D + PAIR, 3 * D + PAIR
    w_s[:, :at_c] = x_s[l]
    w_s[:, at_s:] = s_s[l]
    step = HALF // WALK
    for w in range(WALK):
        centered = energy[0, w] - mean
        for first in (w * step, HALF + w * step):
            rows = slice(first, first + step)
            high, low = split(centered * w_s[rows, at_s:].astype(F32))
            w_s[rows, at_c:at_low] = high
            w_s[rows, at_low:at_s] = low
    with_h = dot_t(w_s[:, :D], w_s[...])
    with_p = dot_t(w_s[:, at_p:at_c], w_s[:, at_p:])
    with_s = dot_t(w_s[:, at_s:], w_s[:, at_s:])
    totals = dot(pick, w_s[:, at_p:])
    totals = totals[:WALK] + totals[WALK:]
    row, col = square_iotas()

    parity = own_parity()

    def put(slot, value):
        half, place = place_of(slot)
        out[parity ^ half, place * B : (place + 1) * B, :] = value * row_scale

    def put_grad(slot, centered, plain):
        half, place = place_of(slot)
        rows = slice(place * B, (place + 1) * B)
        out[parity ^ half, rows, :] = (centered + shifted * plain) * row_scale
        out_0[parity ^ half, rows, :] = plain * row_scale

    lines = {}

    def put_symmetric(slot, line, full):
        low = full[B:, B:]
        put(slot, jnp.where(col >= row, full[:B, :B], low))
        put(slot + 1, full[:B, B:])
        lines[line] = jnp.sum(jnp.where(col == row, low, 0.0), axis=0, keepdims=True) * row_scale

    put_symmetric(0, 0, with_h[:, :D])
    hp = with_h[:, at_p:at_c]
    put(11, hp[:B])
    put(12, hp[B:])
    put(10, with_p[:, :PAIR])
    hc, hs = with_h[:, at_c:at_low] + with_h[:, at_low:at_s], with_h[:, at_s:]
    pc = with_p[:, PAIR : PAIR + D] + with_p[:, PAIR + D : PAIR + 2 * D]
    ps = with_p[:, PAIR + 2 * D :]
    for j in range(2):
        cols = slice(j * B, (j + 1) * B)
        put_grad(19 + j, hc[:B, cols], hs[:B, cols])
        put_grad(21 + j, hc[B:, cols], hs[B:, cols])
        put_grad(31 + j, pc[:, cols], ps[:, cols])
    put_symmetric(17, 3, with_s)

    means = m_s[l]
    up_first = mp == 0
    up = jnp.where(up_first, means[:WALK].astype(F32), means[WALK:].astype(F32)).astype(BF16)
    down = jnp.where(up_first, means[WALK:].astype(F32), means[:WALK].astype(F32)).astype(BF16)
    both = jnp.concatenate([up, down], 1)
    mm = dot_t(both, both) * 64.0
    put_symmetric(2, 1, mm[:D, :D])
    put_symmetric(4, 2, mm[D:, D:])
    for i in range(2):
        for j in range(2):
            put(6 + 2 * i + j, mm[i * B : (i + 1) * B, D + j * B : D + (j + 1) * B])
    totals = jnp.concatenate(
        [totals[:, :PAIR], totals[:, PAIR : PAIR + D] + totals[:, PAIR + D : PAIR + 2 * D], totals[:, PAIR + 2 * D :]], 1
    )
    t_high, t_low = split(totals)
    side = dot_t(jnp.concatenate([both, both], 0), jnp.concatenate([t_high, t_low], 0))
    for i in range(4):
        rows = slice(i * B, (i + 1) * B)
        put(13 + i, side[rows, :B])
        for j in range(2):
            at = (1 + j) * B
            put_grad(23 + 2 * i + j, side[rows, at : at + B], side[rows, at + D : at + D + B])
    lines[4] = jnp.full((1, B), mult * (1.0 / 16.0), F32)
    last = KEPT - B
    out[parity ^ 1, last:, :] = jnp.zeros((B, B), F32)
    for line, value in lines.items():
        out[parity ^ 1, last + line : last + line + 1, :] = value


def tie_kernel(out, out_0, near, far, to_0, to_1, to_2, to_3, row_sum):
    zh_sum = jnp.sum(near[...] + far[...], axis=1, keepdims=True)
    row_sum[...] = jnp.broadcast_to(zh_sum, (8, B))
    grads = GRADS * B
    to_0[:grads, :] = out_0[1]
    to_0[grads:, :] = row_sum[...]
    for target, (first, end) in zip((to_1, to_2, to_3), OUT_STREAMS):
        target[: (end - first) * B, :] = out[1, first * B : end * B, :]
    to_1[OUT_STREAMS[0][1] * B :, :] = row_sum[...]


def add_kernel(out, out_0, from_0, from_1, from_2, from_3, row_sum, row_two, total):
    grads = GRADS * B
    near, far = from_0[grads:, :], from_1[OUT_STREAMS[0][1] * B :, :]
    energy = (row_sum[...] + row_two[...]) + (near + far)
    shifted = energy[:1, :] * (1.0 / 256.0) + SHIFT
    for part, (first, end) in zip((from_1, from_2, from_3), OUT_STREAMS):
        for place in range(first, end):
            rows = slice(place * B, (place + 1) * B)
            value = out[0, rows, :] + part[(place - first) * B : (place - first + 1) * B, :]
            if place < GRADS:
                value = value - shifted * (out_0[0, rows, :] + from_0[rows, :])
            total[rows, :] = value


def cut_kernel(kept, to_0, to_1, to_2, to_3, to_4):
    for target, (first, end) in zip((to_0, to_1, to_2, to_3, to_4), BACK_STREAMS):
        target[...] = kept[first * B : end * B, :]


def reader(kept, parts, streams):
    parity = own_parity()

    def read(slot, size=B):
        half, place = place_of(slot)
        for part, (begin, end) in zip(parts, streams):
            if begin <= place < end:
                other = part[(place - begin) * B : (place - begin) * B + size, :]
        own = kept[place * B : place * B + size, :]
        return jnp.where(parity == half, own, other)

    return read


def finish_kernel(
    kept, from_2, from_3, from_4, natural, curvature, other, a_out, s_out, direction, a_v, s_v, d_v, sems
):
    row, col = square_iotas()
    read = reader(kept, (from_2, from_3, from_4), BACK_STREAMS[2:])
    lines = read(33, 8)
    inverse = 1.0 / lines[4:5, :]
    copies = []

    def get(slot):
        return read(slot) * inverse

    def symmetric(slot, line):
        tri = get(slot)
        off = get(slot + 1)
        flipped = tri.T
        diag = lines[line : line + 1, :] * inverse
        first = jnp.where(col >= row, tri, flipped)
        second = jnp.where(col < row, tri, flipped)
        second = jnp.where(col == row, jnp.broadcast_to(diag, (B, B)), second)
        return [[first, off], [off.T, second]]

    def place(target, i, j, value):
        target[i * B : (i + 1) * B, j * B : (j + 1) * B] = value

    def send(source, target, first, end):
        rows = slice(first * B, end * B)
        copy = pltpu.make_async_copy(source.at[rows], target.at[rows], sems.at[len(copies)])
        copy.start()
        copies.append(copy)

    ss = symmetric(17, 3)
    for i in range(2):
        for j in range(2):
            place(s_v, i, j, ss[i][j])
    send(s_v, s_out, 0, 2)
    uu = symmetric(2, 1)
    dd = symmetric(4, 2)
    ud = [[get(6 + 2 * i + j) for j in range(2)] for i in range(2)]
    du = [[ud[j][i].T for j in range(2)] for i in range(2)]
    sides = [get(11 + i) for i in range(6)]
    for i in range(2):
        for j in range(2):
            place(a_v, 2 + i, j, (uu[i][j] + ud[i][j]) * 0.5)
            place(a_v, 2 + i, 2 + j, uu[i][j])
            place(a_v, 2 + i, 4 + j, ud[i][j])
        place(a_v, 2 + i, 6, sides[2 + i])
    send(a_v, a_out, 2, 4)
    for i in range(2):
        for j in range(2):
            place(a_v, 4 + i, j, (du[i][j] + dd[i][j]) * 0.5)
            place(a_v, 4 + i, 2 + j, du[i][j])
            place(a_v, 4 + i, 4 + j, dd[i][j])
        place(a_v, 4 + i, 6, sides[4 + i])
    send(a_v, a_out, 4, 6)
    hh = symmetric(0, 0)
    for i in range(2):
        for j in range(2):
            place(a_v, i, j, hh[i][j])
            place(a_v, i, 2 + j, (uu[i][j] + du[i][j]) * 0.5)
            place(a_v, i, 4 + j, (ud[i][j] + dd[i][j]) * 0.5)
        place(a_v, i, 6, sides[i])
    send(a_v, a_out, 0, 2)
    for i in range(6):
        place(a_v, 6, i, sides[i].T)
    place(a_v, 6, 6, get(10))
    send(a_v, a_out, 6, 7)
    total = curvature[:, :1] + other[:, :1]
    d_v[...] = natural[...] * lax.rsqrt(total * (1.0 / ENTRIES))
    send(d_v, direction, 0, 7)
    for copy in copies:
        copy.wait()


def natural_kernel(kept, from_0, from_1, a_inverse, s_inverse, natural, curvature):
    get = reader(kept, (from_0, from_1), BACK_STREAMS[:2])

    grad = jnp.concatenate(
        [jnp.concatenate([get(19 + 2 * i), get(20 + 2 * i)], 1) for i in range(7)], 0
    )
    g_high, g_low = split(grad)
    s_high, s_low = split(s_inverse[...])
    half = dot(jnp.concatenate([g_high, g_high, g_low], 1), jnp.concatenate([s_high, s_low, s_high], 0))
    h_high, h_low = split(half)
    h_terms = jnp.concatenate([h_high, h_low, h_high], 0)
    total = jnp.zeros((1, D), F32)
    for i in range(7):
        rows = slice(i * B, (i + 1) * B)
        a_high, a_low = split(a_inverse[rows, :])
        part = dot(jnp.concatenate([a_high, a_high, a_low], 1), h_terms)
        natural[rows, :] = part
        total = total + jnp.sum(part * grad[rows, :], axis=0, keepdims=True)
    curvature[...] = jnp.broadcast_to(jnp.sum(total, axis=1, keepdims=True), (1, B))


def call(kernel, out_shapes, in_spaces, limit_mib, name, scratch=(), flops=0, moved=0, out_spaces=None):
    return pl.pallas_call(
        kernel,
        out_shape=tuple(jax.ShapeDtypeStruct(shape, dtype) for shape, dtype in out_shapes),
        in_specs=[pl.BlockSpec(memory_space=space) for space in in_spaces],
        out_specs=tuple(pl.BlockSpec(memory_space=space) for space in out_spaces or [V] * len(out_shapes)),
        scratch_shapes=scratch,
        compiler_params=pltpu.CompilerParams(vmem_limit_bytes=limit_mib * 1024 * 1024),
        cost_estimate=pl.CostEstimate(flops=flops, bytes_accessed=moved, transcendentals=0),
        name=name,
    )


V, S = pltpu.VMEM, pltpu.SMEM


def parity_groups():
    groups = {}
    for place in range(256):
        rest, c = divmod(place, 2)
        rest, x = divmod(rest, 4)
        rest, zh = divmod(rest, 4)
        zl, y = divmod(rest, 4)
        groups.setdefault((zh, c, (x + y + zl) % 2), []).append(place)
    return [groups[key] for key in sorted(groups)]


def same_parity(value):
    axes = ("zl", "y", "zh", "x", "c")
    return lax.all_to_all(value, axes, 0, 0, axis_index_groups=parity_groups(), tiled=True)


LOW, HIGH = [(0, 1), (1, 0), (2, 3), (3, 2)], [(1, 2), (2, 1), (3, 0), (0, 3)]


def to_neighbours(parts):
    ways = (("x", LOW), ("y", LOW), ("zl", [(0, 1), (1, 0)]), ("x", HIGH), ("y", HIGH))
    return [lax.ppermute(part, axis, pairs) for part, (axis, pairs) in zip(parts, ways)]


def streams_of(streams):
    return [(((end - first) * B, B), F32) for first, end in streams]


def body(features, psi_grad, pair_means, energies, multiplicity, weights, a_inverse, s_inverse):
    feat = features.reshape(HALF, D)
    psi = psi_grad.reshape(HALF, D)
    pair = pair_means.reshape(2, HALF, PAIR)
    swap = [(0, 1), (1, 0)]

    oth_feat = lax.ppermute(feat.astype(F32), "c", swap)
    oth_pair = lax.ppermute(pair.astype(F32), "c", swap)
    far_1 = lax.ppermute(energies, "zh", LOW)
    oth_psi = lax.ppermute(psi.astype(F32), "c", swap)

    x_s, d_s, m_s = call(
        forward_kernel,
        [((2, ROWS, D + PAIR), BF16), ((2, ROWS, D), F32), ((2, 2 * WALK, D), BF16)],
        [V] * 5,
        16,
        "forward",
        flops=1_000_000_000,
        moved=6_000_000,
    )(feat, pair, oth_feat, oth_pair, weights)
    (sum_2,) = call(pair_kernel, [((1, WALK), F32)], [V] * 3, 4, "pair")(m_s, energies, far_1)
    far_2 = lax.ppermute(sum_2, "zh", HIGH)

    grads = GRADS * B
    out, out_0 = call(
        factors_kernel,
        [((2, KEPT, B), F32), ((2, grads, B), F32)],
        [V] * 7 + [S] * 2,
        24,
        "factors",
        scratch=[
            pltpu.VMEM((2, ROWS, D), BF16),
            pltpu.VMEM((ROWS, 4 * D + PAIR), BF16),
        ],
        flops=2_500_000_000,
        moved=8_000_000,
    )(x_s, d_s, m_s, psi, oth_psi, weights, energies, energies, multiplicity)

    sizes = [((end - first) * B, B) for first, end in OUT_STREAMS]
    to_0, to_1, to_2, to_3, row_sum = call(
        tie_kernel,
        [((grads + 8, B), F32), ((sizes[0][0] + 8, B), F32), (sizes[1], F32), (sizes[2], F32), ((8, B), F32)],
        [V] * 4,
        8,
        "tie",
        moved=3_000_000,
    )(out, out_0, sum_2, far_2)
    from_0 = lax.ppermute(to_0, "x", LOW)
    from_1 = lax.ppermute(to_1, "x", HIGH)
    from_2 = lax.ppermute(to_2, "y", LOW)
    from_3 = lax.ppermute(to_3, "zl", swap)
    row_two = lax.ppermute(row_sum, "x", [(0, 2), (1, 3), (2, 0), (3, 1)])
    (total,) = call(add_kernel, [((KEPT, B), F32)], [V] * 8, 10, "add", moved=3_000_000)(
        out, out_0, from_0, from_1, from_2, from_3, row_sum, row_two
    )
    mine = jnp.sum(same_parity(total).reshape(GROUP, CHUNK, B), axis=0)
    one, two, three = (
        lax.ppermute(mine, "zh", [(i, (i + k) % 4) for i in range(4)]) for k in (1, 2, 3)
    )
    mine = (mine + two) + (one + three)
    kept = same_parity(jnp.broadcast_to(mine[None], (GROUP, CHUNK, B)).reshape(KEPT, B))
    parts = call(cut_kernel, streams_of(BACK_STREAMS), [V], 6, "cut", moved=2_200_000)(kept)
    parts = to_neighbours(parts)

    natural, curvature = call(
        natural_kernel,
        [((DIN, D), F32), ((1, B), F32)],
        [V] * 5,
        18,
        "natural",
        flops=1_500_000_000,
        moved=5_000_000,
    )(kept, *parts[:2], a_inverse[0], s_inverse[0])
    other = lax.ppermute(curvature, "c", swap)
    a_sum, s_sum, direction = call(
        finish_kernel,
        [((DIN, DIN), F32), ((D, D), F32), ((DIN, D), F32)],
        [V] * 7,
        16,
        "finish",
        scratch=[
            pltpu.VMEM((DIN, DIN), F32),
            pltpu.VMEM((D, D), F32),
            pltpu.VMEM((DIN, D), F32),
            pltpu.SemaphoreType.DMA((6,)),
        ],
        out_spaces=(pl.ANY,) * 3,
        flops=10_000_000,
        moved=7_000_000,
    )(kept, *parts[2:], natural, curvature, other)
    return a_sum[None], s_sum[None], direction[None]


def solution(mesh):
    fine = Mesh(mesh.devices.reshape(2, 4, 4, 4, 2), ("zl", "y", "zh", "x", "c"))
    twist, walker = ("zl", "y"), ("zh", "x")
    return jax.shard_map(
        body,
        mesh=fine,
        in_specs=(
            P(twist, walker, "c", None),
            P(twist, walker, "c", None),
            P(twist, None, walker, "c", None),
            P(twist, walker),
            P(twist),
            P(),
            P("c", None, None),
            P("c", None, None),
        ),
        out_specs=(P("c", None, None),) * 3,
        check_vma=False,
    )
```

```python
import jax
import jax.numpy as jnp
from jax import lax
from jax.experimental import pallas as pl
from jax.experimental.pallas import tpu as pltpu
from jax.sharding import Mesh, PartitionSpec as P

F32, BF16 = jnp.float32, jnp.bfloat16
D, PAIR, DIN = 256, 128, 896
WALK, HALF, ROWS = 16, 512, 1024
B = 128
GROUP = 16
SLOTS = 17
KEPT = SLOTS * B
CHUNK = KEPT // GROUP
HALVES = (
    (19, 20, 21, 23, 24, 25, 26, 0, 1, 10, 11, 2, 3, 6, 7, 13, 14),
    (22, 31, 32, 27, 28, 29, 30, 12, 17, 18, 33, 4, 5, 8, 9, 15, 16),
)
GRADS, FACTORS = 3, 4
DIRECT = (0, 1, 2, 7, 8, 9, 10)
BACK_STREAMS = ((0, 4), (4, 7), (7, 12), (12, 15), (15, 17))
ENTRIES = 2 * DIN * D
SHIFT = 7.0


def dot_t(a, b):
    return lax.dot_general(a, b, (((0,), (0,)), ((), ())), preferred_element_type=F32)


def dot_nt(a, b):
    return lax.dot_general(a, b, (((1,), (1,)), ((), ())), preferred_element_type=F32)


def dot(a, b):
    return jnp.dot(a, b, preferred_element_type=F32)


def split(a):
    high = a.astype(BF16)
    return high, (a - high.astype(F32)).astype(BF16)


def per_walker(a):
    n = a.shape[1]
    return jnp.broadcast_to(a[:, None, :], (WALK, HALF // WALK, n)).reshape(HALF, n)


def square_iotas():
    return lax.broadcasted_iota(jnp.int32, (B, B), 0), lax.broadcasted_iota(jnp.int32, (B, B), 1)


def own_parity():
    return lax.rem(lax.axis_index("x") + lax.axis_index("y") + lax.axis_index("zl"), 2)


def walker_table():
    group = lax.broadcasted_iota(jnp.int32, (2 * WALK, ROWS), 1) // (HALF // WALK)
    return (group == lax.broadcasted_iota(jnp.int32, (2 * WALK, ROWS), 0)).astype(BF16)


def place_of(slot):
    half = 0 if slot in HALVES[0] else 1
    return half, HALVES[half].index(slot)


def forward_kernel(feat, pair, oth_feat, oth_pair, weights, x_s, d_s, m_s):
    mp = lax.axis_index("c")
    own_row = pl.multiple_of(D + D * mp, D)
    oth_row = pl.multiple_of(2 * D - D * mp, D)
    x_s[0, :HALF, :D] = feat[...]
    x_s[0, HALF:, :D] = oth_feat[...].astype(BF16)
    for l in range(2):
        x_s[l, :HALF, D:] = pair[l]
        x_s[l, HALF:, D:] = oth_pair[l].astype(BF16)
    pick = walker_table()
    for l in range(2):
        means = (dot(pick, x_s[l, :, :D]) * (1.0 / 32.0)).astype(BF16)
        m_s[l] = means
        z_walk = dot(means[:WALK], weights[l, pl.ds(own_row, D), :]) + dot(
            means[WALK:], weights[l, pl.ds(oth_row, D), :]
        )
        z_wide = per_walker(z_walk)
        for half in range(2):
            rows = slice(half * HALF, (half + 1) * HALF)
            z = dot(x_s[l, rows, :D], weights[l, :D, :]) + dot(
                x_s[l, rows, D:], weights[l, 3 * D :, :]
            )
            t = jnp.tanh(z + z_wide)
            d_s[l, rows, :] = 1.0 - t * t
            if l == 0:
                x_s[1, rows, :D] = (x_s[0, rows, :D].astype(F32) + t).astype(BF16)


def pair_kernel(after, near, far, sums):
    sums[...] = near[...] + far[...]


def factors_kernel(x_s, d_s, m_s, psi, oth_psi, weights, energies, energy, multiplicity, out, out_0, fac, s_s, w_s):
    mp = lax.axis_index("c")
    own_row = pl.multiple_of(D + D * mp, D)
    oth_row = pl.multiple_of(2 * D - D * mp, D)
    pick = walker_table()
    s_s[1, :HALF, :] = (psi[...].astype(F32) * d_s[1, :HALF, :]).astype(BF16)
    s_s[1, HALF:, :] = (oth_psi[...] * d_s[1, HALF:, :]).astype(BF16)
    q_both = dot(pick, s_s[1])
    q_high, q_low = split(q_both[:WALK] + q_both[WALK:])
    for half in range(2):
        rows = slice(half * HALF, (half + 1) * HALF)
        w_spin = weights[1, pl.ds(own_row if half == 0 else oth_row, D), :]
        spin = (dot_nt(q_high, w_spin) + dot_nt(q_low, w_spin)) * (1.0 / 32.0)
        up = psi[...].astype(F32) if half == 0 else oth_psi[...]
        u = up + dot_nt(s_s[1, rows, :], weights[1, :D, :]) + per_walker(spin)
        s_s[0, rows, :] = (u * d_s[0, rows, :]).astype(BF16)

    l = mp
    mult = multiplicity[0].astype(F32)
    row_scale = mult * (1.0 / 16384.0)
    mean = jnp.sum(energies[...], axis=1, keepdims=True) * (1.0 / WALK)
    shifted = mean + SHIFT
    at_p, at_c, at_low, at_s = D, D + PAIR, 2 * D + PAIR, 3 * D + PAIR
    w_s[:, :at_c] = x_s[l]
    w_s[:, at_s:] = s_s[l]
    step = HALF // WALK
    for w in range(WALK):
        centered = energy[0, w] - mean
        for first in (w * step, HALF + w * step):
            rows = slice(first, first + step)
            high, low = split(centered * w_s[rows, at_s:].astype(F32))
            w_s[rows, at_c:at_low] = high
            w_s[rows, at_low:at_s] = low
    with_h = dot_t(w_s[:, :D], w_s[...])
    with_p = dot_t(w_s[:, at_p:at_c], w_s[:, at_p:])
    with_s = dot_t(w_s[:, at_s:], w_s[:, at_s:])
    p_sum, s_sum = dot(pick, w_s[:, at_p:at_c]), dot(pick, w_s[:, at_s:])
    row, col = square_iotas()

    parity = own_parity()

    def put(slot, value):
        half, place = place_of(slot)
        first = DIRECT.index(place) * B
        out[parity ^ half, first : first + B, :] = value * row_scale

    def put_grad(slot, centered, plain):
        half, place = place_of(slot)
        rows = slice(place * B, (place + 1) * B)
        out[parity ^ half, rows, :] = (centered + shifted * plain) * row_scale
        out_0[parity ^ half, rows, :] = plain * row_scale

    lines = {}

    def put_symmetric(slot, line, full):
        low = full[B:, B:]
        put(slot, jnp.where(col >= row, full[:B, :B], low))
        put(slot + 1, full[:B, B:])
        lines[line] = jnp.sum(jnp.where(col == row, low, 0.0), axis=0, keepdims=True) * row_scale

    put_symmetric(0, 0, with_h[:, :D])
    hp = with_h[:, at_p:at_c]
    put(11, hp[:B])
    put(12, hp[B:])
    put(10, with_p[:, :PAIR])
    hc, hs = with_h[:, at_c:at_low] + with_h[:, at_low:at_s], with_h[:, at_s:]
    pc = with_p[:, PAIR : PAIR + D] + with_p[:, PAIR + D : PAIR + 2 * D]
    ps = with_p[:, PAIR + 2 * D :]
    for j in range(2):
        cols = slice(j * B, (j + 1) * B)
        put_grad(19 + j, hc[:B, cols], hs[:B, cols])
        put_grad(21 + j, hc[B:, cols], hs[B:, cols])
        put_grad(31 + j, pc[:, cols], ps[:, cols])
    put_symmetric(17, 3, with_s)

    means = m_s[l].astype(F32)
    up_first = mp == 0
    up = jnp.where(up_first, means[:WALK], means[WALK:])
    down = jnp.where(up_first, means[WALK:], means[:WALK])
    p_sum, s_sum = p_sum[:WALK] + p_sum[WALK:], s_sum[:WALK] + s_sum[WALK:]
    for j, value in enumerate(
        (up[:, :B], up[:, B:], down[:, :B], down[:, B:], p_sum, s_sum[:, :B], s_sum[:, B:])
    ):
        fac[j * WALK : (j + 1) * WALK, :] = value
    for w in range(WALK):
        fac[7 * WALK + w : 7 * WALK + w + 1, :] = jnp.full((1, B), energy[0, w], F32)

    lines[4] = jnp.full((1, B), mult * (1.0 / 16.0), F32)
    half, place = place_of(33)
    first = DIRECT.index(place) * B
    out[parity ^ half, first : first + B, :] = jnp.zeros((B, B), F32)
    for line, value in lines.items():
        out[parity ^ half, first + line : first + line + 1, :] = value


def tie_kernel(out, out_0, fac, near, far, to_0, to_1, to_2, row_sum):
    zh_sum = jnp.sum(near[...] + far[...], axis=1, keepdims=True)
    row_sum[...] = jnp.broadcast_to(zh_sum, (8, B))
    grads = GRADS * B
    to_0[:B, :] = fac[...]
    to_0[B : B + grads, :] = out_0[1]
    to_0[B + grads :, :] = row_sum[...]
    to_1[:grads, :] = out[1, :grads, :]
    to_1[grads:, :] = row_sum[...]
    to_2[...] = out[1, grads:, :]


def add_kernel(out, out_0, fac, from_0, from_1, from_2, row_sum, row_two, multiplicity, total):
    parity = own_parity()
    grads = GRADS * B
    energy = (row_sum[...] + row_two[...]) + (from_0[B + grads :, :] + from_1[grads:, :])
    mean = energy[:1, :] * (1.0 / 256.0)
    plain = out_0[0] + from_0[B : B + grads, :]
    total[:grads, :] = (out[0, :grads, :] + from_1[:grads, :]) - (mean + SHIFT) * plain
    first = DIRECT[GRADS] * B
    total[first : first + FACTORS * B, :] = out[0, grads:, :] + from_2[...]

    def part(j):
        rows = slice(j * WALK, (j + 1) * WALK)
        return jnp.concatenate([fac[rows, :], from_0[rows, :]], 0)

    row_scale = multiplicity[0].astype(F32) * (1.0 / 16384.0)
    both = jnp.concatenate([part(j) for j in range(4)], 1).astype(BF16)
    centered = part(7) - mean
    sums = jnp.concatenate([part(4), part(5) * centered, part(6) * centered], 1)
    high, low = split(sums)
    side = dot_t(jnp.concatenate([both, both], 0), jnp.concatenate([high, low], 0)) * row_scale
    mm = dot_t(both, both) * (64.0 * row_scale)
    row, col = square_iotas()
    blocks, lines = {}, {}
    for slot, line, full in ((2, 1, mm[:D, :D]), (4, 2, mm[D:, D:])):
        last = full[B:, B:]
        blocks[slot] = jnp.where(col >= row, full[:B, :B], last)
        blocks[slot + 1] = full[:B, B:]
        lines[line] = jnp.sum(jnp.where(col == row, last, 0.0), axis=0, keepdims=True)
    for i in range(2):
        for j in range(2):
            blocks[6 + 2 * i + j] = mm[i * B : (i + 1) * B, D + j * B : D + (j + 1) * B]
    for i in range(4):
        rows = slice(i * B, (i + 1) * B)
        blocks[13 + i] = side[rows, :B]
        for j in range(2):
            blocks[23 + 2 * i + j] = side[rows, (1 + j) * B : (2 + j) * B]

    for half in range(2):

        @pl.when(parity == half)
        def _():
            for slot, value in blocks.items():
                if place_of(slot)[0] == half:
                    place = place_of(slot)[1]
                    total[place * B : (place + 1) * B, :] = value
            if half == place_of(33)[0]:
                base = place_of(33)[1] * B
                for line, value in lines.items():
                    total[base + line : base + line + 1, :] = value


def cut_kernel(kept, to_0, to_1, to_2, to_3, to_4):
    for target, (first, end) in zip((to_0, to_1, to_2, to_3, to_4), BACK_STREAMS):
        target[...] = kept[first * B : end * B, :]


def reader(kept, parts, streams):
    parity = own_parity()

    def read(slot, size=B):
        half, place = place_of(slot)
        for part, (begin, end) in zip(parts, streams):
            if begin <= place < end:
                other = part[(place - begin) * B : (place - begin) * B + size, :]
        own = kept[place * B : place * B + size, :]
        return jnp.where(parity == half, own, other)

    return read


def finish_kernel(
    kept, from_2, from_3, from_4, natural, curvature, other, a_out, s_out, direction, a_v, s_v, d_v, sems
):
    row, col = square_iotas()
    read = reader(kept, (from_2, from_3, from_4), BACK_STREAMS[2:])
    lines = read(33, 8)
    inverse = 1.0 / lines[4:5, :]
    copies = []

    def get(slot):
        return read(slot) * inverse

    def symmetric(slot, line):
        tri = get(slot)
        off = get(slot + 1)
        flipped = tri.T
        diag = lines[line : line + 1, :] * inverse
        first = jnp.where(col >= row, tri, flipped)
        second = jnp.where(col < row, tri, flipped)
        second = jnp.where(col == row, jnp.broadcast_to(diag, (B, B)), second)
        return [[first, off], [off.T, second]]

    def place(target, i, j, value):
        target[i * B : (i + 1) * B, j * B : (j + 1) * B] = value

    def send(source, target, first, end):
        rows = slice(first * B, end * B)
        copy = pltpu.make_async_copy(source.at[rows], target.at[rows], sems.at[len(copies)])
        copy.start()
        copies.append(copy)

    ss = symmetric(17, 3)
    for i in range(2):
        for j in range(2):
            place(s_v, i, j, ss[i][j])
    send(s_v, s_out, 0, 2)
    uu = symmetric(2, 1)
    dd = symmetric(4, 2)
    ud = [[get(6 + 2 * i + j) for j in range(2)] for i in range(2)]
    du = [[ud[j][i].T for j in range(2)] for i in range(2)]
    sides = [get(11 + i) for i in range(6)]
    for i in range(2):
        for j in range(2):
            place(a_v, 2 + i, j, (uu[i][j] + ud[i][j]) * 0.5)
            place(a_v, 2 + i, 2 + j, uu[i][j])
            place(a_v, 2 + i, 4 + j, ud[i][j])
        place(a_v, 2 + i, 6, sides[2 + i])
    send(a_v, a_out, 2, 4)
    for i in range(2):
        for j in range(2):
            place(a_v, 4 + i, j, (du[i][j] + dd[i][j]) * 0.5)
            place(a_v, 4 + i, 2 + j, du[i][j])
            place(a_v, 4 + i, 4 + j, dd[i][j])
        place(a_v, 4 + i, 6, sides[4 + i])
    send(a_v, a_out, 4, 6)
    hh = symmetric(0, 0)
    for i in range(2):
        for j in range(2):
            place(a_v, i, j, hh[i][j])
            place(a_v, i, 2 + j, (uu[i][j] + du[i][j]) * 0.5)
            place(a_v, i, 4 + j, (ud[i][j] + dd[i][j]) * 0.5)
        place(a_v, i, 6, sides[i])
    send(a_v, a_out, 0, 2)
    for i in range(6):
        place(a_v, 6, i, sides[i].T)
    place(a_v, 6, 6, get(10))
    send(a_v, a_out, 6, 7)
    total = curvature[:, :1] + other[:, :1]
    d_v[...] = natural[...] * lax.rsqrt(total * (1.0 / ENTRIES))
    send(d_v, direction, 0, 7)
    for copy in copies:
        copy.wait()


def natural_kernel(kept, from_0, from_1, a_inverse, s_inverse, natural, curvature):
    get = reader(kept, (from_0, from_1), BACK_STREAMS[:2])

    grad = jnp.concatenate(
        [jnp.concatenate([get(19 + 2 * i), get(20 + 2 * i)], 1) for i in range(7)], 0
    )
    g_high, g_low = split(grad)
    s_high, s_low = split(s_inverse[...])
    half = dot(jnp.concatenate([g_high, g_high, g_low], 1), jnp.concatenate([s_high, s_low, s_high], 0))
    h_high, h_low = split(half)
    h_terms = jnp.concatenate([h_high, h_low, h_high], 0)
    total = jnp.zeros((1, D), F32)
    for i in range(7):
        rows = slice(i * B, (i + 1) * B)
        a_high, a_low = split(a_inverse[rows, :])
        part = dot(jnp.concatenate([a_high, a_high, a_low], 1), h_terms)
        natural[rows, :] = part
        total = total + jnp.sum(part * grad[rows, :], axis=0, keepdims=True)
    curvature[...] = jnp.broadcast_to(jnp.sum(total, axis=1, keepdims=True), (1, B))


def call(kernel, out_shapes, in_spaces, limit_mib, name, scratch=(), flops=0, moved=0, out_spaces=None):
    return pl.pallas_call(
        kernel,
        out_shape=tuple(jax.ShapeDtypeStruct(shape, dtype) for shape, dtype in out_shapes),
        in_specs=[pl.BlockSpec(memory_space=space) for space in in_spaces],
        out_specs=tuple(pl.BlockSpec(memory_space=space) for space in out_spaces or [V] * len(out_shapes)),
        scratch_shapes=scratch,
        compiler_params=pltpu.CompilerParams(vmem_limit_bytes=limit_mib * 1024 * 1024),
        cost_estimate=pl.CostEstimate(flops=flops, bytes_accessed=moved, transcendentals=0),
        name=name,
    )


V, S = pltpu.VMEM, pltpu.SMEM


def parity_groups():
    groups = {}
    for place in range(256):
        rest, c = divmod(place, 2)
        rest, x = divmod(rest, 4)
        rest, zh = divmod(rest, 4)
        zl, y = divmod(rest, 4)
        groups.setdefault((zh, c, (x + y + zl) % 2), []).append(place)
    return [groups[key] for key in sorted(groups)]


def same_parity(value):
    axes = ("zl", "y", "zh", "x", "c")
    return lax.all_to_all(value, axes, 0, 0, axis_index_groups=parity_groups(), tiled=True)


LOW, HIGH = [(0, 1), (1, 0), (2, 3), (3, 2)], [(1, 2), (2, 1), (3, 0), (0, 3)]


def to_neighbours(parts):
    ways = (("x", LOW), ("y", LOW), ("zl", [(0, 1), (1, 0)]), ("x", HIGH), ("y", HIGH))
    return [lax.ppermute(part, axis, pairs) for part, (axis, pairs) in zip(parts, ways)]


def streams_of(streams):
    return [(((end - first) * B, B), F32) for first, end in streams]


def body(features, psi_grad, pair_means, energies, multiplicity, weights, a_inverse, s_inverse):
    feat = features.reshape(HALF, D)
    psi = psi_grad.reshape(HALF, D)
    pair = pair_means.reshape(2, HALF, PAIR)
    swap = [(0, 1), (1, 0)]

    oth_feat = lax.ppermute(feat.astype(F32), "c", swap)
    oth_pair = lax.ppermute(pair.astype(F32), "c", swap)
    far_1 = lax.ppermute(energies, "zh", LOW)
    oth_psi = lax.ppermute(psi.astype(F32), "c", swap)

    x_s, d_s, m_s = call(
        forward_kernel,
        [((2, ROWS, D + PAIR), BF16), ((2, ROWS, D), F32), ((2, 2 * WALK, D), BF16)],
        [V] * 5,
        16,
        "forward",
        flops=1_000_000_000,
        moved=6_000_000,
    )(feat, pair, oth_feat, oth_pair, weights)
    (sum_2,) = call(pair_kernel, [((1, WALK), F32)], [V] * 3, 4, "pair")(m_s, energies, far_1)
    far_2 = lax.ppermute(sum_2, "zh", HIGH)

    grads = GRADS * B
    out, out_0, fac = call(
        factors_kernel,
        [((2, len(DIRECT) * B, B), F32), ((2, grads, B), F32), ((B, B), F32)],
        [V] * 7 + [S] * 2,
        24,
        "factors",
        scratch=[
            pltpu.VMEM((2, ROWS, D), BF16),
            pltpu.VMEM((ROWS, 4 * D + PAIR), BF16),
        ],
        flops=2_500_000_000,
        moved=8_000_000,
    )(x_s, d_s, m_s, psi, oth_psi, weights, energies, energies, multiplicity)

    to_0, to_1, to_2, row_sum = call(
        tie_kernel,
        [((B + grads + 8, B), F32), ((grads + 8, B), F32), ((FACTORS * B, B), F32), ((8, B), F32)],
        [V] * 5,
        6,
        "tie",
        moved=2_000_000,
    )(out, out_0, fac, sum_2, far_2)
    from_0 = lax.ppermute(to_0, "x", LOW)
    from_2 = lax.ppermute(to_2, "y", LOW)
    from_1 = lax.ppermute(to_1, "x", HIGH)
    row_two = lax.ppermute(row_sum, "x", [(0, 2), (1, 3), (2, 0), (3, 1)])
    (total,) = call(
        add_kernel, [((KEPT, B), F32)], [V] * 8 + [S], 12, "add", flops=50_000_000, moved=3_000_000
    )(out, out_0, fac, from_0, from_1, from_2, row_sum, row_two, multiplicity)
    mine = jnp.sum(same_parity(total).reshape(GROUP, CHUNK, B), axis=0)
    one, two, three = (
        lax.ppermute(mine, "zh", [(i, (i + k) % 4) for i in range(4)]) for k in (1, 2, 3)
    )
    mine = (mine + two) + (one + three)
    kept = same_parity(jnp.broadcast_to(mine[None], (GROUP, CHUNK, B)).reshape(KEPT, B))
    parts = call(cut_kernel, streams_of(BACK_STREAMS), [V], 6, "cut", moved=2_200_000)(kept)
    parts = to_neighbours(parts)

    natural, curvature = call(
        natural_kernel,
        [((DIN, D), F32), ((1, B), F32)],
        [V] * 5,
        18,
        "natural",
        flops=1_500_000_000,
        moved=5_000_000,
    )(kept, *parts[:2], a_inverse[0], s_inverse[0])
    other = lax.ppermute(curvature, "c", swap)
    a_sum, s_sum, direction = call(
        finish_kernel,
        [((DIN, DIN), F32), ((D, D), F32), ((DIN, D), F32)],
        [V] * 7,
        16,
        "finish",
        scratch=[
            pltpu.VMEM((DIN, DIN), F32),
            pltpu.VMEM((D, D), F32),
            pltpu.VMEM((DIN, D), F32),
            pltpu.SemaphoreType.DMA((6,)),
        ],
        out_spaces=(pl.ANY,) * 3,
        flops=10_000_000,
        moved=7_000_000,
    )(kept, *parts[2:], natural, curvature, other)
    return a_sum[None], s_sum[None], direction[None]


def solution(mesh):
    fine = Mesh(mesh.devices.reshape(2, 4, 4, 4, 2), ("zl", "y", "zh", "x", "c"))
    twist, walker = ("zl", "y"), ("zh", "x")
    return jax.shard_map(
        body,
        mesh=fine,
        in_specs=(
            P(twist, walker, "c", None),
            P(twist, walker, "c", None),
            P(twist, None, walker, "c", None),
            P(twist, walker),
            P(twist),
            P(),
            P("c", None, None),
            P("c", None, None),
        ),
        out_specs=(P("c", None, None),) * 3,
        check_vma=False,
    )
```

```python
import jax
import jax.numpy as jnp
from jax import lax
from jax.experimental import pallas as pl
from jax.experimental.pallas import tpu as pltpu
from jax.sharding import Mesh, PartitionSpec as P

F32, BF16 = jnp.float32, jnp.bfloat16
D, PAIR, DIN = 256, 128, 896
WALK, HALF, ROWS = 16, 512, 1024
B = 128
GROUP = 16
SLOTS = 17
KEPT = SLOTS * B
CHUNK = KEPT // GROUP
HALVES = (
    (19, 20, 21, 23, 24, 25, 26, 0, 1, 10, 11, 2, 3, 6, 7, 13, 14),
    (22, 31, 32, 27, 28, 29, 30, 12, 17, 18, 33, 4, 5, 8, 9, 15, 16),
)
GRADS, FACTORS = 3, 4
DIRECT = (0, 1, 2, 7, 8, 9, 10)
BACK_STREAMS = ((0, 4), (4, 7), (7, 12), (12, 15), (15, 17))
ENTRIES = 2 * DIN * D
SHIFT = 7.0


def dot_t(a, b):
    return lax.dot_general(a, b, (((0,), (0,)), ((), ())), preferred_element_type=F32)


def dot_nt(a, b):
    return lax.dot_general(a, b, (((1,), (1,)), ((), ())), preferred_element_type=F32)


def dot(a, b):
    return jnp.dot(a, b, preferred_element_type=F32)


def split(a):
    high = a.astype(BF16)
    return high, (a - high.astype(F32)).astype(BF16)


def per_walker(a):
    n = a.shape[1]
    return jnp.broadcast_to(a[:, None, :], (WALK, HALF // WALK, n)).reshape(HALF, n)


def square_iotas():
    return lax.broadcasted_iota(jnp.int32, (B, B), 0), lax.broadcasted_iota(jnp.int32, (B, B), 1)


def own_parity():
    return lax.rem(lax.axis_index("x") + lax.axis_index("y") + lax.axis_index("zl"), 2)


def walker_table():
    group = lax.broadcasted_iota(jnp.int32, (2 * WALK, ROWS), 1) // (HALF // WALK)
    return (group == lax.broadcasted_iota(jnp.int32, (2 * WALK, ROWS), 0)).astype(BF16)


def place_of(slot):
    half = 0 if slot in HALVES[0] else 1
    return half, HALVES[half].index(slot)


def forward_kernel(feat, pair, oth_feat, oth_pair, weights, x_s, d_s, m_s):
    mp = lax.axis_index("c")
    own_row = pl.multiple_of(D + D * mp, D)
    oth_row = pl.multiple_of(2 * D - D * mp, D)
    x_s[0, :HALF, :D] = feat[...]
    x_s[0, HALF:, :D] = oth_feat[...].astype(BF16)
    for l in range(2):
        x_s[l, :HALF, D:] = pair[l]
        x_s[l, HALF:, D:] = oth_pair[l].astype(BF16)
    pick = walker_table()
    for l in range(2):
        means = (dot(pick, x_s[l, :, :D]) * (1.0 / 32.0)).astype(BF16)
        m_s[l] = means
        z_walk = dot(means[:WALK], weights[l, pl.ds(own_row, D), :]) + dot(
            means[WALK:], weights[l, pl.ds(oth_row, D), :]
        )
        z_wide = per_walker(z_walk)
        for half in range(2):
            rows = slice(half * HALF, (half + 1) * HALF)
            z = dot(x_s[l, rows, :D], weights[l, :D, :]) + dot(
                x_s[l, rows, D:], weights[l, 3 * D :, :]
            )
            t = jnp.tanh(z + z_wide)
            d_s[l, rows, :] = 1.0 - t * t
            if l == 0:
                x_s[1, rows, :D] = (x_s[0, rows, :D].astype(F32) + t).astype(BF16)


def pair_kernel(after, near, far, sums):
    sums[...] = near[...] + far[...]


def factors_kernel(x_s, d_s, m_s, psi, oth_psi, weights, energies, energy, multiplicity, out, out_0, fac, s_s, w_s):
    mp = lax.axis_index("c")
    own_row = pl.multiple_of(D + D * mp, D)
    oth_row = pl.multiple_of(2 * D - D * mp, D)
    pick = walker_table()
    s_s[1, :HALF, :] = (psi[...].astype(F32) * d_s[1, :HALF, :]).astype(BF16)
    s_s[1, HALF:, :] = (oth_psi[...] * d_s[1, HALF:, :]).astype(BF16)
    q_both = dot(pick, s_s[1])
    q_high, q_low = split(q_both[:WALK] + q_both[WALK:])
    for half in range(2):
        rows = slice(half * HALF, (half + 1) * HALF)
        w_spin = weights[1, pl.ds(own_row if half == 0 else oth_row, D), :]
        spin = (dot_nt(q_high, w_spin) + dot_nt(q_low, w_spin)) * (1.0 / 32.0)
        up = psi[...].astype(F32) if half == 0 else oth_psi[...]
        u = up + dot_nt(s_s[1, rows, :], weights[1, :D, :]) + per_walker(spin)
        s_s[0, rows, :] = (u * d_s[0, rows, :]).astype(BF16)

    l = mp
    mult = multiplicity[0].astype(F32)
    row_scale = mult * (1.0 / 16384.0)
    mean = jnp.sum(energies[...], axis=1, keepdims=True) * (1.0 / WALK)
    shifted = mean + SHIFT
    at_p, at_c, at_low, at_s = D, D + PAIR, 2 * D + PAIR, 3 * D + PAIR
    w_s[:, :at_c] = x_s[l]
    w_s[:, at_s:] = s_s[l]
    step = HALF // WALK
    for w in range(WALK):
        centered = energy[0, w] - mean
        for first in (w * step, HALF + w * step):
            rows = slice(first, first + step)
            high, low = split(centered * w_s[rows, at_s:].astype(F32))
            w_s[rows, at_c:at_low] = high
            w_s[rows, at_low:at_s] = low
    with_h = dot_t(w_s[:, :D], w_s[...])
    with_p = dot_t(w_s[:, at_p:at_c], w_s[:, at_p:])
    with_s = dot_t(w_s[:, at_s:], w_s[:, at_s:])
    p_sum, s_sum = dot(pick, w_s[:, at_p:at_c]), dot(pick, w_s[:, at_s:])
    row, col = square_iotas()

    parity = own_parity()

    def put(slot, value):
        half, place = place_of(slot)
        first = DIRECT.index(place) * B
        out[parity ^ half, first : first + B, :] = value * row_scale

    def put_grad(slot, centered, plain):
        half, place = place_of(slot)
        rows = slice(place * B, (place + 1) * B)
        out[parity ^ half, rows, :] = (centered + shifted * plain) * row_scale
        out_0[parity ^ half, rows, :] = plain * row_scale

    lines = {}

    def put_symmetric(slot, line, full):
        low = full[B:, B:]
        put(slot, jnp.where(col >= row, full[:B, :B], low))
        put(slot + 1, full[:B, B:])
        lines[line] = jnp.sum(jnp.where(col == row, low, 0.0), axis=0, keepdims=True) * row_scale

    put_symmetric(0, 0, with_h[:, :D])
    hp = with_h[:, at_p:at_c]
    put(11, hp[:B])
    put(12, hp[B:])
    put(10, with_p[:, :PAIR])
    hc, hs = with_h[:, at_c:at_low] + with_h[:, at_low:at_s], with_h[:, at_s:]
    pc = with_p[:, PAIR : PAIR + D] + with_p[:, PAIR + D : PAIR + 2 * D]
    ps = with_p[:, PAIR + 2 * D :]
    for j in range(2):
        cols = slice(j * B, (j + 1) * B)
        put_grad(19 + j, hc[:B, cols], hs[:B, cols])
        put_grad(21 + j, hc[B:, cols], hs[B:, cols])
        put_grad(31 + j, pc[:, cols], ps[:, cols])
    put_symmetric(17, 3, with_s)

    means = m_s[l].astype(F32)
    up_first = mp == 0
    up = jnp.where(up_first, means[:WALK], means[WALK:])
    down = jnp.where(up_first, means[WALK:], means[:WALK])
    p_sum, s_sum = p_sum[:WALK] + p_sum[WALK:], s_sum[:WALK] + s_sum[WALK:]
    for j, value in enumerate(
        (up[:, :B], up[:, B:], down[:, :B], down[:, B:], p_sum, s_sum[:, :B], s_sum[:, B:])
    ):
        fac[j * WALK : (j + 1) * WALK, :] = value
    for w in range(WALK):
        fac[7 * WALK + w : 7 * WALK + w + 1, :] = jnp.full((1, B), energy[0, w], F32)

    lines[4] = jnp.full((1, B), mult * (1.0 / 16.0), F32)
    half, place = place_of(33)
    first = DIRECT.index(place) * B
    out[parity ^ half, first : first + B, :] = jnp.zeros((B, B), F32)
    for line, value in lines.items():
        out[parity ^ half, first + line : first + line + 1, :] = value


def tie_kernel(out, out_0, fac, near, far, to_0, to_1, to_2, row_sum):
    zh_sum = jnp.sum(near[...] + far[...], axis=1, keepdims=True)
    row_sum[...] = jnp.broadcast_to(zh_sum, (8, B))
    grads = GRADS * B
    to_0[:B, :] = fac[...]
    to_0[B : B + grads, :] = out_0[1]
    to_0[B + grads :, :] = row_sum[...]
    to_1[:grads, :] = out[1, :grads, :]
    to_1[grads:, :] = row_sum[...]
    to_2[...] = out[1, grads:, :]


def add_kernel(out, out_0, fac, from_0, from_1, from_2, row_sum, row_two, multiplicity, total):
    parity = own_parity()
    grads = GRADS * B
    energy = (row_sum[...] + row_two[...]) + (from_0[B + grads :, :] + from_1[grads:, :])
    mean = energy[:1, :] * (1.0 / 256.0)
    plain = out_0[0] + from_0[B : B + grads, :]
    total[:grads, :] = (out[0, :grads, :] + from_1[:grads, :]) - (mean + SHIFT) * plain
    first = DIRECT[GRADS] * B
    total[first : first + FACTORS * B, :] = out[0, grads:, :] + from_2[...]

    def part(j):
        rows = slice(j * WALK, (j + 1) * WALK)
        return jnp.concatenate([fac[rows, :], from_0[rows, :]], 0)

    row_scale = multiplicity[0].astype(F32) * (1.0 / 16384.0)
    both = jnp.concatenate([part(j) for j in range(4)], 1).astype(BF16)
    centered = part(7) - mean
    sums = jnp.concatenate([part(4), part(5) * centered, part(6) * centered], 1)
    high, low = split(sums)
    side = dot_t(jnp.concatenate([both, both], 0), jnp.concatenate([high, low], 0)) * row_scale
    mm = dot_t(both, both) * (64.0 * row_scale)
    row, col = square_iotas()
    blocks, lines = {}, {}
    for slot, line, full in ((2, 1, mm[:D, :D]), (4, 2, mm[D:, D:])):
        last = full[B:, B:]
        blocks[slot] = jnp.where(col >= row, full[:B, :B], last)
        blocks[slot + 1] = full[:B, B:]
        lines[line] = jnp.sum(jnp.where(col == row, last, 0.0), axis=0, keepdims=True)
    for i in range(2):
        for j in range(2):
            blocks[6 + 2 * i + j] = mm[i * B : (i + 1) * B, D + j * B : D + (j + 1) * B]
    for i in range(4):
        rows = slice(i * B, (i + 1) * B)
        blocks[13 + i] = side[rows, :B]
        for j in range(2):
            blocks[23 + 2 * i + j] = side[rows, (1 + j) * B : (2 + j) * B]

    for half in range(2):

        @pl.when(parity == half)
        def _():
            for slot, value in blocks.items():
                if place_of(slot)[0] == half:
                    place = place_of(slot)[1]
                    total[place * B : (place + 1) * B, :] = value
            if half == place_of(33)[0]:
                base = place_of(33)[1] * B
                for line, value in lines.items():
                    total[base + line : base + line + 1, :] = value


def cut_kernel(kept, to_0, to_1, to_2, to_3, to_4):
    for target, (first, end) in zip((to_0, to_1, to_2, to_3, to_4), BACK_STREAMS):
        target[...] = kept[first * B : end * B, :]


def reader(kept, parts, streams):
    parity = own_parity()

    def read(slot, size=B):
        half, place = place_of(slot)
        for part, (begin, end) in zip(parts, streams):
            if begin <= place < end:
                other = part[(place - begin) * B : (place - begin) * B + size, :]
        own = kept[place * B : place * B + size, :]
        return jnp.where(parity == half, own, other)

    return read


def finish_kernel(
    kept, from_2, from_3, from_4, natural, curvature, other, a_out, s_out, direction, a_v, s_v, d_v, sems
):
    row, col = square_iotas()
    read = reader(kept, (from_2, from_3, from_4), BACK_STREAMS[2:])
    lines = read(33, 8)
    inverse = 1.0 / lines[4:5, :]
    copies = []

    def get(slot):
        return read(slot) * inverse

    def symmetric(slot, line):
        tri = get(slot)
        off = get(slot + 1)
        flipped = tri.T
        diag = lines[line : line + 1, :] * inverse
        first = jnp.where(col >= row, tri, flipped)
        second = jnp.where(col < row, tri, flipped)
        second = jnp.where(col == row, jnp.broadcast_to(diag, (B, B)), second)
        return [[first, off], [off.T, second]]

    def place(target, i, j, value):
        target[i * B : (i + 1) * B, j * B : (j + 1) * B] = value

    def send(source, target, first, end):
        rows = slice(first * B, end * B)
        copy = pltpu.make_async_copy(source.at[rows], target.at[rows], sems.at[len(copies)])
        copy.start()
        copies.append(copy)

    ss = symmetric(17, 3)
    for i in range(2):
        for j in range(2):
            place(s_v, i, j, ss[i][j])
    send(s_v, s_out, 0, 2)
    uu = symmetric(2, 1)
    dd = symmetric(4, 2)
    ud = [[get(6 + 2 * i + j) for j in range(2)] for i in range(2)]
    du = [[ud[j][i].T for j in range(2)] for i in range(2)]
    sides = [get(11 + i) for i in range(6)]
    for i in range(2):
        for j in range(2):
            place(a_v, 2 + i, j, (uu[i][j] + ud[i][j]) * 0.5)
            place(a_v, 2 + i, 2 + j, uu[i][j])
            place(a_v, 2 + i, 4 + j, ud[i][j])
        place(a_v, 2 + i, 6, sides[2 + i])
    send(a_v, a_out, 2, 4)
    for i in range(2):
        for j in range(2):
            place(a_v, 4 + i, j, (du[i][j] + dd[i][j]) * 0.5)
            place(a_v, 4 + i, 2 + j, du[i][j])
            place(a_v, 4 + i, 4 + j, dd[i][j])
        place(a_v, 4 + i, 6, sides[4 + i])
    send(a_v, a_out, 4, 6)
    hh = symmetric(0, 0)
    for i in range(2):
        for j in range(2):
            place(a_v, i, j, hh[i][j])
            place(a_v, i, 2 + j, (uu[i][j] + du[i][j]) * 0.5)
            place(a_v, i, 4 + j, (ud[i][j] + dd[i][j]) * 0.5)
        place(a_v, i, 6, sides[i])
    send(a_v, a_out, 0, 2)
    for i in range(6):
        place(a_v, 6, i, sides[i].T)
    place(a_v, 6, 6, get(10))
    send(a_v, a_out, 6, 7)
    total = curvature[:, :1] + other[:, :1]
    d_v[...] = natural[...] * lax.rsqrt(total * (1.0 / ENTRIES))
    send(d_v, direction, 0, 7)
    for copy in copies:
        copy.wait()


def natural_kernel(kept, from_0, from_1, a_inverse, s_inverse, natural, curvature):
    get = reader(kept, (from_0, from_1), BACK_STREAMS[:2])

    grad = jnp.concatenate(
        [jnp.concatenate([get(19 + 2 * i), get(20 + 2 * i)], 1) for i in range(7)], 0
    )
    g_high, g_low = split(grad)
    s_high, s_low = split(s_inverse[...])
    half = dot(jnp.concatenate([g_high, g_high, g_low], 1), jnp.concatenate([s_high, s_low, s_high], 0))
    h_high, h_low = split(half)
    h_terms = jnp.concatenate([h_high, h_low, h_high], 0)
    total = jnp.zeros((1, D), F32)
    for i in range(7):
        rows = slice(i * B, (i + 1) * B)
        a_high, a_low = split(a_inverse[rows, :])
        part = dot(jnp.concatenate([a_high, a_high, a_low], 1), h_terms)
        natural[rows, :] = part
        total = total + jnp.sum(part * grad[rows, :], axis=0, keepdims=True)
    curvature[...] = jnp.broadcast_to(jnp.sum(total, axis=1, keepdims=True), (1, B))


def call(kernel, out_shapes, in_spaces, limit_mib, name, scratch=(), flops=0, moved=0, out_spaces=None):
    return pl.pallas_call(
        kernel,
        out_shape=tuple(jax.ShapeDtypeStruct(shape, dtype) for shape, dtype in out_shapes),
        in_specs=[pl.BlockSpec(memory_space=space) for space in in_spaces],
        out_specs=tuple(pl.BlockSpec(memory_space=space) for space in out_spaces or [V] * len(out_shapes)),
        scratch_shapes=scratch,
        compiler_params=pltpu.CompilerParams(vmem_limit_bytes=limit_mib * 1024 * 1024),
        cost_estimate=pl.CostEstimate(flops=flops, bytes_accessed=moved, transcendentals=0),
        name=name,
    )


V, S = pltpu.VMEM, pltpu.SMEM


def parity_groups():
    groups = {}
    for place in range(256):
        rest, c = divmod(place, 2)
        rest, x = divmod(rest, 4)
        rest, zh = divmod(rest, 4)
        zl, y = divmod(rest, 4)
        groups.setdefault((zh, c, (x + y + zl) % 2), []).append(place)
    return [groups[key] for key in sorted(groups)]


def same_parity(value):
    axes = ("zl", "y", "zh", "x", "c")
    return lax.all_to_all(value, axes, 0, 0, axis_index_groups=parity_groups(), tiled=True)


LOW, HIGH = [(0, 1), (1, 0), (2, 3), (3, 2)], [(1, 2), (2, 1), (3, 0), (0, 3)]


def to_neighbours(parts):
    ways = (("x", LOW), ("y", LOW), ("zl", [(0, 1), (1, 0)]), ("x", HIGH), ("y", HIGH))
    return [lax.ppermute(part, axis, pairs) for part, (axis, pairs) in zip(parts, ways)]


def streams_of(streams):
    return [(((end - first) * B, B), F32) for first, end in streams]


def body(features, psi_grad, pair_means, energies, multiplicity, weights, a_inverse, s_inverse):
    feat = features.reshape(HALF, D)
    psi = psi_grad.reshape(HALF, D)
    pair = pair_means.reshape(2, HALF, PAIR)
    swap = [(0, 1), (1, 0)]

    oth_feat = lax.ppermute(feat.astype(F32), "c", swap)
    oth_pair = lax.ppermute(pair.astype(F32), "c", swap)
    far_1 = lax.ppermute(energies, "zh", LOW)
    oth_psi = lax.ppermute(psi.astype(F32), "c", swap)

    x_s, d_s, m_s = call(
        forward_kernel,
        [((2, ROWS, D + PAIR), BF16), ((2, ROWS, D), F32), ((2, 2 * WALK, D), BF16)],
        [V] * 5,
        16,
        "forward",
        flops=1_000_000_000,
        moved=6_000_000,
    )(feat, pair, oth_feat, oth_pair, weights)
    (sum_2,) = call(pair_kernel, [((1, WALK), F32)], [V] * 3, 4, "pair")(m_s, energies, far_1)
    far_2 = lax.ppermute(sum_2, "zh", HIGH)

    grads = GRADS * B
    out, out_0, fac = call(
        factors_kernel,
        [((2, len(DIRECT) * B, B), F32), ((2, grads, B), F32), ((B, B), F32)],
        [V] * 7 + [S] * 2,
        24,
        "factors",
        scratch=[
            pltpu.VMEM((2, ROWS, D), BF16),
            pltpu.VMEM((ROWS, 4 * D + PAIR), BF16),
        ],
        flops=2_500_000_000,
        moved=8_000_000,
    )(x_s, d_s, m_s, psi, oth_psi, weights, energies, energies, multiplicity)

    to_0, to_1, to_2, row_sum = call(
        tie_kernel,
        [((B + grads + 8, B), F32), ((grads + 8, B), F32), ((FACTORS * B, B), F32), ((8, B), F32)],
        [V] * 5,
        6,
        "tie",
        moved=2_000_000,
    )(out, out_0, fac, sum_2, far_2)
    from_0 = lax.ppermute(to_0, "x", LOW)
    from_2 = lax.ppermute(to_2, "y", LOW)
    from_1 = lax.ppermute(to_1, "x", HIGH)
    row_two = lax.ppermute(row_sum, "x", [(0, 2), (1, 3), (2, 0), (3, 1)])
    (total,) = call(
        add_kernel, [((KEPT, B), F32)], [V] * 8 + [S], 12, "add", flops=50_000_000, moved=3_000_000
    )(out, out_0, fac, from_0, from_1, from_2, row_sum, row_two, multiplicity)
    mine = jnp.sum(same_parity(total).reshape(GROUP, CHUNK, B), axis=0)
    one, two, three = (
        lax.ppermute(mine, "zh", [(i, (i + k) % 4) for i in range(4)]) for k in (1, 2, 3)
    )
    mine = (one + three) + (mine + two)
    kept = same_parity(jnp.broadcast_to(mine[None], (GROUP, CHUNK, B)).reshape(KEPT, B))
    parts = call(cut_kernel, streams_of(BACK_STREAMS), [V], 6, "cut", moved=2_200_000)(kept)
    parts = to_neighbours(parts)

    natural, curvature = call(
        natural_kernel,
        [((DIN, D), F32), ((1, B), F32)],
        [V] * 5,
        18,
        "natural",
        flops=1_500_000_000,
        moved=5_000_000,
    )(kept, *parts[:2], a_inverse[0], s_inverse[0])
    other = lax.ppermute(curvature, "c", swap)
    a_sum, s_sum, direction = call(
        finish_kernel,
        [((DIN, DIN), F32), ((D, D), F32), ((DIN, D), F32)],
        [V] * 7,
        16,
        "finish",
        scratch=[
            pltpu.VMEM((DIN, DIN), F32),
            pltpu.VMEM((D, D), F32),
            pltpu.VMEM((DIN, D), F32),
            pltpu.SemaphoreType.DMA((6,)),
        ],
        out_spaces=(pl.ANY,) * 3,
        flops=10_000_000,
        moved=7_000_000,
    )(kept, *parts[2:], natural, curvature, other)
    return a_sum[None], s_sum[None], direction[None]


def solution(mesh):
    fine = Mesh(mesh.devices.reshape(2, 4, 4, 4, 2), ("zl", "y", "zh", "x", "c"))
    twist, walker = ("zl", "y"), ("zh", "x")
    return jax.shard_map(
        body,
        mesh=fine,
        in_specs=(
            P(twist, walker, "c", None),
            P(twist, walker, "c", None),
            P(twist, None, walker, "c", None),
            P(twist, walker),
            P(twist),
            P(),
            P("c", None, None),
            P("c", None, None),
        ),
        out_specs=(P("c", None, None),) * 3,
        check_vma=False,
    )
```

```python
import jax
import jax.numpy as jnp
from jax import lax
from jax.experimental import pallas as pl
from jax.experimental.pallas import tpu as pltpu
from jax.sharding import Mesh, PartitionSpec as P

F32, BF16 = jnp.float32, jnp.bfloat16
D, PAIR, DIN = 256, 128, 896
WALK, HALF, ROWS = 16, 512, 1024
B = 128
GROUP = 16
SLOTS = 17
KEPT = SLOTS * B
CHUNK = KEPT // GROUP
HALVES = (
    (19, 20, 21, 23, 24, 25, 26, 0, 1, 10, 11, 2, 3, 6, 7, 13, 14),
    (22, 31, 32, 27, 28, 29, 30, 12, 17, 18, 33, 4, 5, 8, 9, 15, 16),
)
GRADS, FACTORS = 3, 4
DIRECT = (0, 1, 2, 7, 8, 9, 10)
BACK_STREAMS = ((0, 4), (4, 7), (7, 12), (12, 15), (15, 17))
ENTRIES = 2 * DIN * D
SHIFT = 7.0


def dot_t(a, b):
    return lax.dot_general(a, b, (((0,), (0,)), ((), ())), preferred_element_type=F32)


def dot_nt(a, b):
    return lax.dot_general(a, b, (((1,), (1,)), ((), ())), preferred_element_type=F32)


def dot(a, b):
    return jnp.dot(a, b, preferred_element_type=F32)


def split(a):
    high = a.astype(BF16)
    return high, (a - high.astype(F32)).astype(BF16)


def per_walker(a):
    n = a.shape[1]
    return jnp.broadcast_to(a[:, None, :], (WALK, HALF // WALK, n)).reshape(HALF, n)


def square_iotas():
    return lax.broadcasted_iota(jnp.int32, (B, B), 0), lax.broadcasted_iota(jnp.int32, (B, B), 1)


def own_parity():
    return lax.rem(lax.axis_index("x") + lax.axis_index("y") + lax.axis_index("zl"), 2)


def walker_table():
    group = lax.broadcasted_iota(jnp.int32, (2 * WALK, ROWS), 1) // (HALF // WALK)
    return (group == lax.broadcasted_iota(jnp.int32, (2 * WALK, ROWS), 0)).astype(BF16)


def place_of(slot):
    half = 0 if slot in HALVES[0] else 1
    return half, HALVES[half].index(slot)


def forward_kernel(feat, pair, oth_feat, oth_pair, weights, x_s, d_s, m_s):
    mp = lax.axis_index("c")
    own_row = pl.multiple_of(D + D * mp, D)
    oth_row = pl.multiple_of(2 * D - D * mp, D)
    x_s[0, :HALF, :D] = feat[...]
    x_s[0, HALF:, :D] = oth_feat[...].astype(BF16)
    for l in range(2):
        x_s[l, :HALF, D:] = pair[l]
        x_s[l, HALF:, D:] = oth_pair[l].astype(BF16)
    pick = walker_table()
    for l in range(2):
        means = (dot(pick, x_s[l, :, :D]) * (1.0 / 32.0)).astype(BF16)
        m_s[l] = means
        z_walk = dot(means[:WALK], weights[l, pl.ds(own_row, D), :]) + dot(
            means[WALK:], weights[l, pl.ds(oth_row, D), :]
        )
        z_wide = per_walker(z_walk)
        for half in range(2):
            rows = slice(half * HALF, (half + 1) * HALF)
            z = dot(x_s[l, rows, :D], weights[l, :D, :]) + dot(
                x_s[l, rows, D:], weights[l, 3 * D :, :]
            )
            t = jnp.tanh(z + z_wide)
            d_s[l, rows, :] = 1.0 - t * t
            if l == 0:
                x_s[1, rows, :D] = (x_s[0, rows, :D].astype(F32) + t).astype(BF16)


def pair_kernel(after, near, far, sums):
    sums[...] = near[...] + far[...]


def factors_kernel(x_s, d_s, m_s, psi, oth_psi, weights, energies, energy, multiplicity, out, out_0, fac, s_s, w_s):
    mp = lax.axis_index("c")
    own_row = pl.multiple_of(D + D * mp, D)
    oth_row = pl.multiple_of(2 * D - D * mp, D)
    pick = walker_table()
    s_s[1, :HALF, :] = (psi[...].astype(F32) * d_s[1, :HALF, :]).astype(BF16)
    s_s[1, HALF:, :] = (oth_psi[...] * d_s[1, HALF:, :]).astype(BF16)
    q_both = dot(pick, s_s[1])
    q_high, q_low = split(q_both[:WALK] + q_both[WALK:])
    for half in range(2):
        rows = slice(half * HALF, (half + 1) * HALF)
        w_spin = weights[1, pl.ds(own_row if half == 0 else oth_row, D), :]
        spin = (dot_nt(q_high, w_spin) + dot_nt(q_low, w_spin)) * (1.0 / 32.0)
        up = psi[...].astype(F32) if half == 0 else oth_psi[...]
        u = up + dot_nt(s_s[1, rows, :], weights[1, :D, :]) + per_walker(spin)
        s_s[0, rows, :] = (u * d_s[0, rows, :]).astype(BF16)

    l = mp
    mult = multiplicity[0].astype(F32)
    row_scale = mult * (1.0 / 16384.0)
    mean = jnp.sum(energies[...], axis=1, keepdims=True) * (1.0 / WALK)
    shifted = mean + SHIFT
    at_p, at_c, at_low, at_s = D, D + PAIR, 2 * D + PAIR, 3 * D + PAIR
    w_s[:, :at_c] = x_s[l]
    w_s[:, at_s:] = s_s[l]
    step = HALF // WALK
    for w in range(WALK):
        centered = energy[0, w] - mean
        for first in (w * step, HALF + w * step):
            rows = slice(first, first + step)
            high, low = split(centered * w_s[rows, at_s:].astype(F32))
            w_s[rows, at_c:at_low] = high
            w_s[rows, at_low:at_s] = low
    with_h = dot_t(w_s[:, :D], w_s[...])
    with_p = dot_t(w_s[:, at_p:at_c], w_s[:, at_p:])
    with_s = dot_t(w_s[:, at_s:], w_s[:, at_s:])
    p_sum, s_sum = dot(pick, w_s[:, at_p:at_c]), dot(pick, w_s[:, at_s:])
    row, col = square_iotas()

    parity = own_parity()

    def put(slot, value):
        half, place = place_of(slot)
        first = DIRECT.index(place) * B
        out[parity ^ half, first : first + B, :] = value * row_scale

    def put_grad(slot, centered, plain):
        half, place = place_of(slot)
        rows = slice(place * B, (place + 1) * B)
        out[parity ^ half, rows, :] = (centered + shifted * plain) * row_scale
        out_0[parity ^ half, rows, :] = plain * row_scale

    lines = {}

    def put_symmetric(slot, line, full):
        low = full[B:, B:]
        put(slot, jnp.where(col >= row, full[:B, :B], low))
        put(slot + 1, full[:B, B:])
        lines[line] = jnp.sum(jnp.where(col == row, low, 0.0), axis=0, keepdims=True) * row_scale

    put_symmetric(0, 0, with_h[:, :D])
    hp = with_h[:, at_p:at_c]
    put(11, hp[:B])
    put(12, hp[B:])
    put(10, with_p[:, :PAIR])
    hc, hs = with_h[:, at_c:at_low] + with_h[:, at_low:at_s], with_h[:, at_s:]
    pc = with_p[:, PAIR : PAIR + D] + with_p[:, PAIR + D : PAIR + 2 * D]
    ps = with_p[:, PAIR + 2 * D :]
    for j in range(2):
        cols = slice(j * B, (j + 1) * B)
        put_grad(19 + j, hc[:B, cols], hs[:B, cols])
        put_grad(21 + j, hc[B:, cols], hs[B:, cols])
        put_grad(31 + j, pc[:, cols], ps[:, cols])
    put_symmetric(17, 3, with_s)

    means = m_s[l].astype(F32)
    up_first = mp == 0
    up = jnp.where(up_first, means[:WALK], means[WALK:])
    down = jnp.where(up_first, means[WALK:], means[:WALK])
    p_sum, s_sum = p_sum[:WALK] + p_sum[WALK:], s_sum[:WALK] + s_sum[WALK:]
    for j, value in enumerate(
        (up[:, :B], up[:, B:], down[:, :B], down[:, B:], p_sum, s_sum[:, :B], s_sum[:, B:])
    ):
        fac[j * WALK : (j + 1) * WALK, :] = value
    for w in range(WALK):
        fac[7 * WALK + w : 7 * WALK + w + 1, :] = jnp.full((1, B), energy[0, w], F32)

    lines[4] = jnp.full((1, B), mult * (1.0 / 16.0), F32)
    half, place = place_of(33)
    first = DIRECT.index(place) * B
    out[parity ^ half, first : first + B, :] = jnp.zeros((B, B), F32)
    for line, value in lines.items():
        out[parity ^ half, first + line : first + line + 1, :] = value


def tie_kernel(out, out_0, fac, near, far, to_0, to_1, to_2, row_sum):
    zh_sum = jnp.sum(near[...] + far[...], axis=1, keepdims=True)
    row_sum[...] = jnp.broadcast_to(zh_sum, (8, B))
    grads = GRADS * B
    to_0[:B, :] = fac[...]
    to_0[B : 2 * B, :] = out_0[1, :B, :]
    to_0[2 * B :, :] = row_sum[...]
    to_1[: grads - B, :] = out_0[1, B:, :]
    to_1[grads - B :, :] = row_sum[...]
    to_2[...] = out[1]


def add_kernel(out, out_0, fac, from_0, from_1, from_2, row_sum, row_two, multiplicity, total):
    parity = own_parity()
    grads = GRADS * B
    energy = (row_sum[...] + row_two[...]) + (from_0[2 * B :, :] + from_1[grads - B :, :])
    mean = energy[:1, :] * (1.0 / 256.0)
    plain = out_0[0] + jnp.concatenate([from_0[B : 2 * B, :], from_1[: grads - B, :]], 0)
    total[:grads, :] = (out[0, :grads, :] + from_2[:grads, :]) - (mean + SHIFT) * plain
    first = DIRECT[GRADS] * B
    total[first : first + FACTORS * B, :] = out[0, grads:, :] + from_2[grads:, :]

    def part(j):
        rows = slice(j * WALK, (j + 1) * WALK)
        return jnp.concatenate([fac[rows, :], from_0[rows, :]], 0)

    row_scale = multiplicity[0].astype(F32) * (1.0 / 16384.0)
    both = jnp.concatenate([part(j) for j in range(4)], 1).astype(BF16)
    centered = part(7) - mean
    sums = jnp.concatenate([part(4), part(5) * centered, part(6) * centered], 1)
    high, low = split(sums)
    side = dot_t(jnp.concatenate([both, both], 0), jnp.concatenate([high, low], 0)) * row_scale
    mm = dot_t(both, both) * (64.0 * row_scale)
    row, col = square_iotas()
    blocks, lines = {}, {}
    for slot, line, full in ((2, 1, mm[:D, :D]), (4, 2, mm[D:, D:])):
        last = full[B:, B:]
        blocks[slot] = jnp.where(col >= row, full[:B, :B], last)
        blocks[slot + 1] = full[:B, B:]
        lines[line] = jnp.sum(jnp.where(col == row, last, 0.0), axis=0, keepdims=True)
    for i in range(2):
        for j in range(2):
            blocks[6 + 2 * i + j] = mm[i * B : (i + 1) * B, D + j * B : D + (j + 1) * B]
    for i in range(4):
        rows = slice(i * B, (i + 1) * B)
        blocks[13 + i] = side[rows, :B]
        for j in range(2):
            blocks[23 + 2 * i + j] = side[rows, (1 + j) * B : (2 + j) * B]

    for half in range(2):

        @pl.when(parity == half)
        def _():
            for slot, value in blocks.items():
                if place_of(slot)[0] == half:
                    place = place_of(slot)[1]
                    total[place * B : (place + 1) * B, :] = value
            if half == place_of(33)[0]:
                base = place_of(33)[1] * B
                for line, value in lines.items():
                    total[base + line : base + line + 1, :] = value


def cut_kernel(kept, to_0, to_1, to_2, to_3, to_4):
    for target, (first, end) in zip((to_0, to_1, to_2, to_3, to_4), BACK_STREAMS):
        target[...] = kept[first * B : end * B, :]


def reader(kept, parts, streams):
    parity = own_parity()

    def read(slot, size=B):
        half, place = place_of(slot)
        for part, (begin, end) in zip(parts, streams):
            if begin <= place < end:
                other = part[(place - begin) * B : (place - begin) * B + size, :]
        own = kept[place * B : place * B + size, :]
        return jnp.where(parity == half, own, other)

    return read


def finish_kernel(
    kept, from_2, from_3, from_4, natural, curvature, other, a_out, s_out, direction, a_v, s_v, d_v, sems
):
    row, col = square_iotas()
    read = reader(kept, (from_2, from_3, from_4), BACK_STREAMS[2:])
    lines = read(33, 8)
    inverse = 1.0 / lines[4:5, :]
    copies = []

    def get(slot):
        return read(slot) * inverse

    def symmetric(slot, line):
        tri = get(slot)
        off = get(slot + 1)
        flipped = tri.T
        diag = lines[line : line + 1, :] * inverse
        first = jnp.where(col >= row, tri, flipped)
        second = jnp.where(col < row, tri, flipped)
        second = jnp.where(col == row, jnp.broadcast_to(diag, (B, B)), second)
        return [[first, off], [off.T, second]]

    def place(target, i, j, value):
        target[i * B : (i + 1) * B, j * B : (j + 1) * B] = value

    def send(source, target, first, end):
        rows = slice(first * B, end * B)
        copy = pltpu.make_async_copy(source.at[rows], target.at[rows], sems.at[len(copies)])
        copy.start()
        copies.append(copy)

    ss = symmetric(17, 3)
    for i in range(2):
        for j in range(2):
            place(s_v, i, j, ss[i][j])
    send(s_v, s_out, 0, 2)
    uu = symmetric(2, 1)
    dd = symmetric(4, 2)
    ud = [[get(6 + 2 * i + j) for j in range(2)] for i in range(2)]
    du = [[ud[j][i].T for j in range(2)] for i in range(2)]
    sides = [get(11 + i) for i in range(6)]
    for i in range(2):
        for j in range(2):
            place(a_v, 2 + i, j, (uu[i][j] + ud[i][j]) * 0.5)
            place(a_v, 2 + i, 2 + j, uu[i][j])
            place(a_v, 2 + i, 4 + j, ud[i][j])
        place(a_v, 2 + i, 6, sides[2 + i])
    send(a_v, a_out, 2, 4)
    for i in range(2):
        for j in range(2):
            place(a_v, 4 + i, j, (du[i][j] + dd[i][j]) * 0.5)
            place(a_v, 4 + i, 2 + j, du[i][j])
            place(a_v, 4 + i, 4 + j, dd[i][j])
        place(a_v, 4 + i, 6, sides[4 + i])
    send(a_v, a_out, 4, 6)
    hh = symmetric(0, 0)
    for i in range(2):
        for j in range(2):
            place(a_v, i, j, hh[i][j])
            place(a_v, i, 2 + j, (uu[i][j] + du[i][j]) * 0.5)
            place(a_v, i, 4 + j, (ud[i][j] + dd[i][j]) * 0.5)
        place(a_v, i, 6, sides[i])
    send(a_v, a_out, 0, 2)
    for i in range(6):
        place(a_v, 6, i, sides[i].T)
    place(a_v, 6, 6, get(10))
    send(a_v, a_out, 6, 7)
    total = curvature[:, :1] + other[:, :1]
    d_v[...] = natural[...] * lax.rsqrt(total * (1.0 / ENTRIES))
    send(d_v, direction, 0, 7)
    for copy in copies:
        copy.wait()


def natural_kernel(kept, from_0, from_1, a_inverse, s_inverse, natural, curvature):
    get = reader(kept, (from_0, from_1), BACK_STREAMS[:2])

    grad = jnp.concatenate(
        [jnp.concatenate([get(19 + 2 * i), get(20 + 2 * i)], 1) for i in range(7)], 0
    )
    g_high, g_low = split(grad)
    s_high, s_low = split(s_inverse[...])
    half = dot(jnp.concatenate([g_high, g_high, g_low], 1), jnp.concatenate([s_high, s_low, s_high], 0))
    h_high, h_low = split(half)
    h_terms = jnp.concatenate([h_high, h_low, h_high], 0)
    total = jnp.zeros((1, D), F32)
    for i in range(7):
        rows = slice(i * B, (i + 1) * B)
        a_high, a_low = split(a_inverse[rows, :])
        part = dot(jnp.concatenate([a_high, a_high, a_low], 1), h_terms)
        natural[rows, :] = part
        total = total + jnp.sum(part * grad[rows, :], axis=0, keepdims=True)
    curvature[...] = jnp.broadcast_to(jnp.sum(total, axis=1, keepdims=True), (1, B))


def call(kernel, out_shapes, in_spaces, limit_mib, name, scratch=(), flops=0, moved=0, out_spaces=None):
    return pl.pallas_call(
        kernel,
        out_shape=tuple(jax.ShapeDtypeStruct(shape, dtype) for shape, dtype in out_shapes),
        in_specs=[pl.BlockSpec(memory_space=space) for space in in_spaces],
        out_specs=tuple(pl.BlockSpec(memory_space=space) for space in out_spaces or [V] * len(out_shapes)),
        scratch_shapes=scratch,
        compiler_params=pltpu.CompilerParams(vmem_limit_bytes=limit_mib * 1024 * 1024),
        cost_estimate=pl.CostEstimate(flops=flops, bytes_accessed=moved, transcendentals=0),
        name=name,
    )


V, S = pltpu.VMEM, pltpu.SMEM


def parity_groups():
    groups = {}
    for place in range(256):
        rest, c = divmod(place, 2)
        rest, x = divmod(rest, 4)
        rest, zh = divmod(rest, 4)
        zl, y = divmod(rest, 4)
        groups.setdefault((zh, c, (x + y + zl) % 2), []).append(place)
    return [groups[key] for key in sorted(groups)]


def same_parity(value):
    axes = ("zl", "y", "zh", "x", "c")
    return lax.all_to_all(value, axes, 0, 0, axis_index_groups=parity_groups(), tiled=True)


LOW, HIGH = [(0, 1), (1, 0), (2, 3), (3, 2)], [(1, 2), (2, 1), (3, 0), (0, 3)]


def to_neighbours(parts):
    ways = (("x", LOW), ("y", LOW), ("zl", [(0, 1), (1, 0)]), ("x", HIGH), ("y", HIGH))
    return [lax.ppermute(part, axis, pairs) for part, (axis, pairs) in zip(parts, ways)]


def streams_of(streams):
    return [(((end - first) * B, B), F32) for first, end in streams]


def body(features, psi_grad, pair_means, energies, multiplicity, weights, a_inverse, s_inverse):
    feat = features.reshape(HALF, D)
    psi = psi_grad.reshape(HALF, D)
    pair = pair_means.reshape(2, HALF, PAIR)
    swap = [(0, 1), (1, 0)]

    oth_feat = lax.ppermute(feat.astype(F32), "c", swap)
    oth_pair = lax.ppermute(pair.astype(F32), "c", swap)
    far_1 = lax.ppermute(energies, "zh", LOW)
    oth_psi = lax.ppermute(psi.astype(F32), "c", swap)

    x_s, d_s, m_s = call(
        forward_kernel,
        [((2, ROWS, D + PAIR), BF16), ((2, ROWS, D), F32), ((2, 2 * WALK, D), BF16)],
        [V] * 5,
        16,
        "forward",
        flops=1_000_000_000,
        moved=6_000_000,
    )(feat, pair, oth_feat, oth_pair, weights)
    (sum_2,) = call(pair_kernel, [((1, WALK), F32)], [V] * 3, 4, "pair")(m_s, energies, far_1)
    far_2 = lax.ppermute(sum_2, "zh", HIGH)

    grads = GRADS * B
    out, out_0, fac = call(
        factors_kernel,
        [((2, len(DIRECT) * B, B), F32), ((2, grads, B), F32), ((B, B), F32)],
        [V] * 7 + [S] * 2,
        24,
        "factors",
        scratch=[
            pltpu.VMEM((2, ROWS, D), BF16),
            pltpu.VMEM((ROWS, 4 * D + PAIR), BF16),
        ],
        flops=2_500_000_000,
        moved=8_000_000,
    )(x_s, d_s, m_s, psi, oth_psi, weights, energies, energies, multiplicity)

    to_0, to_1, to_2, row_sum = call(
        tie_kernel,
        [((2 * B + 8, B), F32), ((grads - B + 8, B), F32), ((len(DIRECT) * B, B), F32), ((8, B), F32)],
        [V] * 5,
        6,
        "tie",
        moved=2_000_000,
    )(out, out_0, fac, sum_2, far_2)
    ways = [(2 * a, 2 * b) for a, b in LOW] + [(2 * a + 1, 2 * b + 1) for a, b in HIGH]
    from_2 = lax.ppermute(to_2, ("y", "c"), ways)
    from_0 = lax.ppermute(to_0, "x", LOW)
    from_1 = lax.ppermute(to_1, "x", HIGH)
    row_two = lax.ppermute(row_sum, "x", [(0, 2), (1, 3), (2, 0), (3, 1)])
    (total,) = call(
        add_kernel, [((KEPT, B), F32)], [V] * 8 + [S], 12, "add", flops=50_000_000, moved=3_000_000
    )(out, out_0, fac, from_0, from_1, from_2, row_sum, row_two, multiplicity)
    mine = jnp.sum(same_parity(total).reshape(GROUP, CHUNK, B), axis=0)
    one, two, three = (
        lax.ppermute(mine, "zh", [(i, (i + k) % 4) for i in range(4)]) for k in (1, 2, 3)
    )
    mine = (mine + two) + (one + three)
    kept = same_parity(jnp.broadcast_to(mine[None], (GROUP, CHUNK, B)).reshape(KEPT, B))
    parts = call(cut_kernel, streams_of(BACK_STREAMS), [V], 6, "cut", moved=2_200_000)(kept)
    parts = to_neighbours(parts)

    natural, curvature = call(
        natural_kernel,
        [((DIN, D), F32), ((1, B), F32)],
        [V] * 5,
        18,
        "natural",
        flops=1_500_000_000,
        moved=5_000_000,
    )(kept, *parts[:2], a_inverse[0], s_inverse[0])
    other = lax.ppermute(curvature, "c", swap)
    a_sum, s_sum, direction = call(
        finish_kernel,
        [((DIN, DIN), F32), ((D, D), F32), ((DIN, D), F32)],
        [V] * 7,
        16,
        "finish",
        scratch=[
            pltpu.VMEM((DIN, DIN), F32),
            pltpu.VMEM((D, D), F32),
            pltpu.VMEM((DIN, D), F32),
            pltpu.SemaphoreType.DMA((6,)),
        ],
        out_spaces=(pl.ANY,) * 3,
        flops=10_000_000,
        moved=7_000_000,
    )(kept, *parts[2:], natural, curvature, other)
    return a_sum[None], s_sum[None], direction[None]


def solution(mesh):
    fine = Mesh(mesh.devices.reshape(2, 4, 4, 4, 2), ("zl", "y", "zh", "x", "c"))
    twist, walker = ("zl", "y"), ("zh", "x")
    return jax.shard_map(
        body,
        mesh=fine,
        in_specs=(
            P(twist, walker, "c", None),
            P(twist, walker, "c", None),
            P(twist, None, walker, "c", None),
            P(twist, walker),
            P(twist),
            P(),
            P("c", None, None),
            P("c", None, None),
        ),
        out_specs=(P("c", None, None),) * 3,
        check_vma=False,
    )
```
